256 devices in a mesh: emb: 64 (over x, z, core), sec: 4 (over y).
Axes of the slice: x: 4, y: 4, z: 8, core: 2. Of those that a mesh axis runs over, the one named last changes fastest.
Arguments:
- emb_table: float32 [32, 32768, 64], P('sec', 'emb'), may hold values from -4 to 4
- emb_accum: float32 [32, 32768, 64], P('sec', 'emb'), may hold values from 1e-05 to 0.001
- slot_ids: int32 [16384, 32, 2], P('emb', 'sec'), may hold values from 0 to 32767, as said below
- bag_len: int32 [16384, 32], P('emb', 'sec'), may hold values from 1 to 2
- expert_w: bfloat16 [2048, 2048], P(None, 'sec'), may hold values from -0.125 to 0.125
- tower_w: bfloat16 [2048, 2048], P(None, 'sec'), may hold values from -0.125 to 0.125
- tower_out: float32 [4, 512], P('sec'), may hold values from -0.25 to 0.25
- section_task: int32 [4], P('sec'), may hold values from 0 to 2, as said below
- click_like: float32 [16384, 2], P('emb'), may hold values from 0 to 1
- watch: float32 [16384], P('emb'), may hold values from -3 to 3
Outputs:
- new_table: float32 [32, 32768, 64], P('sec', 'emb')
- new_accum: float32 [32, 32768, 64], P('sec', 'emb')
- expert_grad: float32 [2048, 2048], P('emb', 'sec')
- tower_grad: float32 [2048, 2048], P('emb', 'sec')
- head_grad: float32 [4, 512], P('sec')
The draws below stay inside these ranges and needn't reach their ends.
Inputs may be any that keep to these rules, and one draw needn't show every extreme that they name: `slot_ids`: the shard of id r is r // 512. Of the 4096 ids of one device (the examples of one emb index, the slots of one sec index), at most 128 fall in one shard, bag positions beyond bag_len included; in every draw one shard gets exactly 128 from every device. `section_task`: each of the 3 tasks owns at least one section.
All inputs are finite; a program needn't handle non-finite values.
Results may differ from the reference program's by a relative error of at most 0.017.
Values may be sent and summed in bfloat16 or wider, within the bound.
A program may use at most 128 MiB of HBM per device.

```python
import math
import jax
import jax.numpy as jnp
from jax import lax

DIM = 64
SLOTS_DEV = 8
BAG = 2
HID = 2048
SECW = 512
B_DEV = 256
ROWS_DEV = 512
SHARDS = 64
SECTIONS = 4
SLOTS = 32
FEATURES = 2048
EXAMPLES = 16384
ROWS = 32768
CAP = 128


def draw_slot_ids(key, part):
    key = jax.random.fold_in(key, 5)
    key_spread, key_shard, key_others, key_mix, key_rows = jax.random.split(key, 5)
    count = B_DEV * SLOTS_DEV * BAG
    blocks = SHARDS * SECTIONS
    spread = jax.random.randint(key_spread, (blocks, SHARDS // 2), 0, CAP // 2 + 1)
    spread = spread.at[:, 0].set(0)
    tallies = jnp.stack([CAP - spread, spread], axis=2).reshape(blocks, SHARDS)
    boundary = jnp.cumsum(tallies, axis=1)
    positions = jnp.arange(count, dtype=jnp.int32)
    labels = jax.vmap(lambda edge_row: jnp.searchsorted(edge_row, positions, side='right'))(boundary)
    hot_shard = jax.random.randint(key_shard, (), 0, SHARDS)
    others = jax.random.permutation(key_others, jnp.tile(jnp.arange(1, SHARDS, dtype=jnp.int32), (blocks, 1)), axis=1, independent=True)
    relabel = (jnp.concatenate([jnp.zeros((blocks, 1), jnp.int32), others], axis=1) + hot_shard) % SHARDS
    owners = jnp.take_along_axis(relabel, labels.astype(jnp.int32), axis=1)
    owners = jax.random.permutation(key_mix, owners, axis=1, independent=True)
    local_rows = jax.random.randint(key_rows, (blocks, count), 0, ROWS_DEV)
    row_ids = owners * ROWS_DEV + local_rows
    row_ids = row_ids.reshape(SHARDS, SECTIONS, B_DEV, SLOTS_DEV, BAG).transpose(0, 2, 1, 3, 4)
    return row_ids.reshape(SHARDS * B_DEV, SECTIONS * SLOTS_DEV, BAG).astype(jnp.int32)


def draw_section_task(key, part):
    key = jax.random.fold_in(key, 11)
    key_spare, key_order = jax.random.split(key)
    spare = jax.random.randint(key_spare, (SECTIONS,), 0, 3)
    places = jnp.arange(SECTIONS, dtype=jnp.int32)
    base = jnp.where(places < 3, places % 3, spare)
    return jax.random.permutation(key_order, base).astype(jnp.int32)


def with_ends(entries, rng, low, high):
    dims = entries.shape
    place = [jax.random.randint(jax.random.fold_in(rng, axis), (), 0, dims[axis]) for axis in range(len(dims))]
    entries = entries.at[tuple(place)].set(low)
    longest = dims.index(max(dims))
    place[longest] = (place[longest] + 1) % dims[longest]
    return entries.at[tuple(place)].set(high)


def block_scale(key, dims, shards, low, high):
    def one(dim, parts):
        draws = jax.random.uniform(jax.random.fold_in(jax.random.fold_in(key, 6), dim), (parts,), jnp.float32, low / len(shards), high / len(shards))
        return jnp.repeat(jnp.exp(draws), dims[dim] // parts).reshape((-1,) + (1,) * (len(dims) - dim - 1))

    factor_of = one(*shards[0])
    for cut in shards[1:]:
        factor_of = factor_of * one(*cut)
    return factor_of


def bell_draw(key, dims, width, reach, cuts=(), kind=jnp.bfloat16):
    array = width * jax.random.normal(key, dims, jnp.float32)
    if cuts:
        array = array * block_scale(key, dims, cuts, -0.22, 0.18)
    return jnp.clip(array, -reach, reach).astype(kind)


def setup_inputs(seed: int = 0) -> dict:
    key_list = jax.random.split(jax.random.key(seed), 11)
    emb_table = bell_draw(key_list[0], (SLOTS, ROWS, DIM), 0.5, 4.0, ((0, 4), (1, 64)), jnp.float32)
    emb_accum = jnp.clip(jnp.exp(math.log(0.001) - 4.6051703 * jax.random.uniform(key_list[1], (SLOTS, ROWS, DIM), jnp.float32) ** block_scale(key_list[1], (SLOTS, ROWS, DIM), ((0, 4), (1, 64)), -0.2, 0.2)), 9.999999747378752e-06, 0.001)
    slot_ids = draw_slot_ids(jax.random.fold_in(key_list[10], 71), 0)
    bag_len = with_ends(jax.random.randint(key_list[3], (EXAMPLES, SLOTS), 1, BAG + 1), jax.random.fold_in(key_list[3], 1), 1, BAG).astype(jnp.int32)
    expert_w = bell_draw(key_list[4], (FEATURES, HID), FEATURES ** -0.5, 0.125, ((1, 4),))
    tower_w = bell_draw(key_list[5], (HID, SECTIONS * SECW), HID ** -0.5, 0.125, ((1, 4),))
    tower_out = bell_draw(key_list[6], (SECTIONS, SECW), SECW ** -0.5, 0.25, ((0, 4),), jnp.float32)
    section_task = draw_section_task(jax.random.fold_in(key_list[10], 71), 0)
    click_like = jnp.clip(1.0 * jax.random.uniform(key_list[8], (EXAMPLES, 2), jnp.float32) ** block_scale(key_list[8], (EXAMPLES, 2), ((0, 64),), -0.2, 0.2), 0.0, 1.0)
    watch = bell_draw(key_list[9], (EXAMPLES,), 0.5, 3.0, ((0, 64),), jnp.float32)
    return {"emb_table": emb_table, "emb_accum": emb_accum, "slot_ids": slot_ids, "bag_len": bag_len, "expert_w": expert_w, "tower_w": tower_w, "tower_out": tower_out, "section_task": section_task, "click_like": click_like, "watch": watch}


learn_rate = 0.2

def silu_slope(value):
    logistic = jax.nn.sigmoid(value)
    return logistic * (1.0 + value * (1.0 - logistic))

def reference(emb_table, emb_accum, slot_ids, bag_len, expert_w, tower_w, tower_out, section_task, click_like, watch):
    slot_index = jnp.arange(SLOTS, dtype=jnp.int32)[None, :, None]
    looked = emb_table[slot_index, slot_ids].astype(jnp.bfloat16)
    in_bag = jnp.arange(BAG, dtype=jnp.int32)[None, None, :] < bag_len[:, :, None]
    pooled = lax.optimization_barrier(jnp.sum(jnp.where(in_bag[..., None], looked.astype(jnp.float32), jnp.float32(0.0)), axis=2))
    features = pooled.reshape(EXAMPLES, SLOTS * DIM).astype(jnp.bfloat16)
    pre_expert = jnp.dot(features, expert_w, preferred_element_type=jnp.float32)
    hidden = jax.nn.silu(pre_expert).astype(jnp.bfloat16)
    pre_tower = jnp.dot(hidden, tower_w, preferred_element_type=jnp.float32).reshape(EXAMPLES, SECTIONS, SECW)
    active = jax.nn.silu(pre_tower)
    section_share = lax.optimization_barrier(jnp.sum(active * tower_out[None], axis=2))
    choose = (section_task[:, None] == jnp.arange(3, dtype=jnp.int32)[None, :]).astype(jnp.float32)
    logits = lax.optimization_barrier(jnp.sum(section_share[:, :, None] * choose[None], axis=1))
    chance = jax.nn.sigmoid(logits[:, :2])
    watch_err = (logits[:, 0] + logits[:, 1] + logits[:, 2] - watch)[:, None]
    residual = jnp.concatenate([chance - click_like + watch_err, watch_err], axis=1)
    task_back = lax.optimization_barrier(jnp.sum(residual[:, None, :] * choose[None], axis=2))
    head_grad = lax.optimization_barrier(jnp.sum(active * task_back[:, :, None], axis=0))
    tower_delta = (task_back[:, :, None] * tower_out[None] * silu_slope(pre_tower)).astype(jnp.bfloat16)
    tower_delta = tower_delta.reshape(EXAMPLES, SECTIONS * SECW)
    tower_grad = jnp.dot(hidden.T, tower_delta, preferred_element_type=jnp.float32)
    hidden_grad = jnp.dot(tower_delta, tower_w.T, preferred_element_type=jnp.float32)
    expert_delta = (hidden_grad * silu_slope(pre_expert)).astype(jnp.bfloat16)
    expert_grad = jnp.dot(features.T, expert_delta, preferred_element_type=jnp.float32)
    feature_grad = jnp.dot(expert_delta, expert_w.T, preferred_element_type=jnp.float32)
    feature_grad = feature_grad.reshape(EXAMPLES, SLOTS, 1, DIM)
    lookup_grad = jnp.where(in_bag[..., None], feature_grad, jnp.float32(0.0))
    row_grad = jnp.zeros(emb_table.shape, jnp.float32).at[slot_index, slot_ids].add(lookup_grad)
    new_accum = emb_accum + row_grad * row_grad
    new_table = emb_table - learn_rate * row_grad / jnp.sqrt(new_accum)
    return (new_table, new_accum, expert_grad, tower_grad, head_grad)
```

```python
import jax
import jax.numpy as jnp
from jax import lax
from jax.experimental import pallas as pl
from jax.experimental.pallas import tpu as pltpu
from jax.sharding import PartitionSpec as P

MESH = pl.DeviceIdType.MESH
learn_rate = 0.2
f32 = jnp.float32
bf16 = jnp.bfloat16
i32 = jnp.int32

EMB = 64
SEC = 4
XS = 4
ZS = 8
CAP = 128
DIM = 64
SLOTS = 8
BATCH = 256
ROWS = 512
WIDE = 512


def mm(a, b):
    return lax.dot_general(a, b, (((1,), (0,)), ((), ())), preferred_element_type=f32)


def mm_nt(a, b):
    return lax.dot_general(a, b, (((1,), (1,)), ((), ())), preferred_element_type=f32)


def silu_slope(value):
    logistic = jax.nn.sigmoid(value)
    return logistic * (1.0 + value * (1.0 - logistic))


def hot(size, keys):
    rows = lax.broadcasted_iota(i32, (size, keys.shape[1]), 0)
    return jnp.where(rows == keys, 1.0, 0.0).astype(bf16)


def remote(src, dst, send, recv, **where):
    return pltpu.make_async_remote_copy(
        src_ref=src, dst_ref=dst, send_sem=send, recv_sem=recv, device_id=where, device_id_type=MESH
    )


def greet(emb, sec=None):
    barrier = pltpu.get_barrier_semaphore()

    @pl.loop(1, EMB)
    def _(d):
        pl.semaphore_signal(barrier, inc=1, device_id={"emb": lax.rem(emb + d, EMB)}, device_id_type=MESH)

    if sec is not None:
        for d in range(1, SEC):
            pl.semaphore_signal(barrier, inc=1, device_id={"sec": lax.rem(sec + d, SEC)}, device_id_type=MESH)


def meet(sec=None):
    pl.semaphore_wait(pltpu.get_barrier_semaphore(), EMB - 1 + (0 if sec is None else SEC - 1))


def route(ids_ref, ob, pos):
    before = lax.broadcasted_iota(i32, (BATCH, BATCH), 0)
    after = lax.broadcasted_iota(i32, (BATCH, BATCH), 1)
    upper = jnp.where(before < after, 1.0, 0.0).astype(bf16)
    shard_row = lax.broadcasted_iota(i32, (EMB, BATCH), 0)
    rank_row = lax.broadcasted_iota(i32, (CAP, BATCH), 0)
    carry = jnp.zeros((EMB, 1), f32)
    total = jnp.zeros((EMB, 2 * CAP), f32)
    for q in range(2 * SLOTS):
        ids = ids_ref[q : q + 1, :]
        owner = ids >> 9
        key = (ids & (ROWS - 1)) + ((q // 2) * ROWS + 1)
        owned = jnp.where(shard_row == owner, 1.0, 0.0)
        owned_b = owned.astype(bf16)
        prefix = mm(owned_b, upper) + carry
        rank = jnp.sum(owned * prefix, axis=0, keepdims=True).astype(i32)
        carry = carry + jnp.sum(owned, axis=1, keepdims=True)
        pos[q] = owner * CAP + rank
        ranked = rank_row == rank
        high = jnp.where(ranked, (key >> 6).astype(f32), 0.0).astype(bf16)
        low = jnp.where(ranked, (key & 63).astype(f32), 0.0).astype(bf16)
        total = total + mm_nt(owned_b, jnp.concatenate([high, low], axis=0))
    keys = (total[:, :CAP] * 64.0 + total[:, CAP:]).astype(i32) - 1
    for s in range(EMB):
        ob[s] = keys[s : s + 1, :]


def lookup_kernel(
    ids_ref, bag_ref, table_ref, feat_ref, pos_ref, key_ref,
    ob, ib, out_rows, in_rows, wide_rows, tb, id_send, id_recv, row_send, row_recv,
):
    me = lax.axis_index("emb")
    greet(me)
    route(ids_ref, ob, pos_ref)
    meet()

    @pl.loop(1, EMB)
    def _(d):
        peer = lax.rem(me + d, EMB)
        remote(ob.at[peer], ib.at[me], id_send.at[peer], id_recv.at[me], emb=peer).start()

    ib[me] = ob[me]
    tb[...] = table_ref[...].astype(bf16)

    @pl.loop(0, EMB // 2)
    def _(t):
        a = lax.rem(me + EMB - 2 * t, EMB)
        b = lax.rem(me + EMB - 2 * t - 1, EMB)

        @pl.when(t > 0)
        def _():
            remote(ob.at[a], ib.at[a], id_send.at[a], id_recv.at[a], emb=a).wait_recv()

        remote(ob.at[b], ib.at[b], id_send.at[b], id_recv.at[b], emb=b).wait_recv()
        keys = jnp.concatenate([ib[a], ib[b]], axis=1)
        slot = keys >> 9
        picked = mm(tb[...], hot(ROWS, keys & (ROWS - 1)))
        rows = jnp.zeros((DIM, 2 * CAP), f32)
        for s in range(SLOTS):
            rows = rows + jnp.where(slot == s, picked[s * DIM : (s + 1) * DIM], 0.0)
        rows = rows.astype(bf16)
        out_rows[a] = rows[:, :CAP]
        out_rows[b] = rows[:, CAP:]

        @pl.when(t == 0)
        def _():
            in_rows[me] = rows[:, :CAP]

        @pl.when(t > 0)
        def _():
            remote(out_rows.at[a], in_rows.at[me], row_send.at[a], row_recv.at[me], emb=a).start()

        remote(out_rows.at[b], in_rows.at[me], row_send.at[b], row_recv.at[me], emb=b).start()

    @pl.loop(1, EMB)
    def _(d):
        peer = lax.rem(me + d, EMB)
        remote(ob.at[peer], ib.at[peer], id_send.at[peer], id_recv.at[peer], emb=peer).wait_send()
        remote(out_rows.at[peer], in_rows.at[peer], row_send.at[peer], row_recv.at[peer], emb=peer).wait_recv()

    for h in range(8):
        wide_rows[:, h * CAP : (h + 1) * CAP] = in_rows[h * 8 : (h + 1) * 8].reshape(8 * DIM, CAP)

    @pl.loop(0, SLOTS)
    def _(s):
        pooled = jnp.zeros((DIM, BATCH), f32)
        for k in range(2):
            place = pos_ref[2 * s + k]
            shard = place >> 7
            low = jnp.where(bag_ref[s] > k, shard & 7, -1)
            picked = mm(wide_rows[...], hot(8 * CAP, (shard >> 3) * CAP + (place & (CAP - 1))))
            for g in range(8):
                pooled = pooled + jnp.where(low == g, picked[g * DIM : (g + 1) * DIM], 0.0)
        feat_ref[pl.ds(pl.multiple_of(s * DIM, DIM), DIM), :] = pooled.astype(bf16)

    key_ref[...] = ib[...]

    @pl.loop(1, EMB)
    def _(d):
        peer = lax.rem(me + d, EMB)
        remote(out_rows.at[peer], in_rows.at[peer], row_send.at[peer], row_recv.at[peer], emb=peer).wait_send()


def step_kernel(
    task_ref, feat_ref, pos_ref, key_ref, bag_ref, expert_ref, tower_ref, out_row_ref, out_col_ref, click_ref, watch_ref,
    grad_ref, expert_grad_ref, tower_grad_ref, head_ref,
    feats, hiddens, expert_t, tower_t, pre_e, pre_t, shares, part_out, part_in, whole, own_part,
    core_out, core_in, x_out, x_in, z_out, z_in, head_core, head_x, head_z,
    spread, out_grads, in_grads,
    feat_sem, hidden_sem, share_sem, part_sem, core_sem, x_sem, z_sem, hcore_sem, hx_sem, hz_sem, grad_send, grad_recv,
):
    me = lax.axis_index("emb")
    sec = lax.axis_index("sec")
    core = lax.rem(me, 2)
    z = lax.rem(lax.div(me, 2), ZS)
    x = lax.div(me, 2 * ZS)
    partner = me + 1 - 2 * core
    greet(me, sec)
    feats[sec] = feat_ref[...]
    meet(sec)

    def across(d):
        return lax.rem(sec + d, SEC)

    def spread_out(buffer, sems):
        for d in (2, 1, 3):
            remote(buffer.at[sec], buffer.at[sec], sems.at[0, d], sems.at[1, sec], sec=across(d)).start()

    def arrive(buffer, sems, d):
        remote(buffer.at[sec], buffer.at[across(d)], sems.at[0, d], sems.at[1, across(d)], sec=across(d)).wait_recv()

    def left(buffer, sems):
        for d in (2, 1, 3):
            remote(buffer.at[sec], buffer.at[sec], sems.at[0, d], sems.at[1, sec], sec=across(d)).wait_send()

    def rows_of(r):
        return pl.ds(pl.multiple_of(r * WIDE, WIDE), WIDE)

    spread_out(feats, feat_sem)

    @pl.loop(0, SEC)
    def _(r):
        expert_t[r] = expert_ref[rows_of(r), :].T
        tower_t[r] = tower_ref[rows_of(r), :].T

    pre_e[...] = mm(expert_t[sec], feats[sec])
    for d in (1, 3, 2):
        arrive(feats, feat_sem, d)
        pre_e[...] += mm(expert_t[across(d)], feats[across(d)])
    hiddens[sec] = jax.nn.silu(pre_e[...]).astype(bf16)
    spread_out(hiddens, hidden_sem)
    pre_t[...] = mm(tower_t[sec], hiddens[sec])
    for d in (1, 3, 2):
        arrive(hiddens, hidden_sem, d)
        pre_t[...] += mm(tower_t[across(d)], hiddens[across(d)])
    active = jax.nn.silu(pre_t[...])
    share = jnp.sum(active * out_col_ref[...], axis=0, keepdims=True)
    chosen = jnp.where(lax.broadcasted_iota(i32, (8, BATCH), 0) == task_ref[0], 1.0, 0.0)
    shares[sec] = share * chosen
    spread_out(shares, share_sem)
    slope = out_col_ref[...] * silu_slope(pre_t[...])
    for d in (1, 3, 2):
        arrive(shares, share_sem, d)
    logits = (shares[0] + shares[1]) + (shares[2] + shares[3])
    err = logits[0:1] + logits[1:2] + logits[2:3] - watch_ref[...]
    chance = jax.nn.sigmoid(logits[0:2]) - click_ref[...] + err
    back = chance[0:1] * chosen[0:1] + chance[1:2] * chosen[1:2] + err * chosen[2:3]
    tower_delta = (back * slope).astype(bf16)

    def part_copy(n, d, at):
        return remote(part_out.at[n, d], part_in.at[n, at], part_sem.at[n, 0, d], part_sem.at[n, 1, at], sec=across(d))

    def part(n, weights_ref, delta):
        for d in (2, 1, 3):
            peer = across(d)
            part_out[n, d] = mm(weights_ref[rows_of(peer), :], delta).astype(bf16)
            part_copy(n, d, sec).start()
        own_part[...] = mm(weights_ref[rows_of(sec), :], delta)

    def part_sum(n):
        for d in (1, 3, 2):
            part_copy(n, d, across(d)).wait_recv()
            own_part[...] += part_in[n, across(d)].astype(f32)
        for d in (2, 1, 3):
            part_copy(n, d, sec).wait_send()

    def core_copy(n):
        return remote(core_out.at[n], core_in.at[n], core_sem.at[0, n], core_sem.at[1, n], emb=partner)

    def weight_grad(n, source, delta):
        @pl.loop(0, SEC)
        def _(r):
            whole[n, pl.ds(r * 16, 16)] = mm_nt(source[r], delta).reshape(16, 32, WIDE)

        @pl.loop(0, 32)
        def _(j):
            core_out[n, j] = whole[n, 2 * j + 1 - core].astype(bf16)

        core_copy(n).start()

    def x_copy(n, d):
        to = lax.rem(x + d, XS)
        return remote(
            x_out.at[n, to], x_in.at[n, x], x_sem.at[n, 0, d], x_sem.at[n, 1, x], emb=(to * ZS + z) * 2 + core
        )

    def x_arrive(n, d):
        to = lax.rem(x + d, XS)
        return remote(
            x_out.at[n, to], x_in.at[n, to], x_sem.at[n, 0, d], x_sem.at[n, 1, to], emb=(to * ZS + z) * 2 + core
        )

    def z_copy(n, d):
        to = lax.rem(z + d, ZS)
        return remote(
            z_out.at[n, to], z_in.at[n, z], z_sem.at[n, 0, d], z_sem.at[n, 1, z], emb=(x * ZS + to) * 2 + core
        )

    def z_arrive(n, d):
        to = lax.rem(z + d, ZS)
        return remote(
            z_out.at[n, to], z_in.at[n, to], z_sem.at[n, 0, d], z_sem.at[n, 1, to], emb=(x * ZS + to) * 2 + core
        )

    def core_sum(n):
        core_copy(n).wait()

        @pl.loop(0, 32)
        def _(j):
            value = whole[n, 2 * j + core] + core_in[n, j].astype(f32)
            whole[n, 2 * j + core] = value
            x_out[n, lax.div(j, ZS), lax.rem(j, ZS)] = value.astype(bf16)

        for d in (2, 1, 3):
            x_copy(n, d).start()

    def x_sum(n):
        for d in (1, 3, 2):
            x_arrive(n, d).wait_recv()

        @pl.loop(0, ZS)
        def _(j):
            at = 2 * (x * ZS + j) + core
            value = whole[n, at]
            for d in range(1, XS):
                value = value + x_in[n, lax.rem(x + d, XS), j].astype(f32)
            whole[n, at] = value
            z_out[n, j] = value.astype(bf16)

        for d in range(1, ZS):
            z_copy(n, d).start()

    def z_sum(n, result):
        for d in range(1, ZS):
            z_arrive(n, d).wait_recv()
        value = whole[n, me]
        for d in range(1, ZS):
            value = value + z_in[n, lax.rem(z + d, ZS)].astype(f32)
        result[...] = value
        for d in range(1, XS):
            x_copy(n, d).wait_send()
        for d in range(1, ZS):
            z_copy(n, d).wait_send()

    def hc_copy():
        return remote(head_core.at[0], head_core.at[1], hcore_sem.at[0], hcore_sem.at[1], emb=partner)

    def hx_copy(d, at):
        to = lax.rem(x + d, XS)
        return remote(head_x.at[x], head_x.at[at], hx_sem.at[0, d], hx_sem.at[1, at], emb=(to * ZS + z) * 2 + core)

    def hz_copy(d, at):
        to = lax.rem(z + d, ZS)
        return remote(head_z.at[z], head_z.at[at], hz_sem.at[0, d], hz_sem.at[1, at], emb=(x * ZS + to) * 2 + core)

    part(0, tower_ref, tower_delta)
    head_core[0] = lax.dot_general(
        back, active, (((1,), (1,)), ((), ())), preferred_element_type=f32, precision=lax.Precision.HIGHEST
    )
    hc_copy().start()
    weight_grad(0, hiddens, tower_delta)
    hc_copy().wait()
    head_x[x] = head_core[0] + head_core[1]
    for d in range(1, XS):
        hx_copy(d, x).start()
    core_sum(0)
    left(feats, feat_sem)
    left(hiddens, hidden_sem)
    left(shares, share_sem)
    for d in range(1, XS):
        hx_copy(d, lax.rem(x + d, XS)).wait_recv()
    head_z[z] = (head_x[0] + head_x[1]) + (head_x[2] + head_x[3])
    for d in range(1, ZS):
        hz_copy(d, z).start()

    part_sum(0)
    expert_delta = (own_part[...] * silu_slope(pre_e[...])).astype(bf16)
    part(1, expert_ref, expert_delta)
    weight_grad(1, feats, expert_delta)
    x_sum(0)
    core_sum(1)
    part_sum(1)

    @pl.loop(0, SLOTS)
    def _(s):
        grad = own_part[pl.ds(pl.multiple_of(s * DIM, DIM), DIM), :]
        for k in range(2):
            low = jnp.where(bag_ref[s] > k, (pos_ref[2 * s + k] >> 7) & 7, -1)
            for g in range(8):
                spread[2 * s + k, g * DIM : (g + 1) * DIM, :] = jnp.where(low == g, grad, 0.0).astype(bf16)

    @pl.loop(0, 4)
    def _(t):
        pair = lax.rem(lax.div(me, 16) + t, 4)

        def add(q, total):
            place = pos_ref[q]
            key = ((place >> 10) - 2 * pair) * CAP + (place & (CAP - 1))
            return total + mm_nt(spread[q], hot(2 * CAP, key))

        total = lax.fori_loop(0, 2 * SLOTS, add, jnp.zeros((8 * DIM, 2 * CAP), f32)).astype(bf16)
        for h in range(2):
            for g in range(8):
                peer = (2 * pair + h) * 8 + g
                out_grads[peer] = total[g * DIM : (g + 1) * DIM, h * CAP : (h + 1) * CAP]

                @pl.when(peer != me)
                def _():
                    remote(
                        out_grads.at[peer], in_grads.at[me], grad_send.at[peer], grad_recv.at[me], emb=peer
                    ).start()

                @pl.when(peer == me)
                def _():
                    in_grads[me] = total[g * DIM : (g + 1) * DIM, h * CAP : (h + 1) * CAP]

    x_sum(1)
    z_sum(0, tower_grad_ref)
    for d in range(1, ZS):
        hz_copy(d, lax.rem(z + d, ZS)).wait_recv()
    head = head_z[0]
    for j in range(1, ZS):
        head = head + head_z[j]
    head_ref[...] = head

    @pl.loop(1, EMB)
    def _(d):
        peer = lax.rem(me + d, EMB)
        remote(out_grads.at[peer], in_grads.at[peer], grad_send.at[peer], grad_recv.at[peer], emb=peer).wait_recv()

    grad_ref[...] = jnp.zeros((WIDE, ROWS), f32)

    @pl.loop(0, EMB // 2)
    def _(t):
        keys = jnp.concatenate([key_ref[2 * t], key_ref[2 * t + 1]], axis=1)
        slot = keys >> 9
        grads = jnp.concatenate([in_grads[2 * t], in_grads[2 * t + 1]], axis=1).astype(f32)
        wide = jnp.concatenate([jnp.where(slot == s, grads, 0.0) for s in range(SLOTS)], axis=0).astype(bf16)
        grad_ref[...] += mm_nt(wide, hot(ROWS, keys & (ROWS - 1)))

    z_sum(1, expert_grad_ref)
    for d in range(1, XS):
        hx_copy(d, x).wait_send()
    for d in range(1, ZS):
        hz_copy(d, z).wait_send()

    @pl.loop(1, EMB)
    def _(d):
        peer = lax.rem(me + d, EMB)
        remote(out_grads.at[peer], in_grads.at[peer], grad_send.at[peer], grad_recv.at[peer], emb=peer).wait_send()


def body(
    emb_table,
    emb_accum,
    slot_ids,
    bag_len,
    expert_w,
    tower_w,
    tower_out,
    section_task,
    click_like,
    watch,
):
    vmem = pl.BlockSpec(memory_space=pltpu.VMEM)
    dma = pltpu.SemaphoreType.DMA
    table = emb_table.transpose(0, 2, 1).reshape(SLOTS * DIM, ROWS)
    accum = emb_accum.transpose(0, 2, 1).reshape(SLOTS * DIM, ROWS)
    ids = slot_ids.transpose(1, 2, 0).reshape(2 * SLOTS, BATCH)
    bag = bag_len.T.reshape(SLOTS, 1, BATCH)
    features, places, keys = pl.pallas_call(
        lookup_kernel,
        out_shape=(
            jax.ShapeDtypeStruct((SLOTS * DIM, BATCH), bf16),
            jax.ShapeDtypeStruct((2 * SLOTS, 1, BATCH), i32),
            jax.ShapeDtypeStruct((EMB, 1, CAP), i32),
        ),
        in_specs=[vmem] * 3,
        out_specs=(vmem,) * 3,
        scratch_shapes=[
            pltpu.VMEM((EMB, 1, CAP), i32),
            pltpu.VMEM((EMB, 1, CAP), i32),
            pltpu.VMEM((EMB, DIM, CAP), bf16),
            pltpu.VMEM((EMB, DIM, CAP), bf16),
            pltpu.VMEM((8 * DIM, 8 * CAP), bf16),
            pltpu.VMEM((SLOTS * DIM, ROWS), bf16),
            dma((EMB,)),
            dma((EMB,)),
            dma((EMB,)),
            dma((EMB,)),
        ],
        compiler_params=pltpu.CompilerParams(collective_id=0, has_side_effects=True, vmem_limit_bytes=32 << 20),
    )(ids, bag, table)
    row_grad, expert_grad, tower_grad, head_grad = pl.pallas_call(
        step_kernel,
        out_shape=(
            jax.ShapeDtypeStruct((SLOTS * DIM, ROWS), f32),
            jax.ShapeDtypeStruct((32, WIDE), f32),
            jax.ShapeDtypeStruct((32, WIDE), f32),
            jax.ShapeDtypeStruct((1, WIDE), f32),
        ),
        in_specs=[pl.BlockSpec(memory_space=pltpu.SMEM)] + [vmem] * 10,
        out_specs=(vmem,) * 4,
        scratch_shapes=[
            pltpu.VMEM((SEC, WIDE, BATCH), bf16),
            pltpu.VMEM((SEC, WIDE, BATCH), bf16),
            pltpu.VMEM((SEC, WIDE, WIDE), bf16),
            pltpu.VMEM((SEC, WIDE, WIDE), bf16),
            pltpu.VMEM((WIDE, BATCH), f32),
            pltpu.VMEM((WIDE, BATCH), f32),
            pltpu.VMEM((SEC, 8, BATCH), f32),
            pltpu.VMEM((2, SEC, WIDE, BATCH), bf16),
            pltpu.VMEM((2, SEC, WIDE, BATCH), bf16),
            pltpu.VMEM((2, EMB, 32, WIDE), f32),
            pltpu.VMEM((WIDE, BATCH), f32),
            pltpu.VMEM((2, 32, 32, WIDE), bf16),
            pltpu.VMEM((2, 32, 32, WIDE), bf16),
            pltpu.VMEM((2, XS, ZS, 32, WIDE), bf16),
            pltpu.VMEM((2, XS, ZS, 32, WIDE), bf16),
            pltpu.VMEM((2, ZS, 32, WIDE), bf16),
            pltpu.VMEM((2, ZS, 32, WIDE), bf16),
            pltpu.VMEM((2, 1, WIDE), f32),
            pltpu.VMEM((XS, 1, WIDE), f32),
            pltpu.VMEM((ZS, 1, WIDE), f32),
            pltpu.VMEM((2 * SLOTS, 8 * DIM, BATCH), bf16),
            pltpu.VMEM((EMB, DIM, CAP), bf16),
            pltpu.VMEM((EMB, DIM, CAP), bf16),
            dma((2, SEC)),
            dma((2, SEC)),
            dma((2, SEC)),
            dma((2, 2, SEC)),
            dma((2, 2)),
            dma((2, 2, XS)),
            dma((2, 2, ZS)),
            dma((2,)),
            dma((2, XS)),
            dma((2, ZS)),
            dma((EMB,)),
            dma((EMB,)),
        ],
        compiler_params=pltpu.CompilerParams(collective_id=1, has_side_effects=True, vmem_limit_bytes=60 << 20),
    )(
        section_task,
        features,
        places,
        keys,
        bag,
        expert_w,
        tower_w,
        tower_out,
        tower_out.reshape(WIDE, 1),
        click_like.T,
        watch.reshape(1, BATCH),
    )
    new_accum = accum + row_grad * row_grad
    new_table = table - learn_rate * row_grad / jnp.sqrt(new_accum)

    def back(value):
        return value.reshape(SLOTS, DIM, ROWS).transpose(0, 2, 1)

    return (back(new_table), back(new_accum), expert_grad, tower_grad, head_grad)


def solution(mesh):
    placed = (
        P("sec", "emb", None),
        P("sec", "emb", None),
        P("emb", "sec", None),
        P("emb", "sec"),
        P(None, "sec"),
        P(None, "sec"),
        P("sec", None),
        P("sec"),
        P("emb", None),
        P("emb"),
    )
    return jax.shard_map(
        body,
        mesh=mesh,
        in_specs=placed,
        out_specs=(
            P("sec", "emb", None),
            P("sec", "emb", None),
            P("emb", "sec"),
            P("emb", "sec"),
            P("sec", None),
        ),
        check_vma=False,
    )
```

```python
import jax
import jax.numpy as jnp
from jax import lax
from jax.experimental import pallas as pl
from jax.experimental.pallas import tpu as pltpu
from jax.sharding import PartitionSpec as P

MESH = pl.DeviceIdType.MESH
learn_rate = 0.2
f32 = jnp.float32
bf16 = jnp.bfloat16
i32 = jnp.int32

EMB = 64
SEC = 4
XS = 4
ZS = 8
CAP = 128
DIM = 64
SLOTS = 8
BATCH = 256
ROWS = 512
WIDE = 512


def mm(a, b):
    return lax.dot_general(a, b, (((1,), (0,)), ((), ())), preferred_element_type=f32)


def mm_nt(a, b):
    return lax.dot_general(a, b, (((1,), (1,)), ((), ())), preferred_element_type=f32)


def silu_slope(value):
    logistic = jax.nn.sigmoid(value)
    return logistic * (1.0 + value * (1.0 - logistic))


def hot(size, keys):
    rows = lax.broadcasted_iota(i32, (size, keys.shape[1]), 0)
    return jnp.where(rows == keys, 1.0, 0.0).astype(bf16)


SKIP = ()


class Nothing:
    def start(self):
        pass

    wait = wait_send = wait_recv = start


def remote(src, dst, send, recv, tag, **where):
    if tag in SKIP:
        return Nothing()
    return pltpu.make_async_remote_copy(
        src_ref=src, dst_ref=dst, send_sem=send, recv_sem=recv, device_id=where, device_id_type=MESH
    )


def greet(emb, sec):
    barrier = pltpu.get_barrier_semaphore()

    @pl.loop(1, EMB)
    def _(d):
        pl.semaphore_signal(barrier, inc=1, device_id={"emb": lax.rem(emb + d, EMB)}, device_id_type=MESH)

    for d in range(1, SEC):
        pl.semaphore_signal(barrier, inc=1, device_id={"sec": lax.rem(sec + d, SEC)}, device_id_type=MESH)


def meet():
    pl.semaphore_wait(pltpu.get_barrier_semaphore(), EMB - 1 + SEC - 1)


def route(ids_ref, ob, pos):
    before = lax.broadcasted_iota(i32, (BATCH, BATCH), 0)
    after = lax.broadcasted_iota(i32, (BATCH, BATCH), 1)
    upper = jnp.where(before < after, 1.0, 0.0).astype(bf16)
    shard_row = lax.broadcasted_iota(i32, (EMB, BATCH), 0)
    rank_row = lax.broadcasted_iota(i32, (CAP, BATCH), 0)
    carry = jnp.zeros((EMB, 1), f32)
    total = jnp.zeros((EMB, 2 * CAP), f32)
    for q in range(2 * SLOTS):
        ids = ids_ref[q // 2, q % 2 : q % 2 + 1, :]
        owner = ids >> 9
        key = (ids & (ROWS - 1)) + ((q // 2) * ROWS + 1)
        owned = jnp.where(shard_row == owner, 1.0, 0.0)
        owned_b = owned.astype(bf16)
        prefix = mm(owned_b, upper) + carry
        rank = jnp.sum(owned * prefix, axis=0, keepdims=True).astype(i32)
        carry = carry + jnp.sum(owned, axis=1, keepdims=True)
        pos[q] = owner * CAP + rank
        ranked = rank_row == rank
        high = jnp.where(ranked, (key >> 6).astype(f32), 0.0).astype(bf16)
        low = jnp.where(ranked, (key & 63).astype(f32), 0.0).astype(bf16)
        total = total + mm_nt(owned_b, jnp.concatenate([high, low], axis=0))
    keys = (total[:, :CAP] * 64.0 + total[:, CAP:]).astype(i32) - 1
    for s in range(EMB):
        ob[s] = keys[s : s + 1, :]


def step_kernel(
    task_ref, ids_ref, bag_ref, table_ref, expert_hbm, tower_hbm, out_row_ref, click_ref, watch_ref,
    grad_ref, packed_ref,
    pos, ob, ib, out_rows, in_rows, wide_rows, pooled_ref, tb, expert_ref, tower_ref,
    feats, hiddens, expert_t, tower_t, pre_e, pre_t, shares, part_out, part_in, whole, own_part,
    core_out, core_in, x_out, x_in, z_out, z_in, head_core, head_x, head_z,
    spread, out_grads, in_grads,
    load_sem, id_send, id_recv, row_send, row_recv,
    feat_sem, hidden_sem, share_sem, part_sem, core_sem, x_sem, z_sem, hcore_sem, hx_sem, hz_sem, grad_send, grad_recv,
):
    me = lax.axis_index("emb")
    sec = lax.axis_index("sec")
    core = lax.rem(me, 2)
    z = lax.rem(lax.div(me, 2), ZS)
    x = lax.div(me, 2 * ZS)
    half = lax.div(me, 32)
    inner = lax.rem(me, 32)
    partner = me + 1 - 2 * core
    expert_load = pltpu.make_async_copy(expert_hbm, expert_ref, load_sem.at[0])
    tower_load = pltpu.make_async_copy(tower_hbm, tower_ref, load_sem.at[1])
    expert_load.start()
    tower_load.start()
    greet(me, sec)
    route(ids_ref, ob, pos)
    meet()

    def rows_of(r):
        return pl.ds(pl.multiple_of(r * WIDE, WIDE), WIDE)

    def ahead(d):
        group = lax.rem(half + lax.div(d, 32), 2)
        return group * 32 + lax.rem(inner + d, 32)

    def behind(d):
        group = lax.rem(half + lax.div(d, 32), 2)
        return group * 32 + lax.rem(inner + 64 - d, 32)

    def id_copy(peer, at):
        return remote(ob.at[peer], ib.at[at], id_send.at[peer], id_recv.at[at], tag="ids", emb=peer)

    def row_copy(peer, at):
        return remote(out_rows.at[peer], in_rows.at[at], row_send.at[peer], row_recv.at[at], tag="rows", emb=peer)

    def grad_copy(peer, at):
        return remote(out_grads.at[peer], in_grads.at[at], grad_send.at[peer], grad_recv.at[at], tag="grads", emb=peer)

    @pl.loop(1, EMB)
    def _(d):
        id_copy(ahead(d), me).start()

    ib[me] = ob[me]
    tb[...] = table_ref[...].astype(bf16)
    expert_load.wait()
    tower_load.wait()

    if "transpose" not in SKIP:

        @pl.loop(0, SEC)
        def _(r):
            expert_t[r] = expert_ref[rows_of(r), :].T
            tower_t[r] = tower_ref[rows_of(r), :].T

    @pl.loop(0, EMB // 2)
    def _(t):
        a = behind(2 * t)
        b = behind(2 * t + 1)

        @pl.when(t > 0)
        def _():
            id_copy(a, a).wait_recv()

        id_copy(b, b).wait_recv()
        if "gather" not in SKIP:
            keys = jnp.concatenate([ib[a], ib[b]], axis=1)
            slot = keys >> 9
            picked = mm(tb[...], hot(ROWS, keys & (ROWS - 1)))
            rows = jnp.zeros((DIM, 2 * CAP), f32)
            for s in range(SLOTS):
                rows = rows + jnp.where(slot == s, picked[s * DIM : (s + 1) * DIM], 0.0)
            rows = rows.astype(bf16)
            out_rows[a] = rows[:, :CAP]
            out_rows[b] = rows[:, CAP:]

            @pl.when(t == 0)
            def _():
                in_rows[me] = rows[:, :CAP]

        @pl.when(t > 0)
        def _():
            row_copy(a, me).start()

        row_copy(b, me).start()

    def pool(part, first):
        for h in range(4):
            wide_rows[:, h * CAP : (h + 1) * CAP] = in_rows[pl.ds((part * 4 + h) * 8, 8)].reshape(8 * DIM, CAP)

        @pl.loop(0, SLOTS)
        def _(s):
            rows = pl.ds(pl.multiple_of(s * DIM, DIM), DIM)
            pooled = jnp.zeros((DIM, BATCH), f32) if first else pooled_ref[rows, :]
            for k in range(2):
                place = pos[2 * s + k]
                shard = place >> 7
                low = jnp.where(bag_ref[pl.ds(s, 1), :] > k, shard & 7, -1)
                key = ((shard >> 3) - part * 4) * CAP + (place & (CAP - 1))
                picked = mm(wide_rows[...], hot(4 * CAP, key))
                for g in range(8):
                    pooled = pooled + jnp.where(low == g, picked[g * DIM : (g + 1) * DIM], 0.0)
            if first:
                pooled_ref[rows, :] = pooled
            else:
                feats[sec, rows, :] = pooled.astype(bf16)

    @pl.loop(1, 32)
    def _(d):
        peer = ahead(d)
        row_copy(peer, peer).wait_recv()

    if "pool" not in SKIP:
        pool(half, True)

    @pl.loop(32, EMB)
    def _(d):
        peer = ahead(d)
        row_copy(peer, peer).wait_recv()

    if "pool" not in SKIP:
        pool(1 - half, False)

    def across(d):
        return lax.rem(sec + d, SEC)

    def sec_copy(buffer, sems, tag, d, at):
        return remote(buffer.at[sec], buffer.at[at], sems.at[0, d], sems.at[1, at], tag=tag, sec=across(d))

    def spread_out(buffer, sems, tag):
        for d in (2, 1, 3):
            sec_copy(buffer, sems, tag, d, sec).start()

    def arrive(buffer, sems, tag, d):
        sec_copy(buffer, sems, tag, d, across(d)).wait_recv()

    def left(buffer, sems, tag):
        for d in (2, 1, 3):
            sec_copy(buffer, sems, tag, d, sec).wait_send()

    spread_out(feats, feat_sem, "feats")
    pre_e[...] = mm(expert_t[sec], feats[sec])
    for d in (1, 3, 2):
        arrive(feats, feat_sem, "feats", d)
        pre_e[...] += mm(expert_t[across(d)], feats[across(d)])
    hiddens[sec] = jax.nn.silu(pre_e[...]).astype(bf16)
    spread_out(hiddens, hidden_sem, "hiddens")
    pre_t[...] = mm(tower_t[sec], hiddens[sec])
    for d in (1, 3, 2):
        arrive(hiddens, hidden_sem, "hiddens", d)
        pre_t[...] += mm(tower_t[across(d)], hiddens[across(d)])
    out_col = jnp.broadcast_to(out_row_ref[...], (8, WIDE)).T[:, 0:1]
    active = jax.nn.silu(pre_t[...])
    share = jnp.sum(active * out_col, axis=0, keepdims=True)
    chosen = jnp.where(lax.broadcasted_iota(i32, (8, BATCH), 0) == task_ref[0], 1.0, 0.0)
    shares[sec] = share * chosen
    spread_out(shares, share_sem, "shares")
    slope = out_col * silu_slope(pre_t[...])
    for d in (1, 3, 2):
        arrive(shares, share_sem, "shares", d)
    logits = (shares[0] + shares[1]) + (shares[2] + shares[3])
    err = logits[0:1] + logits[1:2] + logits[2:3] - watch_ref[...]
    chance = jax.nn.sigmoid(logits[0:2]) - click_ref[...] + err
    back = chance[0:1] * chosen[0:1] + chance[1:2] * chosen[1:2] + err * chosen[2:3]
    tower_delta = (back * slope).astype(bf16)

    def part_copy(n, d, at):
        return remote(part_out.at[n, d], part_in.at[n, at], part_sem.at[n, 0, d], part_sem.at[n, 1, at], tag="part", sec=across(d))

    def part(n, weights_ref, delta):
        for d in (2, 1, 3):
            peer = across(d)
            part_out[n, d] = mm(weights_ref[rows_of(peer), :], delta).astype(bf16)
            part_copy(n, d, sec).start()
        own_part[...] = mm(weights_ref[rows_of(sec), :], delta)

    def part_sum(n):
        for d in (1, 3, 2):
            part_copy(n, d, across(d)).wait_recv()
            own_part[...] += part_in[n, across(d)].astype(f32)
        for d in (2, 1, 3):
            part_copy(n, d, sec).wait_send()

    def core_copy(n):
        return remote(core_out.at[n], core_in.at[n], core_sem.at[0, n], core_sem.at[1, n], tag="core", emb=partner)

    def weight_grad(n, source, delta):
        @pl.loop(0, SEC)
        def _(r):
            whole[n, pl.ds(r * 16, 16)] = mm_nt(source[r], delta).reshape(16, 32, WIDE)

        @pl.loop(0, 32)
        def _(j):
            core_out[n, j] = whole[n, 2 * j + 1 - core].astype(bf16)

        core_copy(n).start()

    def x_copy(n, d):
        to = lax.rem(x + d, XS)
        return remote(
            x_out.at[n, to], x_in.at[n, x], x_sem.at[n, 0, d], x_sem.at[n, 1, x], tag="x", emb=(to * ZS + z) * 2 + core
        )

    def x_arrive(n, d):
        to = lax.rem(x + d, XS)
        return remote(
            x_out.at[n, to], x_in.at[n, to], x_sem.at[n, 0, d], x_sem.at[n, 1, to], tag="x", emb=(to * ZS + z) * 2 + core
        )

    def z_copy(n, d):
        to = lax.rem(z + d, ZS)
        return remote(
            z_out.at[n, to], z_in.at[n, z], z_sem.at[n, 0, d], z_sem.at[n, 1, z], tag="z", emb=(x * ZS + to) * 2 + core
        )

    def z_arrive(n, d):
        to = lax.rem(z + d, ZS)
        return remote(
            z_out.at[n, to], z_in.at[n, to], z_sem.at[n, 0, d], z_sem.at[n, 1, to], tag="z", emb=(x * ZS + to) * 2 + core
        )

    def core_sum(n):
        core_copy(n).wait()

        @pl.loop(0, 32)
        def _(j):
            value = whole[n, 2 * j + core] + core_in[n, j].astype(f32)
            whole[n, 2 * j + core] = value
            x_out[n, lax.div(j, ZS), lax.rem(j, ZS)] = value.astype(bf16)

        for d in (2, 1, 3):
            x_copy(n, d).start()

    def x_sum(n):
        for d in (1, 3, 2):
            x_arrive(n, d).wait_recv()

        @pl.loop(0, ZS)
        def _(j):
            at = 2 * (x * ZS + j) + core
            value = whole[n, at]
            for d in range(1, XS):
                value = value + x_in[n, lax.rem(x + d, XS), j].astype(f32)
            whole[n, at] = value
            z_out[n, j] = value.astype(bf16)

        for d in range(1, ZS):
            z_copy(n, d).start()

    def z_sum(n):
        for d in range(1, ZS):
            z_arrive(n, d).wait_recv()
        value = whole[n, me]
        for d in range(1, ZS):
            value = value + z_in[n, lax.rem(z + d, ZS)].astype(f32)
        packed_ref[pl.ds(32 * n, 32), :] = value
        for d in range(1, XS):
            x_copy(n, d).wait_send()
        for d in range(1, ZS):
            z_copy(n, d).wait_send()

    def hc_copy():
        return remote(head_core.at[0], head_core.at[1], hcore_sem.at[0], hcore_sem.at[1], tag="head", emb=partner)

    def hx_copy(d, at):
        to = lax.rem(x + d, XS)
        return remote(head_x.at[x], head_x.at[at], hx_sem.at[0, d], hx_sem.at[1, at], tag="head", emb=(to * ZS + z) * 2 + core)

    def hz_copy(d, at):
        to = lax.rem(z + d, ZS)
        return remote(head_z.at[z], head_z.at[at], hz_sem.at[0, d], hz_sem.at[1, at], tag="head", emb=(x * ZS + to) * 2 + core)

    part(0, tower_ref, tower_delta)
    head_core[0] = lax.dot_general(
        back, active, (((1,), (1,)), ((), ())), preferred_element_type=f32, precision=lax.Precision.HIGHEST
    )
    hc_copy().start()
    weight_grad(0, hiddens, tower_delta)
    hc_copy().wait()
    head_x[x] = head_core[0] + head_core[1]
    for d in range(1, XS):
        hx_copy(d, x).start()
    core_sum(0)
    left(feats, feat_sem, "feats")
    left(hiddens, hidden_sem, "hiddens")
    left(shares, share_sem, "shares")
    for d in range(1, XS):
        hx_copy(d, lax.rem(x + d, XS)).wait_recv()
    head_z[z] = (head_x[0] + head_x[1]) + (head_x[2] + head_x[3])
    for d in range(1, ZS):
        hz_copy(d, z).start()

    part_sum(0)
    expert_delta = (own_part[...] * silu_slope(pre_e[...])).astype(bf16)
    part(1, expert_ref, expert_delta)
    weight_grad(1, feats, expert_delta)
    x_sum(0)
    core_sum(1)
    part_sum(1)

    @pl.loop(0, SLOTS)
    def _(s):
        grad = own_part[pl.ds(pl.multiple_of(s * DIM, DIM), DIM), :]
        for k in range(2):
            low = jnp.where(bag_ref[pl.ds(s, 1), :] > k, (pos[2 * s + k] >> 7) & 7, -1)
            for g in range(8):
                spread[2 * s + k, g * DIM : (g + 1) * DIM, :] = jnp.where(low == g, grad, 0.0).astype(bf16)

    @pl.loop(0, 4)
    def _(t):
        pair = lax.rem(x + t, 4)

        def add(q, total):
            place = pos[q]
            key = ((place >> 10) - 2 * pair) * CAP + (place & (CAP - 1))
            return total + mm_nt(spread[q], hot(2 * CAP, key))

        total = lax.fori_loop(0, 2 * SLOTS, add, jnp.zeros((8 * DIM, 2 * CAP), f32)).astype(bf16)
        for h in range(2):
            for g in range(8):
                peer = (2 * pair + h) * 8 + g
                out_grads[peer] = total[g * DIM : (g + 1) * DIM, h * CAP : (h + 1) * CAP]

                @pl.when(peer != me)
                def _():
                    grad_copy(peer, me).start()

                @pl.when(peer == me)
                def _():
                    in_grads[me] = total[g * DIM : (g + 1) * DIM, h * CAP : (h + 1) * CAP]

    x_sum(1)
    z_sum(0)
    for d in range(1, ZS):
        hz_copy(d, lax.rem(z + d, ZS)).wait_recv()
    head = head_z[0]
    for j in range(1, ZS):
        head = head + head_z[j]
    packed_ref[64:72, :] = jnp.broadcast_to(head, (8, WIDE))

    grad_ref[...] = jnp.zeros((WIDE, ROWS), f32)

    @pl.loop(0, XS)
    def _(t):
        first = lax.rem(x + XS - t, XS) * 16

        @pl.loop(0, 16)
        def _(j):
            peer = first + j

            @pl.when(peer != me)
            def _():
                grad_copy(peer, peer).wait_recv()

        if "scatter" not in SKIP:

            @pl.loop(0, 8)
            def _(j):
                a = first + 2 * j
                keys = jnp.concatenate([ib[a], ib[a + 1]], axis=1)
                slot = keys >> 9
                grads = jnp.concatenate([in_grads[a], in_grads[a + 1]], axis=1).astype(f32)
                wide = jnp.concatenate([jnp.where(slot == s, grads, 0.0) for s in range(SLOTS)], axis=0).astype(bf16)
                grad_ref[...] += mm_nt(wide, hot(ROWS, keys & (ROWS - 1)))

    z_sum(1)
    for d in range(1, XS):
        hx_copy(d, x).wait_send()
    for d in range(1, ZS):
        hz_copy(d, z).wait_send()

    @pl.loop(1, EMB)
    def _(d):
        peer = lax.rem(me + d, EMB)
        id_copy(peer, me).wait_send()
        row_copy(peer, me).wait_send()
        grad_copy(peer, me).wait_send()


def body(
    emb_table,
    emb_accum,
    slot_ids,
    bag_len,
    expert_w,
    tower_w,
    tower_out,
    section_task,
    click_like,
    watch,
):
    vmem = pl.BlockSpec(memory_space=pltpu.VMEM)
    dma = pltpu.SemaphoreType.DMA
    table = emb_table.transpose(0, 2, 1).reshape(SLOTS * DIM, ROWS)
    accum = emb_accum.transpose(0, 2, 1).reshape(SLOTS * DIM, ROWS)
    anywhere = pl.BlockSpec(memory_space=pl.ANY)
    row_grad, packed = pl.pallas_call(
        step_kernel,
        out_shape=(
            jax.ShapeDtypeStruct((SLOTS * DIM, ROWS), f32),
            jax.ShapeDtypeStruct((72, WIDE), f32),
        ),
        in_specs=[pl.BlockSpec(memory_space=pltpu.SMEM), vmem, vmem, vmem, anywhere, anywhere, vmem, vmem, vmem],
        out_specs=(vmem,) * 2,
        scratch_shapes=[
            pltpu.VMEM((2 * SLOTS, 1, BATCH), i32),
            pltpu.VMEM((EMB, 1, CAP), i32),
            pltpu.VMEM((EMB, 1, CAP), i32),
            pltpu.VMEM((EMB, DIM, CAP), bf16),
            pltpu.VMEM((EMB, DIM, CAP), bf16),
            pltpu.VMEM((8 * DIM, 4 * CAP), bf16),
            pltpu.VMEM((8 * DIM, BATCH), f32),
            pltpu.VMEM((SLOTS * DIM, ROWS), bf16),
            pltpu.VMEM((SEC * WIDE, WIDE), bf16),
            pltpu.VMEM((SEC * WIDE, WIDE), bf16),
            pltpu.VMEM((SEC, WIDE, BATCH), bf16),
            pltpu.VMEM((SEC, WIDE, BATCH), bf16),
            pltpu.VMEM((SEC, WIDE, WIDE), bf16),
            pltpu.VMEM((SEC, WIDE, WIDE), bf16),
            pltpu.VMEM((WIDE, BATCH), f32),
            pltpu.VMEM((WIDE, BATCH), f32),
            pltpu.VMEM((SEC, 8, BATCH), f32),
            pltpu.VMEM((2, SEC, WIDE, BATCH), bf16),
            pltpu.VMEM((2, SEC, WIDE, BATCH), bf16),
            pltpu.VMEM((2, EMB, 32, WIDE), f32),
            pltpu.VMEM((WIDE, BATCH), f32),
            pltpu.VMEM((2, 32, 32, WIDE), bf16),
            pltpu.VMEM((2, 32, 32, WIDE), bf16),
            pltpu.VMEM((2, XS, ZS, 32, WIDE), bf16),
            pltpu.VMEM((2, XS, ZS, 32, WIDE), bf16),
            pltpu.VMEM((2, ZS, 32, WIDE), bf16),
            pltpu.VMEM((2, ZS, 32, WIDE), bf16),
            pltpu.VMEM((2, 1, WIDE), f32),
            pltpu.VMEM((XS, 1, WIDE), f32),
            pltpu.VMEM((ZS, 1, WIDE), f32),
            pltpu.VMEM((2 * SLOTS, 8 * DIM, BATCH), bf16),
            pltpu.VMEM((EMB, DIM, CAP), bf16),
            pltpu.VMEM((EMB, DIM, CAP), bf16),
            dma((2,)),
            dma((EMB,)),
            dma((EMB,)),
            dma((EMB,)),
            dma((EMB,)),
            dma((2, SEC)),
            dma((2, SEC)),
            dma((2, SEC)),
            dma((2, 2, SEC)),
            dma((2, 2)),
            dma((2, 2, XS)),
            dma((2, 2, ZS)),
            dma((2,)),
            dma((2, XS)),
            dma((2, ZS)),
            dma((EMB,)),
            dma((EMB,)),
        ],
        compiler_params=pltpu.CompilerParams(collective_id=0, has_side_effects=True, vmem_limit_bytes=60 << 20),
    )(
        section_task,
        slot_ids.transpose(1, 2, 0),
        bag_len.T,
        table,
        expert_w,
        tower_w,
        tower_out,
        click_like.T,
        watch.reshape(1, BATCH),
    )
    tower_grad, expert_grad, head_grad = packed[:32], packed[32:64], packed[64:65]
    new_accum = accum + row_grad * row_grad
    new_table = table - learn_rate * row_grad / jnp.sqrt(new_accum)

    def back(value):
        return value.reshape(SLOTS, DIM, ROWS).transpose(0, 2, 1)

    return (back(new_table), back(new_accum), expert_grad, tower_grad, head_grad)


def solution(mesh):
    placed = (
        P("sec", "emb", None),
        P("sec", "emb", None),
        P("emb", "sec", None),
        P("emb", "sec"),
        P(None, "sec"),
        P(None, "sec"),
        P("sec", None),
        P("sec"),
        P("emb", None),
        P("emb"),
    )
    return jax.shard_map(
        body,
        mesh=mesh,
        in_specs=placed,
        out_specs=(
            P("sec", "emb", None),
            P("sec", "emb", None),
            P("emb", "sec"),
            P("emb", "sec"),
            P("sec", None),
        ),
        check_vma=False,
    )
```

```python
import jax
import jax.numpy as jnp
from jax import lax
from jax.experimental import pallas as pl
from jax.experimental.pallas import tpu as pltpu
from jax.sharding import PartitionSpec as P

MESH = pl.DeviceIdType.MESH
learn_rate = 0.2
f32 = jnp.float32
bf16 = jnp.bfloat16
i32 = jnp.int32

EMB = 64
SEC = 4
XS = 4
ZS = 8
CAP = 128
DIM = 64
SLOTS = 8
BATCH = 256
ROWS = 512
WIDE = 512


def mm(a, b):
    return lax.dot_general(a, b, (((1,), (0,)), ((), ())), preferred_element_type=f32)


def mm_nt(a, b):
    return lax.dot_general(a, b, (((1,), (1,)), ((), ())), preferred_element_type=f32)


def silu_slope(value):
    logistic = jax.nn.sigmoid(value)
    return logistic * (1.0 + value * (1.0 - logistic))


def hot(size, keys):
    rows = lax.broadcasted_iota(i32, (size, keys.shape[1]), 0)
    return jnp.where(rows == keys, 1.0, 0.0).astype(bf16)


SKIP = ()


class Nothing:
    def start(self):
        pass

    wait = wait_send = wait_recv = start


def remote(src, dst, send, recv, tag, **where):
    if tag in SKIP:
        return Nothing()
    return pltpu.make_async_remote_copy(
        src_ref=src, dst_ref=dst, send_sem=send, recv_sem=recv, device_id=where, device_id_type=MESH
    )


def greet(emb, sec):
    barrier = pltpu.get_barrier_semaphore()

    @pl.loop(1, EMB)
    def _(d):
        pl.semaphore_signal(barrier, inc=1, device_id={"emb": lax.rem(emb + d, EMB)}, device_id_type=MESH)

    for d in range(1, SEC):
        pl.semaphore_signal(barrier, inc=1, device_id={"sec": lax.rem(sec + d, SEC)}, device_id_type=MESH)


def meet():
    pl.semaphore_wait(pltpu.get_barrier_semaphore(), EMB - 1 + SEC - 1)


def route(ids_ref, ob, pos):
    before = lax.broadcasted_iota(i32, (BATCH, BATCH), 0)
    after = lax.broadcasted_iota(i32, (BATCH, BATCH), 1)
    upper = jnp.where(before < after, 1.0, 0.0).astype(bf16)
    shard_row = lax.broadcasted_iota(i32, (EMB, BATCH), 0)
    rank_row = lax.broadcasted_iota(i32, (CAP, BATCH), 0)
    carry = jnp.zeros((EMB, 1), f32)
    total = jnp.zeros((EMB, 2 * CAP), f32)
    for q in range(2 * SLOTS):
        ids = ids_ref[q // 2, q % 2 : q % 2 + 1, :]
        owner = ids >> 9
        key = (ids & (ROWS - 1)) + ((q // 2) * ROWS + 1)
        owned = jnp.where(shard_row == owner, 1.0, 0.0)
        owned_b = owned.astype(bf16)
        prefix = mm(owned_b, upper) + carry
        rank = jnp.sum(owned * prefix, axis=0, keepdims=True).astype(i32)
        carry = carry + jnp.sum(owned, axis=1, keepdims=True)
        pos[q] = owner * CAP + rank
        ranked = rank_row == rank
        high = jnp.where(ranked, (key >> 6).astype(f32), 0.0).astype(bf16)
        low = jnp.where(ranked, (key & 63).astype(f32), 0.0).astype(bf16)
        total = total + mm_nt(owned_b, jnp.concatenate([high, low], axis=0))
    keys = (total[:, :CAP] * 64.0 + total[:, CAP:]).astype(i32) - 1
    for s in range(EMB):
        ob[s] = keys[s : s + 1, :]


def step_kernel(
    task_ref, ids_ref, bag_ref, table_ref, expert_hbm, tower_hbm, out_row_ref, click_ref, watch_ref,
    grad_ref, packed_ref,
    pos, ob, ib, out_rows, in_rows, wide_rows, pooled_ref, tb, expert_ref, tower_ref,
    feats, hiddens, expert_t, tower_t, pre_e, pre_t, shares, part_out, part_in, relay, whole, own_part,
    core_out, core_in, x_out, x_in, z_out, z_in, head_core, head_x, head_z,
    spread, hots, row_hots, out_grads, in_grads,
    load_sem, id_send, id_recv, row_send, row_recv,
    feat_sem, hidden_sem, share_sem, part_sem, core_sem, x_sem, z_sem, hcore_sem, hx_sem, hz_sem, grad_send, grad_recv,
):
    me = lax.axis_index("emb")
    sec = lax.axis_index("sec")
    core = lax.rem(me, 2)
    z = lax.rem(lax.div(me, 2), ZS)
    x = lax.div(me, 2 * ZS)
    half = lax.div(me, 32)
    inner = lax.rem(me, 32)
    partner = me + 1 - 2 * core
    expert_load = pltpu.make_async_copy(expert_hbm, expert_ref, load_sem.at[0])
    tower_load = pltpu.make_async_copy(tower_hbm, tower_ref, load_sem.at[1])
    expert_load.start()
    tower_load.start()
    greet(me, sec)
    route(ids_ref, ob, pos)
    meet()

    def rows_of(r):
        return pl.ds(pl.multiple_of(r * WIDE, WIDE), WIDE)

    def ahead(d):
        group = lax.rem(half + lax.div(d, 32), 2)
        return group * 32 + lax.rem(inner + d, 32)

    def behind(d):
        group = lax.rem(half + lax.div(d, 32), 2)
        return group * 32 + lax.rem(inner + 64 - d, 32)

    def id_copy(peer, at):
        return remote(ob.at[peer], ib.at[at], id_send.at[peer], id_recv.at[at], tag="ids", emb=peer)

    def row_copy(peer, at):
        return remote(out_rows.at[peer], in_rows.at[at], row_send.at[peer], row_recv.at[at], tag="rows", emb=peer)

    def grad_copy(peer, at):
        return remote(out_grads.at[peer], in_grads.at[at], grad_send.at[peer], grad_recv.at[at], tag="grads", emb=peer)

    @pl.loop(1, EMB)
    def _(d):
        id_copy(ahead(d), me).start()

    ib[me] = ob[me]
    tb[...] = table_ref[...].astype(bf16)
    expert_load.wait()
    tower_load.wait()

    if "transpose" not in SKIP:

        @pl.loop(0, SEC)
        def _(r):
            expert_t[r] = expert_ref[rows_of(r), :].T
            tower_t[r] = tower_ref[rows_of(r), :].T

    @pl.loop(0, EMB // 2)
    def _(t):
        a = behind(2 * t)
        b = behind(2 * t + 1)

        @pl.when(t > 0)
        def _():
            id_copy(a, a).wait_recv()

        id_copy(b, b).wait_recv()
        if "gather" not in SKIP:
            keys = jnp.concatenate([ib[a], ib[b]], axis=1)
            slot = keys >> 9
            picked = mm(tb[...], hot(ROWS, keys & (ROWS - 1)))
            rows = jnp.zeros((DIM, 2 * CAP), f32)
            for s in range(SLOTS):
                rows = rows + jnp.where(slot == s, picked[s * DIM : (s + 1) * DIM], 0.0)
            rows = rows.astype(bf16)
            out_rows[a] = rows[:, :CAP]
            out_rows[b] = rows[:, CAP:]

            @pl.when(t == 0)
            def _():
                in_rows[me] = rows[:, :CAP]

        @pl.when(t > 0)
        def _():
            row_copy(a, me).start()

        row_copy(b, me).start()

    def pool(part, first):
        for h in range(4):
            wide_rows[:, h * CAP : (h + 1) * CAP] = in_rows[pl.ds((part * 4 + h) * 8, 8)].reshape(8 * DIM, CAP)

        @pl.loop(0, SLOTS)
        def _(s):
            rows = pl.ds(pl.multiple_of(s * DIM, DIM), DIM)
            pooled = jnp.zeros((DIM, BATCH), f32) if first else pooled_ref[rows, :]
            for k in range(2):
                place = pos[2 * s + k]
                shard = place >> 7
                low = jnp.where(bag_ref[pl.ds(s, 1), :] > k, shard & 7, -1)
                key = ((shard >> 3) - part * 4) * CAP + (place & (CAP - 1))
                picked = mm(wide_rows[...], hot(4 * CAP, key))
                for g in range(8):
                    pooled = pooled + jnp.where(low == g, picked[g * DIM : (g + 1) * DIM], 0.0)
            if first:
                pooled_ref[rows, :] = pooled
            else:
                feats[sec, rows, :] = pooled.astype(bf16)

    @pl.loop(1, 32)
    def _(d):
        peer = ahead(d)
        row_copy(peer, peer).wait_recv()

    if "pool" not in SKIP:
        pool(half, True)

    @pl.loop(32, EMB)
    def _(d):
        peer = ahead(d)
        row_copy(peer, peer).wait_recv()

    if "pool" not in SKIP:
        pool(1 - half, False)

    def across(d):
        return lax.rem(sec + d, SEC)

    def sec_copy(buffer, sems, tag, d, at):
        return remote(buffer.at[sec], buffer.at[at], sems.at[0, d], sems.at[1, at], tag=tag, sec=across(d))

    def ring_copy(buffer, sems, tag, i, arriving=False):
        offset, part, way = ((0, 0, 1), (0, 1, 1), (0, 1, 3), (0, 0, 3), (3, 0, 1), (1, 1, 3))[i]
        rows = pl.ds(part * (WIDE // 2), WIDE // 2)
        source = across(offset)
        target = across(4 - way + offset) if arriving else source
        return remote(
            buffer.at[source, rows], buffer.at[target, rows], sems.at[0, i], sems.at[1, i], tag=tag, sec=across(way)
        )

    def gather_sec(buffer, sems, tag, weights, total):
        def came(i):
            ring_copy(buffer, sems, tag, i, True).wait_recv()

        total[...] = mm(weights[sec], buffer[sec])
        came(0)
        ring_copy(buffer, sems, tag, 4).start()
        came(2)
        ring_copy(buffer, sems, tag, 5).start()
        came(1)
        total[...] += mm(weights[across(3)], buffer[across(3)])
        came(3)
        total[...] += mm(weights[across(1)], buffer[across(1)])
        came(4)
        came(5)
        total[...] += mm(weights[across(2)], buffer[across(2)])

    def left(buffer, sems, tag):
        for i in range(6):
            ring_copy(buffer, sems, tag, i).wait_send()

    for i in (0, 2, 1, 3):
        ring_copy(feats, feat_sem, "feats", i).start()
    gather_sec(feats, feat_sem, "feats", expert_t, pre_e)
    hiddens[sec] = jax.nn.silu(pre_e[...]).astype(bf16)
    for i in (0, 2, 1, 3):
        ring_copy(hiddens, hidden_sem, "hiddens", i).start()
    gather_sec(hiddens, hidden_sem, "hiddens", tower_t, pre_t)
    out_col = jnp.broadcast_to(out_row_ref[...], (8, WIDE)).T[:, 0:1]
    active = jax.nn.silu(pre_t[...])
    share = jnp.sum(active * out_col, axis=0, keepdims=True)
    chosen = jnp.where(lax.broadcasted_iota(i32, (8, BATCH), 0) == task_ref[0], 1.0, 0.0)
    shares[sec] = share * chosen
    for d in (2, 1, 3):
        sec_copy(shares, share_sem, "shares", d, sec).start()
    slope = out_col * silu_slope(pre_t[...])
    for d in (1, 3, 2):
        sec_copy(shares, share_sem, "shares", d, across(d)).wait_recv()
    logits = (shares[0] + shares[1]) + (shares[2] + shares[3])
    err = logits[0:1] + logits[1:2] + logits[2:3] - watch_ref[...]
    chance = jax.nn.sigmoid(logits[0:2]) - click_ref[...] + err
    back = chance[0:1] * chosen[0:1] + chance[1:2] * chosen[1:2] + err * chosen[2:3]
    tower_delta = (back * slope).astype(bf16)

    low_half = slice(0, WIDE // 2)
    high_half = slice(WIDE // 2, WIDE)

    def part_copy(n, i):
        return remote(
            part_out.at[n, i], part_in.at[n, i], part_sem.at[n, 0, i], part_sem.at[n, 1, i],
            tag="part", sec=across((1, 3, 1, 3, 1, 3)[i]),
        )

    def part(n, weights_ref, delta):
        def send(i, value):
            part_out[n, i] = value.astype(bf16)
            part_copy(n, i).start()

        value = mm(weights_ref[rows_of(across(2)), :], delta)
        send(0, value[low_half])
        send(1, value[high_half])
        value = mm(weights_ref[rows_of(across(1)), :], delta)
        send(2, value[high_half])
        relay[0] = value[low_half]
        value = mm(weights_ref[rows_of(across(3)), :], delta)
        send(3, value[low_half])
        relay[1] = value[high_half]
        own_part[...] = mm(weights_ref[rows_of(sec), :], delta)
        for i in range(2):
            part_copy(n, i).wait_recv()
            send(4 + i, relay[i] + part_in[n, i].astype(f32))

    def part_sum(n):
        for i in range(2, 6):
            part_copy(n, i).wait_recv()
        own_part[low_half, :] += part_in[n, 3].astype(f32) + part_in[n, 4].astype(f32)
        own_part[high_half, :] += part_in[n, 2].astype(f32) + part_in[n, 5].astype(f32)
        for i in range(6):
            part_copy(n, i).wait_send()

    def core_copy(n):
        return remote(core_out.at[n], core_in.at[n], core_sem.at[0, n], core_sem.at[1, n], tag="core", emb=partner)

    def weight_grad(n, source, delta):
        @pl.loop(0, SEC)
        def _(r):
            whole[n, pl.ds(r * 16, 16)] = mm_nt(source[r], delta).reshape(16, 32, WIDE)

        @pl.loop(0, 32)
        def _(j):
            core_out[n, j] = whole[n, 2 * j + 1 - core].astype(bf16)

        core_copy(n).start()

    def x_copy(n, d):
        to = lax.rem(x + d, XS)
        return remote(
            x_out.at[n, to], x_in.at[n, x], x_sem.at[n, 0, d], x_sem.at[n, 1, x], tag="x", emb=(to * ZS + z) * 2 + core
        )

    def x_arrive(n, d):
        to = lax.rem(x + d, XS)
        return remote(
            x_out.at[n, to], x_in.at[n, to], x_sem.at[n, 0, d], x_sem.at[n, 1, to], tag="x", emb=(to * ZS + z) * 2 + core
        )

    def z_copy(n, d):
        to = lax.rem(z + d, ZS)
        return remote(
            z_out.at[n, to], z_in.at[n, z], z_sem.at[n, 0, d], z_sem.at[n, 1, z], tag="z", emb=(x * ZS + to) * 2 + core
        )

    def z_arrive(n, d):
        to = lax.rem(z + d, ZS)
        return remote(
            z_out.at[n, to], z_in.at[n, to], z_sem.at[n, 0, d], z_sem.at[n, 1, to], tag="z", emb=(x * ZS + to) * 2 + core
        )

    def core_sum(n):
        core_copy(n).wait()

        @pl.loop(0, 32)
        def _(j):
            value = whole[n, 2 * j + core] + core_in[n, j].astype(f32)
            whole[n, 2 * j + core] = value
            x_out[n, lax.div(j, ZS), lax.rem(j, ZS)] = value.astype(bf16)

        for d in (2, 1, 3):
            x_copy(n, d).start()

    def x_sum(n):
        for d in (1, 3, 2):
            x_arrive(n, d).wait_recv()

        @pl.loop(0, ZS)
        def _(j):
            at = 2 * (x * ZS + j) + core
            value = whole[n, at]
            for d in range(1, XS):
                value = value + x_in[n, lax.rem(x + d, XS), j].astype(f32)
            whole[n, at] = value
            z_out[n, j] = value.astype(bf16)

        for d in range(1, ZS):
            z_copy(n, d).start()

    def z_sum(n):
        for d in range(1, ZS):
            z_arrive(n, d).wait_recv()
        value = whole[n, me]
        for d in range(1, ZS):
            value = value + z_in[n, lax.rem(z + d, ZS)].astype(f32)
        packed_ref[pl.ds(32 * n, 32), :] = value
        for d in range(1, XS):
            x_copy(n, d).wait_send()
        for d in range(1, ZS):
            z_copy(n, d).wait_send()

    def hc_copy():
        return remote(head_core.at[0], head_core.at[1], hcore_sem.at[0], hcore_sem.at[1], tag="head", emb=partner)

    def hx_copy(d, at):
        to = lax.rem(x + d, XS)
        return remote(head_x.at[x], head_x.at[at], hx_sem.at[0, d], hx_sem.at[1, at], tag="head", emb=(to * ZS + z) * 2 + core)

    def hz_copy(d, at):
        to = lax.rem(z + d, ZS)
        return remote(head_z.at[z], head_z.at[at], hz_sem.at[0, d], hz_sem.at[1, at], tag="head", emb=(x * ZS + to) * 2 + core)

    part(0, tower_ref, tower_delta)
    head_core[0] = lax.dot_general(
        back, active, (((1,), (1,)), ((), ())), preferred_element_type=f32, precision=lax.Precision.HIGHEST
    )
    hc_copy().start()
    weight_grad(0, hiddens, tower_delta)
    hc_copy().wait()
    head_x[x] = head_core[0] + head_core[1]
    for d in range(1, XS):
        hx_copy(d, x).start()
    core_sum(0)
    left(feats, feat_sem, "feats")
    left(hiddens, hidden_sem, "hiddens")
    for d in (2, 1, 3):
        sec_copy(shares, share_sem, "shares", d, sec).wait_send()
    for d in range(1, XS):
        hx_copy(d, lax.rem(x + d, XS)).wait_recv()
    head_z[z] = (head_x[0] + head_x[1]) + (head_x[2] + head_x[3])
    for d in range(1, ZS):
        hz_copy(d, z).start()

    part_sum(0)
    expert_delta = (own_part[...] * silu_slope(pre_e[...])).astype(bf16)
    part(1, expert_ref, expert_delta)
    weight_grad(1, feats, expert_delta)
    x_sum(0)
    core_sum(1)
    part_sum(1)

    @pl.loop(0, SLOTS)
    def _(s):
        grad = own_part[pl.ds(pl.multiple_of(s * DIM, DIM), DIM), :]
        for k in range(2):
            low = jnp.where(bag_ref[pl.ds(s, 1), :] > k, (pos[2 * s + k] >> 7) & 7, -1)
            columns = pl.ds(pl.multiple_of((2 * s + k) * BATCH, BATCH), BATCH)
            for g in range(8):
                spread[g * DIM : (g + 1) * DIM, columns] = jnp.where(low == g, grad, 0.0).astype(bf16)

    @pl.loop(0, 4)
    def _(t):
        pair = lax.rem(x + t, 4)

        for q in range(2 * SLOTS):
            place = pos[q]
            key = ((place >> 10) - 2 * pair) * CAP + (place & (CAP - 1))
            hots[:, q * BATCH : (q + 1) * BATCH] = hot(2 * CAP, key)
        total = mm_nt(spread[...], hots[...]).astype(bf16)
        for h in range(2):
            for g in range(8):
                peer = (2 * pair + h) * 8 + g
                out_grads[peer] = total[g * DIM : (g + 1) * DIM, h * CAP : (h + 1) * CAP]

                @pl.when(peer != me)
                def _():
                    grad_copy(peer, me).start()

                @pl.when(peer == me)
                def _():
                    in_grads[me] = total[g * DIM : (g + 1) * DIM, h * CAP : (h + 1) * CAP]

    x_sum(1)
    z_sum(0)
    for d in range(1, ZS):
        hz_copy(d, lax.rem(z + d, ZS)).wait_recv()
    head = head_z[0]
    for j in range(1, ZS):
        head = head + head_z[j]
    packed_ref[64:72, :] = jnp.broadcast_to(head, (8, WIDE))

    grad_ref[...] = jnp.zeros((WIDE, ROWS), f32)

    @pl.loop(0, XS)
    def _(t):
        first = lax.rem(x + XS - t, XS) * 16

        @pl.loop(0, 16)
        def _(j):
            peer = first + j

            @pl.when(peer != me)
            def _():
                grad_copy(peer, peer).wait_recv()

        if "scatter" not in SKIP:

            @pl.loop(0, 8)
            def _(j):
                a = first + 2 * j
                keys = jnp.concatenate([ib[a], ib[a + 1]], axis=1)
                slot = keys >> 9
                grads = jnp.concatenate([in_grads[a], in_grads[a + 1]], axis=1).astype(f32)
                wide = jnp.concatenate([jnp.where(slot == s, grads, 0.0) for s in range(SLOTS)], axis=0).astype(bf16)
                columns = pl.ds(pl.multiple_of(j * 2 * CAP, 2 * CAP), 2 * CAP)
                spread[:, columns] = wide
                row_hots[:, columns] = hot(ROWS, keys & (ROWS - 1))

            grad_ref[...] += mm_nt(spread[:, : 16 * CAP], row_hots[...])

    z_sum(1)
    for d in range(1, XS):
        hx_copy(d, x).wait_send()
    for d in range(1, ZS):
        hz_copy(d, z).wait_send()

    @pl.loop(1, EMB)
    def _(d):
        peer = lax.rem(me + d, EMB)
        id_copy(peer, me).wait_send()
        row_copy(peer, me).wait_send()
        grad_copy(peer, me).wait_send()


def body(
    emb_table,
    emb_accum,
    slot_ids,
    bag_len,
    expert_w,
    tower_w,
    tower_out,
    section_task,
    click_like,
    watch,
):
    vmem = pl.BlockSpec(memory_space=pltpu.VMEM)
    dma = pltpu.SemaphoreType.DMA
    table = emb_table.transpose(0, 2, 1).reshape(SLOTS * DIM, ROWS)
    accum = emb_accum.transpose(0, 2, 1).reshape(SLOTS * DIM, ROWS)
    anywhere = pl.BlockSpec(memory_space=pl.ANY)
    row_grad, packed = pl.pallas_call(
        step_kernel,
        out_shape=(
            jax.ShapeDtypeStruct((SLOTS * DIM, ROWS), f32),
            jax.ShapeDtypeStruct((72, WIDE), f32),
        ),
        in_specs=[pl.BlockSpec(memory_space=pltpu.SMEM), vmem, vmem, vmem, anywhere, anywhere, vmem, vmem, vmem],
        out_specs=(vmem,) * 2,
        scratch_shapes=[
            pltpu.VMEM((2 * SLOTS, 1, BATCH), i32),
            pltpu.VMEM((EMB, 1, CAP), i32),
            pltpu.VMEM((EMB, 1, CAP), i32),
            pltpu.VMEM((EMB, DIM, CAP), bf16),
            pltpu.VMEM((EMB, DIM, CAP), bf16),
            pltpu.VMEM((8 * DIM, 4 * CAP), bf16),
            pltpu.VMEM((8 * DIM, BATCH), f32),
            pltpu.VMEM((SLOTS * DIM, ROWS), bf16),
            pltpu.VMEM((SEC * WIDE, WIDE), bf16),
            pltpu.VMEM((SEC * WIDE, WIDE), bf16),
            pltpu.VMEM((SEC, WIDE, BATCH), bf16),
            pltpu.VMEM((SEC, WIDE, BATCH), bf16),
            pltpu.VMEM((SEC, WIDE, WIDE), bf16),
            pltpu.VMEM((SEC, WIDE, WIDE), bf16),
            pltpu.VMEM((WIDE, BATCH), f32),
            pltpu.VMEM((WIDE, BATCH), f32),
            pltpu.VMEM((SEC, 8, BATCH), f32),
            pltpu.VMEM((2, 6, WIDE // 2, BATCH), bf16),
            pltpu.VMEM((2, 6, WIDE // 2, BATCH), bf16),
            pltpu.VMEM((2, WIDE // 2, BATCH), f32),
            pltpu.VMEM((2, EMB, 32, WIDE), f32),
            pltpu.VMEM((WIDE, BATCH), f32),
            pltpu.VMEM((2, 32, 32, WIDE), bf16),
            pltpu.VMEM((2, 32, 32, WIDE), bf16),
            pltpu.VMEM((2, XS, ZS, 32, WIDE), bf16),
            pltpu.VMEM((2, XS, ZS, 32, WIDE), bf16),
            pltpu.VMEM((2, ZS, 32, WIDE), bf16),
            pltpu.VMEM((2, ZS, 32, WIDE), bf16),
            pltpu.VMEM((2, 1, WIDE), f32),
            pltpu.VMEM((XS, 1, WIDE), f32),
            pltpu.VMEM((ZS, 1, WIDE), f32),
            pltpu.VMEM((8 * DIM, 2 * SLOTS * BATCH), bf16),
            pltpu.VMEM((2 * CAP, 2 * SLOTS * BATCH), bf16),
            pltpu.VMEM((ROWS, 16 * CAP), bf16),
            pltpu.VMEM((EMB, DIM, CAP), bf16),
            pltpu.VMEM((EMB, DIM, CAP), bf16),
            dma((2,)),
            dma((EMB,)),
            dma((EMB,)),
            dma((EMB,)),
            dma((EMB,)),
            dma((2, 6)),
            dma((2, 6)),
            dma((2, SEC)),
            dma((2, 2, 6)),
            dma((2, 2)),
            dma((2, 2, XS)),
            dma((2, 2, ZS)),
            dma((2,)),
            dma((2, XS)),
            dma((2, ZS)),
            dma((EMB,)),
            dma((EMB,)),
        ],
        compiler_params=pltpu.CompilerParams(collective_id=0, has_side_effects=True, vmem_limit_bytes=60 << 20),
    )(
        section_task,
        slot_ids.transpose(1, 2, 0),
        bag_len.T,
        table,
        expert_w,
        tower_w,
        tower_out,
        click_like.T,
        watch.reshape(1, BATCH),
    )
    tower_grad, expert_grad, head_grad = packed[:32], packed[32:64], packed[64:65]
    new_accum = accum + row_grad * row_grad
    new_table = table - learn_rate * row_grad / jnp.sqrt(new_accum)

    def back(value):
        return value.reshape(SLOTS, DIM, ROWS).transpose(0, 2, 1)

    return (back(new_table), back(new_accum), expert_grad, tower_grad, head_grad)


def solution(mesh):
    placed = (
        P("sec", "emb", None),
        P("sec", "emb", None),
        P("emb", "sec", None),
        P("emb", "sec"),
        P(None, "sec"),
        P(None, "sec"),
        P("sec", None),
        P("sec"),
        P("emb", None),
        P("emb"),
    )
    return jax.shard_map(
        body,
        mesh=mesh,
        in_specs=placed,
        out_specs=(
            P("sec", "emb", None),
            P("sec", "emb", None),
            P("emb", "sec"),
            P("emb", "sec"),
            P("sec", None),
        ),
        check_vma=False,
    )
```

```python
import jax
import jax.numpy as jnp
from jax import lax
from jax.experimental import pallas as pl
from jax.experimental.pallas import tpu as pltpu
from jax.sharding import PartitionSpec as P

MESH = pl.DeviceIdType.MESH
learn_rate = 0.2
f32 = jnp.float32
bf16 = jnp.bfloat16
i32 = jnp.int32

EMB = 64
SEC = 4
XS = 4
ZS = 8
CAP = 128
DIM = 64
SLOTS = 8
BATCH = 256
ROWS = 512
WIDE = 512


def mm(a, b):
    return lax.dot_general(a, b, (((1,), (0,)), ((), ())), preferred_element_type=f32)


def mm_nt(a, b):
    return lax.dot_general(a, b, (((1,), (1,)), ((), ())), preferred_element_type=f32)


def silu_slope(value):
    logistic = jax.nn.sigmoid(value)
    return logistic * (1.0 + value * (1.0 - logistic))


def hot(size, keys):
    rows = lax.broadcasted_iota(i32, (size, keys.shape[1]), 0)
    return jnp.where(rows == keys, 1.0, 0.0).astype(bf16)


SKIP = ()


class Nothing:
    def start(self):
        pass

    wait = wait_send = wait_recv = start


def remote(src, dst, send, recv, tag, **where):
    if tag in SKIP:
        return Nothing()
    return pltpu.make_async_remote_copy(
        src_ref=src, dst_ref=dst, send_sem=send, recv_sem=recv, device_id=where, device_id_type=MESH
    )


def greet(emb, sec):
    barrier = pltpu.get_barrier_semaphore()

    @pl.loop(1, EMB)
    def _(d):
        pl.semaphore_signal(barrier, inc=1, device_id={"emb": lax.rem(emb + d, EMB)}, device_id_type=MESH)

    for d in range(1, SEC):
        pl.semaphore_signal(barrier, inc=1, device_id={"sec": lax.rem(sec + d, SEC)}, device_id_type=MESH)


def meet():
    pl.semaphore_wait(pltpu.get_barrier_semaphore(), EMB - 1 + SEC - 1)


def route(ids_ref, ob, pos):
    before = lax.broadcasted_iota(i32, (BATCH, BATCH), 0)
    after = lax.broadcasted_iota(i32, (BATCH, BATCH), 1)
    upper = jnp.where(before < after, 1.0, 0.0).astype(bf16)
    shard_row = lax.broadcasted_iota(i32, (EMB, BATCH), 0)
    rank_row = lax.broadcasted_iota(i32, (CAP, BATCH), 0)
    carry = jnp.zeros((EMB, 1), f32)
    total = jnp.zeros((EMB, 2 * CAP), f32)
    for q in range(2 * SLOTS):
        ids = ids_ref[q // 2, q % 2 : q % 2 + 1, :]
        owner = ids >> 9
        key = (ids & (ROWS - 1)) + ((q // 2) * ROWS + 1)
        owned = jnp.where(shard_row == owner, 1.0, 0.0)
        owned_b = owned.astype(bf16)
        prefix = mm(owned_b, upper) + carry
        rank = jnp.sum(owned * prefix, axis=0, keepdims=True).astype(i32)
        carry = carry + jnp.sum(owned, axis=1, keepdims=True)
        pos[q] = owner * CAP + rank
        ranked = rank_row == rank
        high = jnp.where(ranked, (key >> 6).astype(f32), 0.0).astype(bf16)
        low = jnp.where(ranked, (key & 63).astype(f32), 0.0).astype(bf16)
        total = total + mm_nt(owned_b, jnp.concatenate([high, low], axis=0))
    keys = (total[:, :CAP] * 64.0 + total[:, CAP:]).astype(i32) - 1
    for s in range(EMB):
        ob[s] = keys[s : s + 1, :]


def step_kernel(
    task_ref, ids_ref, bag_ref, table_ref, expert_hbm, tower_hbm, out_row_ref, click_ref, watch_ref,
    grad_ref, packed_ref,
    pos, ob, ib, out_rows, in_rows, wide_rows, pooled_ref, tb, expert_ref, tower_ref,
    feats, hiddens, expert_t, tower_t, pre_e, pre_t, shares, part_out, part_in, relay, whole, own_part,
    core_out, core_in, x_out, x_in, z_out, z_in, head_core, head_x, head_z,
    spread, hots, row_hots, out_grads, in_grads,
    load_sem, id_send, id_recv, row_send, row_recv,
    feat_sem, hidden_sem, share_sem, part_sem, core_sem, x_sem, z_sem, hcore_sem, hx_sem, hz_sem, grad_send, grad_recv,
):
    me = lax.axis_index("emb")
    sec = lax.axis_index("sec")
    core = lax.rem(me, 2)
    z = lax.rem(lax.div(me, 2), ZS)
    x = lax.div(me, 2 * ZS)
    half = lax.div(me, 32)
    inner = lax.rem(me, 32)
    partner = me + 1 - 2 * core
    expert_load = pltpu.make_async_copy(expert_hbm, expert_ref, load_sem.at[0])
    tower_load = pltpu.make_async_copy(tower_hbm, tower_ref, load_sem.at[1])
    expert_load.start()
    tower_load.start()
    greet(me, sec)
    route(ids_ref, ob, pos)
    meet()

    def rows_of(r):
        return pl.ds(pl.multiple_of(r * WIDE, WIDE), WIDE)

    def ahead(d):
        group = lax.rem(half + lax.div(d, 32), 2)
        return group * 32 + lax.rem(inner + d, 32)

    def behind(d):
        group = lax.rem(half + lax.div(d, 32), 2)
        return group * 32 + lax.rem(inner + 64 - d, 32)

    def id_copy(peer, at):
        return remote(ob.at[peer], ib.at[at], id_send.at[peer], id_recv.at[at], tag="ids", emb=peer)

    def row_copy(peer, at):
        return remote(out_rows.at[peer], in_rows.at[at], row_send.at[peer], row_recv.at[at], tag="rows", emb=peer)

    def grad_copy(peer, at):
        return remote(out_grads.at[peer], in_grads.at[at], grad_send.at[peer], grad_recv.at[at], tag="grads", emb=peer)

    def across(d):
        return lax.rem(sec + d, SEC)

    def sec_copy(buffer, sems, tag, d, at):
        return remote(buffer.at[sec], buffer.at[at], sems.at[0, d], sems.at[1, at], tag=tag, sec=across(d))

    def ring_copy(buffer, sems, tag, i, arriving=False):
        offset, part, way = ((0, 0, 1), (0, 1, 1), (0, 1, 3), (0, 0, 3), (3, 0, 1), (1, 1, 3))[i]
        rows = pl.ds(part * (WIDE // 2), WIDE // 2)
        source = across(offset)
        target = across(4 - way + offset) if arriving else source
        return remote(
            buffer.at[source, rows], buffer.at[target, rows], sems.at[0, i], sems.at[1, i], tag=tag, sec=across(way)
        )

    def gather_sec(buffer, sems, tag, weights, total):
        def came(i):
            ring_copy(buffer, sems, tag, i, True).wait_recv()

        total[...] = mm(weights[sec], buffer[sec])
        came(0)
        ring_copy(buffer, sems, tag, 4).start()
        came(2)
        ring_copy(buffer, sems, tag, 5).start()
        came(1)
        total[...] += mm(weights[across(3)], buffer[across(3)])
        came(3)
        total[...] += mm(weights[across(1)], buffer[across(1)])
        came(4)
        came(5)
        total[...] += mm(weights[across(2)], buffer[across(2)])

    def left(buffer, sems, tag):
        for i in range(6):
            ring_copy(buffer, sems, tag, i).wait_send()

    @pl.loop(1, EMB)
    def _(d):
        id_copy(ahead(d), me).start()

    ib[me] = ob[me]
    tb[...] = table_ref[...].astype(bf16)
    expert_load.wait()
    tower_load.wait()

    if "transpose" not in SKIP:

        @pl.loop(0, SEC)
        def _(r):
            expert_t[r] = expert_ref[rows_of(r), :].T
            tower_t[r] = tower_ref[rows_of(r), :].T

    @pl.loop(0, EMB // 2)
    def _(t):
        a = behind(2 * t)
        b = behind(2 * t + 1)

        @pl.when(t > 0)
        def _():
            id_copy(a, a).wait_recv()

        id_copy(b, b).wait_recv()
        if "gather" not in SKIP:
            keys = jnp.concatenate([ib[a], ib[b]], axis=1)
            slot = keys >> 9
            picked = mm(tb[...], hot(ROWS, keys & (ROWS - 1)))
            rows = jnp.zeros((DIM, 2 * CAP), f32)
            for s in range(SLOTS):
                rows = rows + jnp.where(slot == s, picked[s * DIM : (s + 1) * DIM], 0.0)
            rows = rows.astype(bf16)
            out_rows[a] = rows[:, :CAP]
            out_rows[b] = rows[:, CAP:]

            @pl.when(t == 0)
            def _():
                in_rows[me] = rows[:, :CAP]

        @pl.when(t > 0)
        def _():
            row_copy(a, me).start()

        row_copy(b, me).start()

    def widen(part):
        for h in range(4):
            wide_rows[:, h * CAP : (h + 1) * CAP] = in_rows[pl.ds((part * 4 + h) * 8, 8)].reshape(8 * DIM, CAP)

    def pool(part, first, begin, end):
        @pl.loop(begin, end)
        def _(s):
            rows = pl.ds(pl.multiple_of(s * DIM, DIM), DIM)
            pooled = jnp.zeros((DIM, BATCH), f32) if first else pooled_ref[rows, :]
            for k in range(2):
                place = pos[2 * s + k]
                shard = place >> 7
                low = jnp.where(bag_ref[pl.ds(s, 1), :] > k, shard & 7, -1)
                key = ((shard >> 3) - part * 4) * CAP + (place & (CAP - 1))
                picked = mm(wide_rows[...], hot(4 * CAP, key))
                for g in range(8):
                    pooled = pooled + jnp.where(low == g, picked[g * DIM : (g + 1) * DIM], 0.0)
            if first:
                pooled_ref[rows, :] = pooled
            else:
                feats[sec, rows, :] = pooled.astype(bf16)

    @pl.loop(1, 32)
    def _(d):
        peer = ahead(d)
        row_copy(peer, peer).wait_recv()

    widen(half)
    pool(half, True, 0, SLOTS)

    @pl.loop(32, EMB)
    def _(d):
        peer = ahead(d)
        row_copy(peer, peer).wait_recv()

    widen(1 - half)
    pool(1 - half, False, 0, SLOTS // 2)
    ring_copy(feats, feat_sem, "feats", 0).start()
    ring_copy(feats, feat_sem, "feats", 3).start()
    pool(1 - half, False, SLOTS // 2, SLOTS)
    ring_copy(feats, feat_sem, "feats", 2).start()
    ring_copy(feats, feat_sem, "feats", 1).start()
    gather_sec(feats, feat_sem, "feats", expert_t, pre_e)
    hiddens[sec] = jax.nn.silu(pre_e[...]).astype(bf16)
    for i in (0, 2, 1, 3):
        ring_copy(hiddens, hidden_sem, "hiddens", i).start()
    gather_sec(hiddens, hidden_sem, "hiddens", tower_t, pre_t)
    out_col = jnp.broadcast_to(out_row_ref[...], (8, WIDE)).T[:, 0:1]
    active = jax.nn.silu(pre_t[...])
    share = jnp.sum(active * out_col, axis=0, keepdims=True)
    chosen = jnp.where(lax.broadcasted_iota(i32, (8, BATCH), 0) == task_ref[0], 1.0, 0.0)
    shares[sec] = share * chosen
    for d in (2, 1, 3):
        sec_copy(shares, share_sem, "shares", d, sec).start()
    slope = out_col * silu_slope(pre_t[...])
    for d in (1, 3, 2):
        sec_copy(shares, share_sem, "shares", d, across(d)).wait_recv()
    logits = (shares[0] + shares[1]) + (shares[2] + shares[3])
    err = logits[0:1] + logits[1:2] + logits[2:3] - watch_ref[...]
    chance = jax.nn.sigmoid(logits[0:2]) - click_ref[...] + err
    back = chance[0:1] * chosen[0:1] + chance[1:2] * chosen[1:2] + err * chosen[2:3]
    tower_delta = (back * slope).astype(bf16)

    low_half = slice(0, WIDE // 2)
    high_half = slice(WIDE // 2, WIDE)

    def part_copy(n, i):
        return remote(
            part_out.at[n, i], part_in.at[n, i], part_sem.at[n, 0, i], part_sem.at[n, 1, i],
            tag="part", sec=across((1, 3, 1, 3, 1, 3)[i]),
        )

    def part(n, weights_ref, delta):
        def send(i, value):
            part_out[n, i] = value.astype(bf16)
            part_copy(n, i).start()

        value = mm(weights_ref[rows_of(across(2)), :], delta)
        send(0, value[low_half])
        send(1, value[high_half])
        value = mm(weights_ref[rows_of(across(1)), :], delta)
        send(2, value[high_half])
        relay[0] = value[low_half]
        value = mm(weights_ref[rows_of(across(3)), :], delta)
        send(3, value[low_half])
        relay[1] = value[high_half]
        own_part[...] = mm(weights_ref[rows_of(sec), :], delta)
        for i in range(2):
            part_copy(n, i).wait_recv()
            send(4 + i, relay[i] + part_in[n, i].astype(f32))

    def part_sum(n):
        for i in range(2, 6):
            part_copy(n, i).wait_recv()
        own_part[low_half, :] += part_in[n, 3].astype(f32) + part_in[n, 4].astype(f32)
        own_part[high_half, :] += part_in[n, 2].astype(f32) + part_in[n, 5].astype(f32)
        for i in range(6):
            part_copy(n, i).wait_send()

    def core_copy(n):
        return remote(core_out.at[n], core_in.at[n], core_sem.at[0, n], core_sem.at[1, n], tag="core", emb=partner)

    def weight_grad(n, source, delta):
        @pl.loop(0, SEC)
        def _(r):
            whole[n, pl.ds(r * 16, 16)] = mm_nt(source[r], delta).reshape(16, 32, WIDE)

        @pl.loop(0, 32)
        def _(j):
            core_out[n, j] = whole[n, 2 * j + 1 - core].astype(bf16)

        core_copy(n).start()

    def x_copy(n, i):
        to = lax.rem(x + (1, 3, 1, 3, 1, 3)[i], XS)
        return remote(
            x_out.at[n, i], x_in.at[n, i], x_sem.at[n, 0, i], x_sem.at[n, 1, i], tag="x", emb=(to * ZS + z) * 2 + core
        )

    def z_copy(n, d):
        to = lax.rem(z + d, ZS)
        return remote(
            z_out.at[n, to], z_in.at[n, z], z_sem.at[n, 0, d], z_sem.at[n, 1, z], tag="z", emb=(x * ZS + to) * 2 + core
        )

    def z_arrive(n, d):
        to = lax.rem(z + d, ZS)
        return remote(
            z_out.at[n, to], z_in.at[n, to], z_sem.at[n, 0, d], z_sem.at[n, 1, to], tag="z", emb=(x * ZS + to) * 2 + core
        )

    def core_sum(n):
        core_copy(n).wait()

        @pl.loop(0, 32)
        def _(j):
            value = whole[n, 2 * j + core] + core_in[n, j].astype(f32)
            whole[n, 2 * j + core] = value

        for i, (d, part) in enumerate(((2, 0), (2, 1), (1, 1), (3, 0))):

            @pl.loop(0, ZS // 2)
            def _(j):
                x_out[n, i, j] = whole[n, place_of(d, part * (ZS // 2) + j)].astype(bf16)

            x_copy(n, i).start()

    def place_of(d, j):
        return 2 * (lax.rem(x + d, XS) * ZS + j) + core

    def x_relay(n):
        for i, d in ((0, 1), (1, 3)):
            x_copy(n, i).wait_recv()

            @pl.loop(0, ZS // 2)
            def _(j):
                value = whole[n, place_of(d, i * (ZS // 2) + j)] + x_in[n, i, j].astype(f32)
                x_out[n, 4 + i, j] = value.astype(bf16)

            x_copy(n, 4 + i).start()

    def x_sum(n):
        for part, (one, two) in enumerate(((3, 4), (2, 5))):
            x_copy(n, one).wait_recv()
            x_copy(n, two).wait_recv()

            @pl.loop(0, ZS // 2)
            def _(j):
                at = part * (ZS // 2) + j
                value = whole[n, place_of(0, at)] + x_in[n, one, j].astype(f32) + x_in[n, two, j].astype(f32)
                whole[n, place_of(0, at)] = value
                z_out[n, at] = value.astype(bf16)

        for d in range(1, ZS):
            z_copy(n, d).start()

    def z_sum(n):
        for d in range(1, ZS):
            z_arrive(n, d).wait_recv()
        value = whole[n, me]
        for d in range(1, ZS):
            value = value + z_in[n, lax.rem(z + d, ZS)].astype(f32)
        packed_ref[pl.ds(32 * n, 32), :] = value
        for i in range(6):
            x_copy(n, i).wait_send()
        for d in range(1, ZS):
            z_copy(n, d).wait_send()

    def hc_copy():
        return remote(head_core.at[0], head_core.at[1], hcore_sem.at[0], hcore_sem.at[1], tag="head", emb=partner)

    def hx_copy(d, at):
        to = lax.rem(x + d, XS)
        return remote(head_x.at[x], head_x.at[at], hx_sem.at[0, d], hx_sem.at[1, at], tag="head", emb=(to * ZS + z) * 2 + core)

    def hz_copy(d, at):
        to = lax.rem(z + d, ZS)
        return remote(head_z.at[z], head_z.at[at], hz_sem.at[0, d], hz_sem.at[1, at], tag="head", emb=(x * ZS + to) * 2 + core)

    part(0, tower_ref, tower_delta)
    head_core[0] = lax.dot_general(
        back, active, (((1,), (1,)), ((), ())), preferred_element_type=f32, precision=lax.Precision.HIGHEST
    )
    hc_copy().start()
    weight_grad(0, hiddens, tower_delta)
    hc_copy().wait()
    head_x[x] = head_core[0] + head_core[1]
    for d in range(1, XS):
        hx_copy(d, x).start()
    core_sum(0)
    left(feats, feat_sem, "feats")
    left(hiddens, hidden_sem, "hiddens")
    for d in (2, 1, 3):
        sec_copy(shares, share_sem, "shares", d, sec).wait_send()
    for d in range(1, XS):
        hx_copy(d, lax.rem(x + d, XS)).wait_recv()
    head_z[z] = (head_x[0] + head_x[1]) + (head_x[2] + head_x[3])
    for d in range(1, ZS):
        hz_copy(d, z).start()

    part_sum(0)
    expert_delta = (own_part[...] * silu_slope(pre_e[...])).astype(bf16)
    part(1, expert_ref, expert_delta)
    x_relay(0)
    weight_grad(1, feats, expert_delta)
    core_sum(1)
    part_sum(1)

    @pl.loop(0, SLOTS)
    def _(s):
        grad = own_part[pl.ds(pl.multiple_of(s * DIM, DIM), DIM), :]
        for k in range(2):
            low = jnp.where(bag_ref[pl.ds(s, 1), :] > k, (pos[2 * s + k] >> 7) & 7, -1)
            columns = pl.ds(pl.multiple_of((2 * s + k) * BATCH, BATCH), BATCH)
            for g in range(8):
                spread[g * DIM : (g + 1) * DIM, columns] = jnp.where(low == g, grad, 0.0).astype(bf16)

    @pl.loop(0, 4)
    def _(t):
        pair = lax.rem(x + t, 4)

        for q in range(2 * SLOTS):
            place = pos[q]
            key = ((place >> 10) - 2 * pair) * CAP + (place & (CAP - 1))
            hots[:, q * BATCH : (q + 1) * BATCH] = hot(2 * CAP, key)
        total = mm_nt(spread[...], hots[...]).astype(bf16)
        for h in range(2):
            for g in range(8):
                peer = (2 * pair + h) * 8 + g
                out_grads[peer] = total[g * DIM : (g + 1) * DIM, h * CAP : (h + 1) * CAP]

                @pl.when(peer != me)
                def _():
                    grad_copy(peer, me).start()

                @pl.when(peer == me)
                def _():
                    in_grads[me] = total[g * DIM : (g + 1) * DIM, h * CAP : (h + 1) * CAP]

        @pl.when(t == 0)
        def _():
            x_relay(1)
            x_sum(0)

    x_sum(1)
    z_sum(0)
    for d in range(1, ZS):
        hz_copy(d, lax.rem(z + d, ZS)).wait_recv()
    head = head_z[0]
    for j in range(1, ZS):
        head = head + head_z[j]
    packed_ref[64:72, :] = jnp.broadcast_to(head, (8, WIDE))

    grad_ref[...] = jnp.zeros((WIDE, ROWS), f32)

    @pl.loop(1, EMB)
    def _(d):
        peer = lax.rem(me + d, EMB)
        id_copy(peer, me).wait_send()
        row_copy(peer, me).wait_send()


    @pl.loop(0, XS)
    def _(t):
        first = lax.rem(x + XS - t, XS) * 16

        @pl.loop(0, 16)
        def _(j):
            peer = first + j

            @pl.when(peer != me)
            def _():
                grad_copy(peer, peer).wait_recv()

        if "scatter" not in SKIP:

            @pl.loop(0, 8)
            def _(j):
                a = first + 2 * j
                keys = jnp.concatenate([ib[a], ib[a + 1]], axis=1)
                slot = keys >> 9
                grads = jnp.concatenate([in_grads[a], in_grads[a + 1]], axis=1).astype(f32)
                wide = jnp.concatenate([jnp.where(slot == s, grads, 0.0) for s in range(SLOTS)], axis=0).astype(bf16)
                columns = pl.ds(pl.multiple_of(j * 2 * CAP, 2 * CAP), 2 * CAP)
                spread[:, columns] = wide
                row_hots[:, columns] = hot(ROWS, keys & (ROWS - 1))

            grad_ref[...] += mm_nt(spread[:, : 16 * CAP], row_hots[...])

    z_sum(1)
    for d in range(1, XS):
        hx_copy(d, x).wait_send()
    for d in range(1, ZS):
        hz_copy(d, z).wait_send()

    @pl.loop(1, EMB)
    def _(d):
        peer = lax.rem(me + d, EMB)
        grad_copy(peer, me).wait_send()


def update_kernel(table_ref, accum_ref, grad_ref, packed_ref, new_table, new_accum, tower_grad, expert_grad, head_grad):
    grad = grad_ref[...]
    accum = accum_ref[...] + grad * grad
    new_accum[...] = accum
    new_table[...] = table_ref[...] - learn_rate * grad / jnp.sqrt(accum)

    @pl.when(pl.program_id(0) == 0)
    def _():
        tower_grad[...] = packed_ref[:32, :]
        expert_grad[...] = packed_ref[32:64, :]
        head_grad[...] = packed_ref[64:65, :]


def body(
    emb_table,
    emb_accum,
    slot_ids,
    bag_len,
    expert_w,
    tower_w,
    tower_out,
    section_task,
    click_like,
    watch,
):
    vmem = pl.BlockSpec(memory_space=pltpu.VMEM)
    dma = pltpu.SemaphoreType.DMA
    table = emb_table.transpose(0, 2, 1).reshape(SLOTS * DIM, ROWS)
    accum = emb_accum.transpose(0, 2, 1).reshape(SLOTS * DIM, ROWS)
    anywhere = pl.BlockSpec(memory_space=pl.ANY)
    row_grad, packed = pl.pallas_call(
        step_kernel,
        out_shape=(
            jax.ShapeDtypeStruct((SLOTS * DIM, ROWS), f32),
            jax.ShapeDtypeStruct((72, WIDE), f32),
        ),
        in_specs=[pl.BlockSpec(memory_space=pltpu.SMEM), vmem, vmem, vmem, anywhere, anywhere, vmem, vmem, vmem],
        out_specs=(vmem,) * 2,
        scratch_shapes=[
            pltpu.VMEM((2 * SLOTS, 1, BATCH), i32),
            pltpu.VMEM((EMB, 1, CAP), i32),
            pltpu.VMEM((EMB, 1, CAP), i32),
            pltpu.VMEM((EMB, DIM, CAP), bf16),
            pltpu.VMEM((EMB, DIM, CAP), bf16),
            pltpu.VMEM((8 * DIM, 4 * CAP), bf16),
            pltpu.VMEM((8 * DIM, BATCH), f32),
            pltpu.VMEM((SLOTS * DIM, ROWS), bf16),
            pltpu.VMEM((SEC * WIDE, WIDE), bf16),
            pltpu.VMEM((SEC * WIDE, WIDE), bf16),
            pltpu.VMEM((SEC, WIDE, BATCH), bf16),
            pltpu.VMEM((SEC, WIDE, BATCH), bf16),
            pltpu.VMEM((SEC, WIDE, WIDE), bf16),
            pltpu.VMEM((SEC, WIDE, WIDE), bf16),
            pltpu.VMEM((WIDE, BATCH), f32),
            pltpu.VMEM((WIDE, BATCH), f32),
            pltpu.VMEM((SEC, 8, BATCH), f32),
            pltpu.VMEM((2, 6, WIDE // 2, BATCH), bf16),
            pltpu.VMEM((2, 6, WIDE // 2, BATCH), bf16),
            pltpu.VMEM((2, WIDE // 2, BATCH), f32),
            pltpu.VMEM((2, EMB, 32, WIDE), f32),
            pltpu.VMEM((WIDE, BATCH), f32),
            pltpu.VMEM((2, 32, 32, WIDE), bf16),
            pltpu.VMEM((2, 32, 32, WIDE), bf16),
            pltpu.VMEM((2, 6, ZS // 2, 32, WIDE), bf16),
            pltpu.VMEM((2, 6, ZS // 2, 32, WIDE), bf16),
            pltpu.VMEM((2, ZS, 32, WIDE), bf16),
            pltpu.VMEM((2, ZS, 32, WIDE), bf16),
            pltpu.VMEM((2, 1, WIDE), f32),
            pltpu.VMEM((XS, 1, WIDE), f32),
            pltpu.VMEM((ZS, 1, WIDE), f32),
            pltpu.VMEM((8 * DIM, 2 * SLOTS * BATCH), bf16),
            pltpu.VMEM((2 * CAP, 2 * SLOTS * BATCH), bf16),
            pltpu.VMEM((ROWS, 16 * CAP), bf16),
            pltpu.VMEM((EMB, DIM, CAP), bf16),
            pltpu.VMEM((EMB, DIM, CAP), bf16),
            dma((2,)),
            dma((EMB,)),
            dma((EMB,)),
            dma((EMB,)),
            dma((EMB,)),
            dma((2, 6)),
            dma((2, 6)),
            dma((2, SEC)),
            dma((2, 2, 6)),
            dma((2, 2)),
            dma((2, 2, 6)),
            dma((2, 2, ZS)),
            dma((2,)),
            dma((2, XS)),
            dma((2, ZS)),
            dma((EMB,)),
            dma((EMB,)),
        ],
        compiler_params=pltpu.CompilerParams(collective_id=0, has_side_effects=True, vmem_limit_bytes=60 << 20),
    )(
        section_task,
        slot_ids.transpose(1, 2, 0),
        bag_len.T,
        table,
        expert_w,
        tower_w,
        tower_out,
        click_like.T,
        watch.reshape(1, BATCH),
    )
    tile = pl.BlockSpec((128, ROWS), lambda i: (i, 0))
    piece = pl.BlockSpec((32, WIDE), lambda i: (0, 0))
    line = pl.BlockSpec((1, WIDE), lambda i: (0, 0))
    whole_table = jax.ShapeDtypeStruct((SLOTS * DIM, ROWS), f32)
    new_table, new_accum, tower_grad, expert_grad, head_grad = pl.pallas_call(
        update_kernel,
        grid=(SLOTS * DIM // 128,),
        out_shape=(
            whole_table,
            whole_table,
            jax.ShapeDtypeStruct((32, WIDE), f32),
            jax.ShapeDtypeStruct((32, WIDE), f32),
            jax.ShapeDtypeStruct((1, WIDE), f32),
        ),
        in_specs=[tile, tile, tile, pl.BlockSpec((72, WIDE), lambda i: (0, 0))],
        out_specs=(tile, tile, piece, piece, line),
    )(table, accum, row_grad, packed)

    def back(value):
        return value.reshape(SLOTS, DIM, ROWS).transpose(0, 2, 1)

    return (back(new_table), back(new_accum), expert_grad, tower_grad, head_grad)


def solution(mesh):
    placed = (
        P("sec", "emb", None),
        P("sec", "emb", None),
        P("emb", "sec", None),
        P("emb", "sec"),
        P(None, "sec"),
        P(None, "sec"),
        P("sec", None),
        P("sec"),
        P("emb", None),
        P("emb"),
    )
    return jax.shard_map(
        body,
        mesh=mesh,
        in_specs=placed,
        out_specs=(
            P("sec", "emb", None),
            P("sec", "emb", None),
            P("emb", "sec"),
            P("emb", "sec"),
            P("sec", None),
        ),
        check_vma=False,
    )
```

```python
import jax
import jax.numpy as jnp
from jax import lax
from jax.experimental import pallas as pl
from jax.experimental.pallas import tpu as pltpu
from jax.sharding import PartitionSpec as P

MESH = pl.DeviceIdType.MESH
learn_rate = 0.2
f32 = jnp.float32
bf16 = jnp.bfloat16
i32 = jnp.int32

EMB = 64
SEC = 4
XS = 4
ZS = 8
CAP = 128
DIM = 64
SLOTS = 8
BATCH = 256
ROWS = 512
WIDE = 512


def mm(a, b):
    return lax.dot_general(a, b, (((1,), (0,)), ((), ())), preferred_element_type=f32)


def mm_nt(a, b):
    return lax.dot_general(a, b, (((1,), (1,)), ((), ())), preferred_element_type=f32)


def silu_slope(value):
    logistic = jax.nn.sigmoid(value)
    return logistic * (1.0 + value * (1.0 - logistic))


def hot(size, keys):
    rows = lax.broadcasted_iota(i32, (size, keys.shape[1]), 0)
    return jnp.where(rows == keys, 1.0, 0.0).astype(bf16)


SKIP = ()


class Nothing:
    def start(self):
        pass

    wait = wait_send = wait_recv = start


def remote(src, dst, send, recv, tag, **where):
    if tag in SKIP:
        return Nothing()
    return pltpu.make_async_remote_copy(
        src_ref=src, dst_ref=dst, send_sem=send, recv_sem=recv, device_id=where, device_id_type=MESH
    )


def greet(emb, sec):
    barrier = pltpu.get_barrier_semaphore()

    @pl.loop(1, EMB)
    def _(d):
        pl.semaphore_signal(barrier, inc=1, device_id={"emb": lax.rem(emb + d, EMB)}, device_id_type=MESH)

    for d in range(1, SEC):
        pl.semaphore_signal(barrier, inc=1, device_id={"sec": lax.rem(sec + d, SEC)}, device_id_type=MESH)


def meet():
    pl.semaphore_wait(pltpu.get_barrier_semaphore(), EMB - 1 + SEC - 1)


def route(ids_ref, ob, pos):
    before = lax.broadcasted_iota(i32, (BATCH, BATCH), 0)
    after = lax.broadcasted_iota(i32, (BATCH, BATCH), 1)
    upper = jnp.where(before < after, 1.0, 0.0).astype(bf16)
    shard_row = lax.broadcasted_iota(i32, (EMB, BATCH), 0)
    rank_row = lax.broadcasted_iota(i32, (CAP, BATCH), 0)
    carry = jnp.zeros((EMB, 1), f32)
    total = jnp.zeros((EMB, 2 * CAP), f32)
    for q in range(2 * SLOTS):
        ids = ids_ref[q // 2, q % 2 : q % 2 + 1, :]
        owner = ids >> 9
        key = (ids & (ROWS - 1)) + ((q // 2) * ROWS + 1)
        owned = jnp.where(shard_row == owner, 1.0, 0.0)
        owned_b = owned.astype(bf16)
        prefix = mm(owned_b, upper) + carry
        rank = jnp.sum(owned * prefix, axis=0, keepdims=True).astype(i32)
        carry = carry + jnp.sum(owned, axis=1, keepdims=True)
        pos[q] = owner * CAP + rank
        ranked = rank_row == rank
        high = jnp.where(ranked, (key >> 6).astype(f32), 0.0).astype(bf16)
        low = jnp.where(ranked, (key & 63).astype(f32), 0.0).astype(bf16)
        total = total + mm_nt(owned_b, jnp.concatenate([high, low], axis=0))
    keys = (total[:, :CAP] * 64.0 + total[:, CAP:]).astype(i32) - 1
    for s in range(EMB):
        ob[s] = keys[s : s + 1, :]


def step_kernel(
    task_ref, ids_ref, bag_ref, table_ref, expert_hbm, tower_hbm, out_row_ref, click_ref, watch_ref,
    grad_ref, packed_ref,
    pos, ob, ib, out_rows, in_rows, wide_rows, pooled_ref, tb, expert_ref, tower_ref,
    feats, hiddens, expert_t, tower_t, pre_e, pre_t, shares, part_out, part_in, relay, whole, own_part,
    core_out, core_in, x_out, x_in, z_out, z_in, head_core, head_x, head_z,
    spread, hots, row_hots, out_grads, in_grads,
    load_sem, id_send, id_recv, row_send, row_recv,
    feat_sem, hidden_sem, share_sem, part_sem, core_sem, x_sem, z_sem, hcore_sem, hx_sem, hz_sem, grad_send, grad_recv,
):
    me = lax.axis_index("emb")
    sec = lax.axis_index("sec")
    core = lax.rem(me, 2)
    z = lax.rem(lax.div(me, 2), ZS)
    x = lax.div(me, 2 * ZS)
    half = lax.div(me, 32)
    inner = lax.rem(me, 32)
    partner = me + 1 - 2 * core
    expert_load = pltpu.make_async_copy(expert_hbm, expert_ref, load_sem.at[0])
    tower_load = pltpu.make_async_copy(tower_hbm, tower_ref, load_sem.at[1])
    expert_load.start()
    tower_load.start()
    greet(me, sec)
    route(ids_ref, ob, pos)
    meet()

    def rows_of(r):
        return pl.ds(pl.multiple_of(r * WIDE, WIDE), WIDE)

    def ahead(d):
        group = lax.rem(half + lax.div(d, 32), 2)
        return group * 32 + lax.rem(inner + d, 32)

    def z_shift(i):
        step, odd = lax.div(i + 1, 2), lax.rem(i, 2)
        return lax.rem(step * odd + (ZS - step) * (1 - odd), ZS)

    def chip(t, way):
        group = lax.rem(half + lax.div(t, 16), 2)
        column = 2 * group + lax.rem(x + lax.div(t, ZS), 2)
        return (column * ZS + lax.rem(z + ZS + way * z_shift(lax.rem(t, ZS)), ZS)) * 2

    def id_copy(peer, at):
        return remote(ob.at[peer], ib.at[at], id_send.at[peer], id_recv.at[at], tag="ids", emb=peer)

    def row_copy(peer, at):
        return remote(out_rows.at[peer], in_rows.at[at], row_send.at[peer], row_recv.at[at], tag="rows", emb=peer)

    def grad_copy(peer, at):
        return remote(out_grads.at[peer], in_grads.at[at], grad_send.at[peer], grad_recv.at[at], tag="grads", emb=peer)

    def across(d):
        return lax.rem(sec + d, SEC)

    def sec_copy(buffer, sems, tag, d, at):
        return remote(buffer.at[sec], buffer.at[at], sems.at[0, d], sems.at[1, at], tag=tag, sec=across(d))

    def ring_copy(buffer, sems, tag, i, arriving=False):
        offset, part, way = ((0, 0, 1), (0, 1, 1), (0, 1, 3), (0, 0, 3), (3, 0, 1), (1, 1, 3))[i]
        rows = pl.ds(part * (WIDE // 2), WIDE // 2)
        source = across(offset)
        target = across(4 - way + offset) if arriving else source
        return remote(
            buffer.at[source, rows], buffer.at[target, rows], sems.at[0, i], sems.at[1, i], tag=tag, sec=across(way)
        )

    def gather_sec(buffer, sems, tag, weights, total):
        def came(i):
            ring_copy(buffer, sems, tag, i, True).wait_recv()

        total[...] = mm(weights[sec], buffer[sec])
        came(0)
        ring_copy(buffer, sems, tag, 4).start()
        came(2)
        ring_copy(buffer, sems, tag, 5).start()
        came(1)
        total[...] += mm(weights[across(3)], buffer[across(3)])
        came(3)
        total[...] += mm(weights[across(1)], buffer[across(1)])
        came(4)
        came(5)
        total[...] += mm(weights[across(2)], buffer[across(2)])

    def left(buffer, sems, tag):
        for i in range(6):
            ring_copy(buffer, sems, tag, i).wait_send()

    @pl.loop(0, EMB // 2)
    def _(t):
        base = chip(t, 1)

        @pl.when(t > 0)
        def _():
            id_copy(base + core, me).start()

        id_copy(base + 1 - core, me).start()

    ib[me] = ob[me]
    tb[...] = table_ref[...].astype(bf16)
    expert_load.wait()
    tower_load.wait()

    if "transpose" not in SKIP:

        @pl.loop(0, SEC)
        def _(r):
            expert_t[r] = expert_ref[rows_of(r), :].T
            tower_t[r] = tower_ref[rows_of(r), :].T

    @pl.loop(0, EMB // 2)
    def _(t):
        a = chip(t, -1) + core
        b = chip(t, -1) + 1 - core

        @pl.when(t > 0)
        def _():
            id_copy(a, a).wait_recv()

        id_copy(b, b).wait_recv()
        if "gather" not in SKIP:
            keys = jnp.concatenate([ib[a], ib[b]], axis=1)
            slot = keys >> 9
            picked = mm(tb[...], hot(ROWS, keys & (ROWS - 1)))
            rows = jnp.zeros((DIM, 2 * CAP), f32)
            for s in range(SLOTS):
                rows = rows + jnp.where(slot == s, picked[s * DIM : (s + 1) * DIM], 0.0)
            rows = rows.astype(bf16)
            out_rows[a] = rows[:, :CAP]
            out_rows[b] = rows[:, CAP:]

            @pl.when(t == 0)
            def _():
                in_rows[me] = rows[:, :CAP]

        @pl.when(t > 0)
        def _():
            row_copy(a, me).start()

        row_copy(b, me).start()

    def widen(part):
        for h in range(4):
            wide_rows[:, h * CAP : (h + 1) * CAP] = in_rows[pl.ds((part * 4 + h) * 8, 8)].reshape(8 * DIM, CAP)

    def pool(part, first, begin, end):
        @pl.loop(begin, end)
        def _(s):
            rows = pl.ds(pl.multiple_of(s * DIM, DIM), DIM)
            pooled = jnp.zeros((DIM, BATCH), f32) if first else pooled_ref[rows, :]
            for k in range(2):
                place = pos[2 * s + k]
                shard = place >> 7
                low = jnp.where(bag_ref[pl.ds(s, 1), :] > k, shard & 7, -1)
                key = ((shard >> 3) - part * 4) * CAP + (place & (CAP - 1))
                picked = mm(wide_rows[...], hot(4 * CAP, key))
                for g in range(8):
                    pooled = pooled + jnp.where(low == g, picked[g * DIM : (g + 1) * DIM], 0.0)
            if first:
                pooled_ref[rows, :] = pooled
            else:
                feats[sec, rows, :] = pooled.astype(bf16)

    @pl.loop(1, 32)
    def _(d):
        peer = ahead(d)
        row_copy(peer, peer).wait_recv()

    widen(half)
    pool(half, True, 0, SLOTS)

    @pl.loop(32, EMB)
    def _(d):
        peer = ahead(d)
        row_copy(peer, peer).wait_recv()

    widen(1 - half)
    pool(1 - half, False, 0, SLOTS // 2)
    ring_copy(feats, feat_sem, "feats", 0).start()
    ring_copy(feats, feat_sem, "feats", 3).start()
    pool(1 - half, False, SLOTS // 2, SLOTS)
    ring_copy(feats, feat_sem, "feats", 2).start()
    ring_copy(feats, feat_sem, "feats", 1).start()
    gather_sec(feats, feat_sem, "feats", expert_t, pre_e)
    hiddens[sec] = jax.nn.silu(pre_e[...]).astype(bf16)
    for i in (0, 2, 1, 3):
        ring_copy(hiddens, hidden_sem, "hiddens", i).start()
    gather_sec(hiddens, hidden_sem, "hiddens", tower_t, pre_t)
    out_col = jnp.broadcast_to(out_row_ref[...], (8, WIDE)).T[:, 0:1]
    active = jax.nn.silu(pre_t[...])
    share = jnp.sum(active * out_col, axis=0, keepdims=True)
    chosen = jnp.where(lax.broadcasted_iota(i32, (8, BATCH), 0) == task_ref[0], 1.0, 0.0)
    shares[sec] = share * chosen
    for d in (2, 1, 3):
        sec_copy(shares, share_sem, "shares", d, sec).start()
    slope = out_col * silu_slope(pre_t[...])
    for d in (1, 3, 2):
        sec_copy(shares, share_sem, "shares", d, across(d)).wait_recv()
    logits = (shares[0] + shares[1]) + (shares[2] + shares[3])
    err = logits[0:1] + logits[1:2] + logits[2:3] - watch_ref[...]
    chance = jax.nn.sigmoid(logits[0:2]) - click_ref[...] + err
    back = chance[0:1] * chosen[0:1] + chance[1:2] * chosen[1:2] + err * chosen[2:3]
    tower_delta = (back * slope).astype(bf16)

    low_half = slice(0, WIDE // 2)
    high_half = slice(WIDE // 2, WIDE)

    def part_copy(n, i):
        return remote(
            part_out.at[n, i], part_in.at[n, i], part_sem.at[n, 0, i], part_sem.at[n, 1, i],
            tag="part", sec=across((1, 3, 1, 3, 1, 3)[i]),
        )

    def part(n, weights_ref, delta):
        def send(i, value):
            part_out[n, i] = value.astype(bf16)
            part_copy(n, i).start()

        value = mm(weights_ref[rows_of(across(2)), :], delta)
        send(0, value[low_half])
        send(1, value[high_half])
        value = mm(weights_ref[rows_of(across(1)), :], delta)
        send(2, value[high_half])
        relay[0] = value[low_half]
        value = mm(weights_ref[rows_of(across(3)), :], delta)
        send(3, value[low_half])
        relay[1] = value[high_half]
        own_part[...] = mm(weights_ref[rows_of(sec), :], delta)
        for i in range(2):
            part_copy(n, i).wait_recv()
            send(4 + i, relay[i] + part_in[n, i].astype(f32))

    def part_sum(n):
        for i in range(2, 6):
            part_copy(n, i).wait_recv()
        own_part[low_half, :] += part_in[n, 3].astype(f32) + part_in[n, 4].astype(f32)
        own_part[high_half, :] += part_in[n, 2].astype(f32) + part_in[n, 5].astype(f32)
        for i in range(6):
            part_copy(n, i).wait_send()

    def core_copy(n):
        return remote(core_out.at[n], core_in.at[n], core_sem.at[0, n], core_sem.at[1, n], tag="core", emb=partner)

    def weight_grad(n, source, delta):
        @pl.loop(0, SEC)
        def _(r):
            whole[n, pl.ds(r * 16, 16)] = mm_nt(source[r], delta).reshape(16, 32, WIDE)

        @pl.loop(0, 32)
        def _(j):
            core_out[n, j] = whole[n, 2 * j + 1 - core].astype(bf16)

        core_copy(n).start()

    def x_copy(n, i):
        to = lax.rem(x + (1, 3, 1, 3, 1, 3)[i], XS)
        return remote(
            x_out.at[n, i], x_in.at[n, i], x_sem.at[n, 0, i], x_sem.at[n, 1, i], tag="x", emb=(to * ZS + z) * 2 + core
        )

    def z_copy(n, d):
        to = lax.rem(z + d, ZS)
        return remote(
            z_out.at[n, to], z_in.at[n, z], z_sem.at[n, 0, d], z_sem.at[n, 1, z], tag="z", emb=(x * ZS + to) * 2 + core
        )

    def z_arrive(n, d):
        to = lax.rem(z + d, ZS)
        return remote(
            z_out.at[n, to], z_in.at[n, to], z_sem.at[n, 0, d], z_sem.at[n, 1, to], tag="z", emb=(x * ZS + to) * 2 + core
        )

    def core_sum(n):
        core_copy(n).wait()

        @pl.loop(0, 32)
        def _(j):
            value = whole[n, 2 * j + core] + core_in[n, j].astype(f32)
            whole[n, 2 * j + core] = value

        for i, (d, part) in enumerate(((2, 0), (2, 1), (1, 1), (3, 0))):

            @pl.loop(0, ZS // 2)
            def _(j):
                x_out[n, i, j] = whole[n, place_of(d, part * (ZS // 2) + j)].astype(bf16)

            x_copy(n, i).start()

    def place_of(d, j):
        return 2 * (lax.rem(x + d, XS) * ZS + j) + core

    def x_relay(n):
        for i, d in ((0, 1), (1, 3)):
            x_copy(n, i).wait_recv()

            @pl.loop(0, ZS // 2)
            def _(j):
                value = whole[n, place_of(d, i * (ZS // 2) + j)] + x_in[n, i, j].astype(f32)
                x_out[n, 4 + i, j] = value.astype(bf16)

            x_copy(n, 4 + i).start()

    def x_sum(n):
        for part, (one, two) in enumerate(((3, 4), (2, 5))):
            x_copy(n, one).wait_recv()
            x_copy(n, two).wait_recv()

            @pl.loop(0, ZS // 2)
            def _(j):
                at = part * (ZS // 2) + j
                value = whole[n, place_of(0, at)] + x_in[n, one, j].astype(f32) + x_in[n, two, j].astype(f32)
                whole[n, place_of(0, at)] = value
                z_out[n, at] = value.astype(bf16)

        for d in range(1, ZS):
            z_copy(n, d).start()

    def z_sum(n):
        for d in range(1, ZS):
            z_arrive(n, d).wait_recv()
        value = whole[n, me]
        for d in range(1, ZS):
            value = value + z_in[n, lax.rem(z + d, ZS)].astype(f32)
        packed_ref[pl.ds(32 * n, 32), :] = value
        for i in range(6):
            x_copy(n, i).wait_send()
        for d in range(1, ZS):
            z_copy(n, d).wait_send()

    def hc_copy():
        return remote(head_core.at[0], head_core.at[1], hcore_sem.at[0], hcore_sem.at[1], tag="head", emb=partner)

    def hx_copy(d, at):
        to = lax.rem(x + d, XS)
        return remote(head_x.at[x], head_x.at[at], hx_sem.at[0, d], hx_sem.at[1, at], tag="head", emb=(to * ZS + z) * 2 + core)

    def hz_copy(d, at):
        to = lax.rem(z + d, ZS)
        return remote(head_z.at[z], head_z.at[at], hz_sem.at[0, d], hz_sem.at[1, at], tag="head", emb=(x * ZS + to) * 2 + core)

    part(0, tower_ref, tower_delta)
    head_core[0] = lax.dot_general(
        back, active, (((1,), (1,)), ((), ())), preferred_element_type=f32, precision=lax.Precision.HIGHEST
    )
    hc_copy().start()
    weight_grad(0, hiddens, tower_delta)
    part_sum(0)
    expert_delta = (own_part[...] * silu_slope(pre_e[...])).astype(bf16)
    part(1, expert_ref, expert_delta)
    core_sum(0)
    hc_copy().wait()
    head_x[x] = head_core[0] + head_core[1]
    for d in range(1, XS):
        hx_copy(d, x).start()
    weight_grad(1, feats, expert_delta)
    left(feats, feat_sem, "feats")
    left(hiddens, hidden_sem, "hiddens")
    for d in (2, 1, 3):
        sec_copy(shares, share_sem, "shares", d, sec).wait_send()
    for d in range(1, XS):
        hx_copy(d, lax.rem(x + d, XS)).wait_recv()
    head_z[z] = (head_x[0] + head_x[1]) + (head_x[2] + head_x[3])
    for d in range(1, ZS):
        hz_copy(d, z).start()
    part_sum(1)

    @pl.loop(0, SLOTS)
    def _(s):
        grad = own_part[pl.ds(pl.multiple_of(s * DIM, DIM), DIM), :]
        for k in range(2):
            low = jnp.where(bag_ref[pl.ds(s, 1), :] > k, (pos[2 * s + k] >> 7) & 7, -1)
            columns = pl.ds(pl.multiple_of((2 * s + k) * BATCH, BATCH), BATCH)
            for g in range(8):
                spread[g * DIM : (g + 1) * DIM, columns] = jnp.where(low == g, grad, 0.0).astype(bf16)

    @pl.loop(0, 4)
    def _(t):
        pair = lax.rem(x + t, 4)

        for q in range(2 * SLOTS):
            place = pos[q]
            key = ((place >> 10) - 2 * pair) * CAP + (place & (CAP - 1))
            hots[:, q * BATCH : (q + 1) * BATCH] = hot(2 * CAP, key)
        total = mm_nt(spread[...], hots[...]).astype(bf16)
        for h in range(2):
            for g in range(8):
                peer = (2 * pair + h) * 8 + g
                out_grads[peer] = total[g * DIM : (g + 1) * DIM, h * CAP : (h + 1) * CAP]

        @pl.when(t == 0)
        def _():
            in_grads[me] = out_grads[me]

        @pl.loop(0, ZS)
        def _(j):
            base = (pair * ZS + lax.rem(z + z_shift(j), ZS)) * 2
            for c in range(2):
                peer = base + c

                @pl.when(peer != me)
                def _():
                    grad_copy(peer, me).start()

        @pl.when(t == 0)
        def _():
            core_sum(1)
            x_relay(0)

        @pl.when(t == 1)
        def _():
            x_sum(0)
            x_relay(1)

    x_sum(1)
    z_sum(0)
    for d in range(1, ZS):
        hz_copy(d, lax.rem(z + d, ZS)).wait_recv()
    head = head_z[0]
    for j in range(1, ZS):
        head = head + head_z[j]
    packed_ref[64:72, :] = jnp.broadcast_to(head, (8, WIDE))

    grad_ref[...] = jnp.zeros((WIDE, ROWS), f32)

    @pl.loop(1, EMB)
    def _(d):
        peer = lax.rem(me + d, EMB)
        id_copy(peer, me).wait_send()
        row_copy(peer, me).wait_send()


    @pl.loop(0, XS)
    def _(t):
        first = lax.rem(x + XS - t, XS) * 16

        @pl.loop(0, 16)
        def _(j):
            peer = first + j

            @pl.when(peer != me)
            def _():
                grad_copy(peer, peer).wait_recv()

        if "scatter" not in SKIP:

            @pl.loop(0, 8)
            def _(j):
                a = first + 2 * j
                keys = jnp.concatenate([ib[a], ib[a + 1]], axis=1)
                slot = keys >> 9
                grads = jnp.concatenate([in_grads[a], in_grads[a + 1]], axis=1).astype(f32)
                wide = jnp.concatenate([jnp.where(slot == s, grads, 0.0) for s in range(SLOTS)], axis=0).astype(bf16)
                columns = pl.ds(pl.multiple_of(j * 2 * CAP, 2 * CAP), 2 * CAP)
                spread[:, columns] = wide
                row_hots[:, columns] = hot(ROWS, keys & (ROWS - 1))

            grad_ref[...] += mm_nt(spread[:, : 16 * CAP], row_hots[...])

    z_sum(1)
    for d in range(1, XS):
        hx_copy(d, x).wait_send()
    for d in range(1, ZS):
        hz_copy(d, z).wait_send()

    @pl.loop(1, EMB)
    def _(d):
        peer = lax.rem(me + d, EMB)
        grad_copy(peer, me).wait_send()


def update_kernel(table_ref, accum_ref, grad_ref, packed_ref, new_table, new_accum, tower_grad, expert_grad, head_grad):
    grad = grad_ref[...]
    accum = accum_ref[...] + grad * grad
    new_accum[...] = accum
    new_table[...] = table_ref[...] - learn_rate * grad / jnp.sqrt(accum)

    @pl.when(pl.program_id(0) == 0)
    def _():
        tower_grad[...] = packed_ref[:32, :]
        expert_grad[...] = packed_ref[32:64, :]
        head_grad[...] = packed_ref[64:65, :]


def body(
    emb_table,
    emb_accum,
    slot_ids,
    bag_len,
    expert_w,
    tower_w,
    tower_out,
    section_task,
    click_like,
    watch,
):
    vmem = pl.BlockSpec(memory_space=pltpu.VMEM)
    dma = pltpu.SemaphoreType.DMA
    table = emb_table.transpose(0, 2, 1).reshape(SLOTS * DIM, ROWS)
    accum = emb_accum.transpose(0, 2, 1).reshape(SLOTS * DIM, ROWS)
    anywhere = pl.BlockSpec(memory_space=pl.ANY)
    row_grad, packed = pl.pallas_call(
        step_kernel,
        out_shape=(
            jax.ShapeDtypeStruct((SLOTS * DIM, ROWS), f32),
            jax.ShapeDtypeStruct((72, WIDE), f32),
        ),
        in_specs=[pl.BlockSpec(memory_space=pltpu.SMEM), vmem, vmem, vmem, anywhere, anywhere, vmem, vmem, vmem],
        out_specs=(vmem,) * 2,
        scratch_shapes=[
            pltpu.VMEM((2 * SLOTS, 1, BATCH), i32),
            pltpu.VMEM((EMB, 1, CAP), i32),
            pltpu.VMEM((EMB, 1, CAP), i32),
            pltpu.VMEM((EMB, DIM, CAP), bf16),
            pltpu.VMEM((EMB, DIM, CAP), bf16),
            pltpu.VMEM((8 * DIM, 4 * CAP), bf16),
            pltpu.VMEM((8 * DIM, BATCH), f32),
            pltpu.VMEM((SLOTS * DIM, ROWS), bf16),
            pltpu.VMEM((SEC * WIDE, WIDE), bf16),
            pltpu.VMEM((SEC * WIDE, WIDE), bf16),
            pltpu.VMEM((SEC, WIDE, BATCH), bf16),
            pltpu.VMEM((SEC, WIDE, BATCH), bf16),
            pltpu.VMEM((SEC, WIDE, WIDE), bf16),
            pltpu.VMEM((SEC, WIDE, WIDE), bf16),
            pltpu.VMEM((WIDE, BATCH), f32),
            pltpu.VMEM((WIDE, BATCH), f32),
            pltpu.VMEM((SEC, 8, BATCH), f32),
            pltpu.VMEM((2, 6, WIDE // 2, BATCH), bf16),
            pltpu.VMEM((2, 6, WIDE // 2, BATCH), bf16),
            pltpu.VMEM((2, WIDE // 2, BATCH), f32),
            pltpu.VMEM((2, EMB, 32, WIDE), f32),
            pltpu.VMEM((WIDE, BATCH), f32),
            pltpu.VMEM((2, 32, 32, WIDE), bf16),
            pltpu.VMEM((2, 32, 32, WIDE), bf16),
            pltpu.VMEM((2, 6, ZS // 2, 32, WIDE), bf16),
            pltpu.VMEM((2, 6, ZS // 2, 32, WIDE), bf16),
            pltpu.VMEM((2, ZS, 32, WIDE), bf16),
            pltpu.VMEM((2, ZS, 32, WIDE), bf16),
            pltpu.VMEM((2, 1, WIDE), f32),
            pltpu.VMEM((XS, 1, WIDE), f32),
            pltpu.VMEM((ZS, 1, WIDE), f32),
            pltpu.VMEM((8 * DIM, 2 * SLOTS * BATCH), bf16),
            pltpu.VMEM((2 * CAP, 2 * SLOTS * BATCH), bf16),
            pltpu.VMEM((ROWS, 16 * CAP), bf16),
            pltpu.VMEM((EMB, DIM, CAP), bf16),
            pltpu.VMEM((EMB, DIM, CAP), bf16),
            dma((2,)),
            dma((EMB,)),
            dma((EMB,)),
            dma((EMB,)),
            dma((EMB,)),
            dma((2, 6)),
            dma((2, 6)),
            dma((2, SEC)),
            dma((2, 2, 6)),
            dma((2, 2)),
            dma((2, 2, 6)),
            dma((2, 2, ZS)),
            dma((2,)),
            dma((2, XS)),
            dma((2, ZS)),
            dma((EMB,)),
            dma((EMB,)),
        ],
        compiler_params=pltpu.CompilerParams(collective_id=0, has_side_effects=True, vmem_limit_bytes=60 << 20),
    )(
        section_task,
        slot_ids.transpose(1, 2, 0),
        bag_len.T,
        table,
        expert_w,
        tower_w,
        tower_out,
        click_like.T,
        watch.reshape(1, BATCH),
    )
    tile = pl.BlockSpec((128, ROWS), lambda i: (i, 0))
    piece = pl.BlockSpec((32, WIDE), lambda i: (0, 0))
    line = pl.BlockSpec((1, WIDE), lambda i: (0, 0))
    whole_table = jax.ShapeDtypeStruct((SLOTS * DIM, ROWS), f32)
    new_table, new_accum, tower_grad, expert_grad, head_grad = pl.pallas_call(
        update_kernel,
        grid=(SLOTS * DIM // 128,),
        out_shape=(
            whole_table,
            whole_table,
            jax.ShapeDtypeStruct((32, WIDE), f32),
            jax.ShapeDtypeStruct((32, WIDE), f32),
            jax.ShapeDtypeStruct((1, WIDE), f32),
        ),
        in_specs=[tile, tile, tile, pl.BlockSpec((72, WIDE), lambda i: (0, 0))],
        out_specs=(tile, tile, piece, piece, line),
    )(table, accum, row_grad, packed)

    def back(value):
        return value.reshape(SLOTS, DIM, ROWS).transpose(0, 2, 1)

    return (back(new_table), back(new_accum), expert_grad, tower_grad, head_grad)


def solution(mesh):
    placed = (
        P("sec", "emb", None),
        P("sec", "emb", None),
        P("emb", "sec", None),
        P("emb", "sec"),
        P(None, "sec"),
        P(None, "sec"),
        P("sec", None),
        P("sec"),
        P("emb", None),
        P("emb"),
    )
    return jax.shard_map(
        body,
        mesh=mesh,
        in_specs=placed,
        out_specs=(
            P("sec", "emb", None),
            P("sec", "emb", None),
            P("emb", "sec"),
            P("emb", "sec"),
            P("sec", None),
        ),
        check_vma=False,
    )
```

```python
import jax
import jax.numpy as jnp
from jax import lax
from jax.experimental import pallas as pl
from jax.experimental.pallas import tpu as pltpu
from jax.sharding import PartitionSpec as P

MESH = pl.DeviceIdType.MESH
learn_rate = 0.2
f32 = jnp.float32
bf16 = jnp.bfloat16
i32 = jnp.int32

EMB = 64
SEC = 4
XS = 4
ZS = 8
CAP = 128
DIM = 64
SLOTS = 8
BATCH = 256
ROWS = 512
WIDE = 512


def mm(a, b):
    return lax.dot_general(a, b, (((1,), (0,)), ((), ())), preferred_element_type=f32)


def mm_nt(a, b):
    return lax.dot_general(a, b, (((1,), (1,)), ((), ())), preferred_element_type=f32)


def silu_slope(value):
    logistic = jax.nn.sigmoid(value)
    return logistic * (1.0 + value * (1.0 - logistic))


def hot(size, keys):
    rows = lax.broadcasted_iota(i32, (size, keys.shape[1]), 0)
    return jnp.where(rows == keys, 1.0, 0.0).astype(bf16)


SKIP = ()


class Nothing:
    def start(self):
        pass

    wait = wait_send = wait_recv = start


def remote(src, dst, send, recv, tag, **where):
    if tag in SKIP:
        return Nothing()
    return pltpu.make_async_remote_copy(
        src_ref=src, dst_ref=dst, send_sem=send, recv_sem=recv, device_id=where, device_id_type=MESH
    )


def greet(emb, sec):
    barrier = pltpu.get_barrier_semaphore()

    @pl.loop(1, EMB)
    def _(d):
        pl.semaphore_signal(barrier, inc=1, device_id={"emb": lax.rem(emb + d, EMB)}, device_id_type=MESH)

    for d in range(1, SEC):
        pl.semaphore_signal(barrier, inc=1, device_id={"sec": lax.rem(sec + d, SEC)}, device_id_type=MESH)


def meet():
    pl.semaphore_wait(pltpu.get_barrier_semaphore(), EMB - 1 + SEC - 1)


def route(ids_ref, ob, pos):
    before = lax.broadcasted_iota(i32, (BATCH, BATCH), 0)
    after = lax.broadcasted_iota(i32, (BATCH, BATCH), 1)
    upper = jnp.where(before < after, 1.0, 0.0).astype(bf16)
    shard_row = lax.broadcasted_iota(i32, (EMB, BATCH), 0)
    rank_row = lax.broadcasted_iota(i32, (CAP, BATCH), 0)
    carry = jnp.zeros((EMB, 1), f32)
    total = jnp.zeros((EMB, 2 * CAP), f32)
    for q in range(2 * SLOTS):
        ids = ids_ref[q // 2, q % 2 : q % 2 + 1, :]
        owner = ids >> 9
        key = (ids & (ROWS - 1)) + ((q // 2) * ROWS + 1)
        owned = jnp.where(shard_row == owner, 1.0, 0.0)
        owned_b = owned.astype(bf16)
        prefix = mm(owned_b, upper) + carry
        rank = jnp.sum(owned * prefix, axis=0, keepdims=True).astype(i32)
        carry = carry + jnp.sum(owned, axis=1, keepdims=True)
        pos[q] = owner * CAP + rank
        ranked = rank_row == rank
        high = jnp.where(ranked, (key >> 6).astype(f32), 0.0).astype(bf16)
        low = jnp.where(ranked, (key & 63).astype(f32), 0.0).astype(bf16)
        total = total + mm_nt(owned_b, jnp.concatenate([high, low], axis=0))
    keys = (total[:, :CAP] * 64.0 + total[:, CAP:]).astype(i32) - 1
    for s in range(EMB):
        ob[s] = keys[s : s + 1, :]


def step_kernel(
    task_ref, ids_ref, bag_ref, table_ref, expert_hbm, tower_hbm, out_row_ref, click_ref, watch_ref,
    grad_ref, packed_ref,
    pos, ob, ib, out_rows, in_rows, wide_rows, pooled_ref, tb, expert_ref, tower_ref,
    feats, hiddens, expert_t, tower_t, pre_e, pre_t, shares, part_out, part_in, relay, whole, own_part,
    core_out, core_in, x_out, x_in, z_out, z_in, head_core, head_x, head_z,
    spread, hots, row_hots, out_grads, in_grads,
    load_sem, id_send, id_recv, row_send, row_recv,
    feat_sem, hidden_sem, share_sem, part_sem, core_sem, x_sem, z_sem, hcore_sem, hx_sem, hz_sem, grad_send, grad_recv,
):
    me = lax.axis_index("emb")
    sec = lax.axis_index("sec")
    core = lax.rem(me, 2)
    z = lax.rem(lax.div(me, 2), ZS)
    x = lax.div(me, 2 * ZS)
    half = lax.div(me, 32)
    inner = lax.rem(me, 32)
    partner = me + 1 - 2 * core
    expert_load = pltpu.make_async_copy(expert_hbm, expert_ref, load_sem.at[0])
    tower_load = pltpu.make_async_copy(tower_hbm, tower_ref, load_sem.at[1])
    expert_load.start()
    tower_load.start()
    greet(me, sec)
    route(ids_ref, ob, pos)
    meet()

    def rows_of(r):
        return pl.ds(pl.multiple_of(r * WIDE, WIDE), WIDE)

    def ahead(d):
        group = lax.rem(half + lax.div(d, 32), 2)
        return group * 32 + lax.rem(inner + d, 32)

    def z_shift(i):
        step, odd = lax.div(i + 1, 2), lax.rem(i, 2)
        return lax.rem(step * odd + (ZS - step) * (1 - odd), ZS)

    def chip(t, way):
        group = lax.rem(half + lax.div(t, 16), 2)
        column = 2 * group + lax.rem(x + lax.div(t, ZS), 2)
        return (column * ZS + lax.rem(z + ZS + way * z_shift(lax.rem(t, ZS)), ZS)) * 2

    def id_copy(peer, at):
        return remote(ob.at[peer], ib.at[at], id_send.at[peer], id_recv.at[at], tag="ids", emb=peer)

    def row_copy(peer, at):
        return remote(out_rows.at[peer], in_rows.at[at], row_send.at[peer], row_recv.at[at], tag="rows", emb=peer)

    def grad_copy(peer, at):
        return remote(out_grads.at[peer], in_grads.at[at], grad_send.at[peer], grad_recv.at[at], tag="grads", emb=peer)

    def across(d):
        return lax.rem(sec + d, SEC)

    def sec_copy(buffer, sems, tag, d, at):
        return remote(buffer.at[sec], buffer.at[at], sems.at[0, d], sems.at[1, at], tag=tag, sec=across(d))

    def ring_copy(buffer, sems, tag, i, arriving=False):
        offset, part, way = ((0, 0, 1), (0, 1, 1), (0, 1, 3), (0, 0, 3), (3, 0, 1), (1, 1, 3))[i]
        rows = pl.ds(part * (WIDE // 2), WIDE // 2)
        source = across(offset)
        target = across(4 - way + offset) if arriving else source
        return remote(
            buffer.at[source, rows], buffer.at[target, rows], sems.at[0, i], sems.at[1, i], tag=tag, sec=across(way)
        )

    def gather_sec(buffer, sems, tag, weights, total):
        def came(i):
            ring_copy(buffer, sems, tag, i, True).wait_recv()

        total[...] = mm(weights[sec], buffer[sec])
        came(0)
        ring_copy(buffer, sems, tag, 4).start()
        came(2)
        ring_copy(buffer, sems, tag, 5).start()
        came(1)
        total[...] += mm(weights[across(3)], buffer[across(3)])
        came(3)
        total[...] += mm(weights[across(1)], buffer[across(1)])
        came(4)
        came(5)
        total[...] += mm(weights[across(2)], buffer[across(2)])

    def left(buffer, sems, tag):
        for i in range(6):
            ring_copy(buffer, sems, tag, i).wait_send()

    @pl.loop(0, EMB // 2)
    def _(t):
        base = chip(t, 1)

        @pl.when(t > 0)
        def _():
            id_copy(base + core, me).start()

        id_copy(base + 1 - core, me).start()

    ib[me] = ob[me]
    tb[...] = table_ref[...].astype(bf16)
    expert_load.wait()
    tower_load.wait()

    if "transpose" not in SKIP:

        @pl.loop(0, SEC)
        def _(r):
            expert_t[r] = expert_ref[rows_of(r), :].T
            tower_t[r] = tower_ref[rows_of(r), :].T

    @pl.loop(0, EMB // 2)
    def _(t):
        a = chip(t, -1) + core
        b = chip(t, -1) + 1 - core

        @pl.when(t > 0)
        def _():
            id_copy(a, a).wait_recv()

        id_copy(b, b).wait_recv()
        if "gather" not in SKIP:
            keys = jnp.concatenate([ib[a], ib[b]], axis=1)
            slot = keys >> 9
            picked = mm(tb[...], hot(ROWS, keys & (ROWS - 1)))
            rows = jnp.zeros((DIM, 2 * CAP), f32)
            for s in range(SLOTS):
                rows = rows + jnp.where(slot == s, picked[s * DIM : (s + 1) * DIM], 0.0)
            rows = rows.astype(bf16)
            out_rows[a] = rows[:, :CAP]
            out_rows[b] = rows[:, CAP:]

            @pl.when(t == 0)
            def _():
                in_rows[me] = rows[:, :CAP]

        @pl.when(t > 0)
        def _():
            row_copy(a, me).start()

        row_copy(b, me).start()

    def widen(part):
        for h in range(4):
            wide_rows[:, h * CAP : (h + 1) * CAP] = in_rows[pl.ds((part * 4 + h) * 8, 8)].reshape(8 * DIM, CAP)

    def pool(part, first, begin, end):
        @pl.loop(begin, end)
        def _(s):
            rows = pl.ds(pl.multiple_of(s * DIM, DIM), DIM)
            pooled = jnp.zeros((DIM, BATCH), f32) if first else pooled_ref[rows, :]
            for k in range(2):
                place = pos[2 * s + k]
                shard = place >> 7
                low = jnp.where(bag_ref[pl.ds(s, 1), :] > k, shard & 7, -1)
                key = ((shard >> 3) - part * 4) * CAP + (place & (CAP - 1))
                picked = mm(wide_rows[...], hot(4 * CAP, key))
                for g in range(8):
                    pooled = pooled + jnp.where(low == g, picked[g * DIM : (g + 1) * DIM], 0.0)
            if first:
                pooled_ref[rows, :] = pooled
            else:
                feats[sec, rows, :] = pooled.astype(bf16)

    @pl.loop(1, 32)
    def _(d):
        peer = ahead(d)
        row_copy(peer, peer).wait_recv()

    widen(half)
    pool(half, True, 0, SLOTS)

    @pl.loop(32, EMB)
    def _(d):
        peer = ahead(d)
        row_copy(peer, peer).wait_recv()

    widen(1 - half)
    pool(1 - half, False, 0, SLOTS // 2)
    ring_copy(feats, feat_sem, "feats", 0).start()
    ring_copy(feats, feat_sem, "feats", 3).start()
    pool(1 - half, False, SLOTS // 2, SLOTS)
    ring_copy(feats, feat_sem, "feats", 2).start()
    ring_copy(feats, feat_sem, "feats", 1).start()
    gather_sec(feats, feat_sem, "feats", expert_t, pre_e)
    hiddens[sec] = jax.nn.silu(pre_e[...]).astype(bf16)
    for i in (0, 2, 1, 3):
        ring_copy(hiddens, hidden_sem, "hiddens", i).start()
    gather_sec(hiddens, hidden_sem, "hiddens", tower_t, pre_t)
    out_col = jnp.broadcast_to(out_row_ref[...], (8, WIDE)).T[:, 0:1]
    active = jax.nn.silu(pre_t[...])
    share = jnp.sum(active * out_col, axis=0, keepdims=True)
    chosen = jnp.where(lax.broadcasted_iota(i32, (8, BATCH), 0) == task_ref[0], 1.0, 0.0)
    shares[sec] = share * chosen
    for d in (2, 1, 3):
        sec_copy(shares, share_sem, "shares", d, sec).start()
    slope = out_col * silu_slope(pre_t[...])
    for d in (1, 3, 2):
        sec_copy(shares, share_sem, "shares", d, across(d)).wait_recv()
    logits = (shares[0] + shares[1]) + (shares[2] + shares[3])
    err = logits[0:1] + logits[1:2] + logits[2:3] - watch_ref[...]
    chance = jax.nn.sigmoid(logits[0:2]) - click_ref[...] + err
    back = chance[0:1] * chosen[0:1] + chance[1:2] * chosen[1:2] + err * chosen[2:3]
    tower_delta = (back * slope).astype(bf16)

    low_half = slice(0, WIDE // 2)
    high_half = slice(WIDE // 2, WIDE)

    def part_copy(n, i):
        return remote(
            part_out.at[n, i], part_in.at[n, i], part_sem.at[n, 0, i], part_sem.at[n, 1, i],
            tag="part", sec=across((1, 3, 1, 3, 1, 3)[i]),
        )

    def part(n, weights_ref, delta):
        def send(i, value):
            part_out[n, i] = value.astype(bf16)
            part_copy(n, i).start()

        value = mm(weights_ref[rows_of(across(2)), :], delta)
        send(0, value[low_half])
        send(1, value[high_half])
        value = mm(weights_ref[rows_of(across(1)), :], delta)
        send(2, value[high_half])
        relay[0] = value[low_half]
        value = mm(weights_ref[rows_of(across(3)), :], delta)
        send(3, value[low_half])
        relay[1] = value[high_half]
        own_part[...] = mm(weights_ref[rows_of(sec), :], delta)
        for i in range(2):
            part_copy(n, i).wait_recv()
            send(4 + i, relay[i] + part_in[n, i].astype(f32))

    def part_sum(n):
        for i in range(2, 6):
            part_copy(n, i).wait_recv()
        own_part[low_half, :] += part_in[n, 3].astype(f32) + part_in[n, 4].astype(f32)
        own_part[high_half, :] += part_in[n, 2].astype(f32) + part_in[n, 5].astype(f32)
        for i in range(6):
            part_copy(n, i).wait_send()

    def core_copy(n):
        return remote(core_out.at[n], core_in.at[n], core_sem.at[0, n], core_sem.at[1, n], tag="core", emb=partner)

    def weight_grad(n, source, delta):
        @pl.loop(0, SEC)
        def _(r):
            whole[n, pl.ds(r * 16, 16)] = mm_nt(source[r], delta).reshape(16, 32, WIDE)

        @pl.loop(0, 32)
        def _(j):
            core_out[n, j] = whole[n, 2 * j + 1 - core].astype(bf16)

        core_copy(n).start()

    def x_copy(n, i):
        to = lax.rem(x + (1, 3, 1, 3, 1, 3)[i], XS)
        return remote(
            x_out.at[n, i], x_in.at[n, i], x_sem.at[n, 0, i], x_sem.at[n, 1, i], tag="x", emb=(to * ZS + z) * 2 + core
        )

    def z_copy(n, d):
        to = lax.rem(z + d, ZS)
        return remote(
            z_out.at[n, to], z_in.at[n, z], z_sem.at[n, 0, d], z_sem.at[n, 1, z], tag="z", emb=(x * ZS + to) * 2 + core
        )

    def z_arrive(n, d):
        to = lax.rem(z + d, ZS)
        return remote(
            z_out.at[n, to], z_in.at[n, to], z_sem.at[n, 0, d], z_sem.at[n, 1, to], tag="z", emb=(x * ZS + to) * 2 + core
        )

    def core_sum(n):
        core_copy(n).wait()

        @pl.loop(0, 32)
        def _(j):
            value = whole[n, 2 * j + core] + core_in[n, j].astype(f32)
            whole[n, 2 * j + core] = value

        for i, (d, part) in enumerate(((2, 0), (2, 1), (1, 1), (3, 0))):

            @pl.loop(0, ZS // 2)
            def _(j):
                x_out[n, i, j] = whole[n, place_of(d, part * (ZS // 2) + j)].astype(bf16)

            x_copy(n, i).start()

    def place_of(d, j):
        return 2 * (lax.rem(x + d, XS) * ZS + j) + core

    def x_relay(n):
        for i, d in ((0, 1), (1, 3)):
            x_copy(n, i).wait_recv()

            @pl.loop(0, ZS // 2)
            def _(j):
                value = whole[n, place_of(d, i * (ZS // 2) + j)] + x_in[n, i, j].astype(f32)
                x_out[n, 4 + i, j] = value.astype(bf16)

            x_copy(n, 4 + i).start()

    def x_sum(n):
        for part, (one, two) in enumerate(((3, 4), (2, 5))):
            x_copy(n, one).wait_recv()
            x_copy(n, two).wait_recv()

            @pl.loop(0, ZS // 2)
            def _(j):
                at = part * (ZS // 2) + j
                value = whole[n, place_of(0, at)] + x_in[n, one, j].astype(f32) + x_in[n, two, j].astype(f32)
                whole[n, place_of(0, at)] = value
                z_out[n, at] = value.astype(bf16)

        for d in range(1, ZS):
            z_copy(n, d).start()

    def z_sum(n):
        for d in range(1, ZS):
            z_arrive(n, d).wait_recv()
        value = whole[n, me]
        for d in range(1, ZS):
            value = value + z_in[n, lax.rem(z + d, ZS)].astype(f32)
        packed_ref[pl.ds(32 * n, 32), :] = value
        for i in range(6):
            x_copy(n, i).wait_send()
        for d in range(1, ZS):
            z_copy(n, d).wait_send()

    def hc_copy():
        return remote(head_core.at[0], head_core.at[1], hcore_sem.at[0], hcore_sem.at[1], tag="head", emb=partner)

    def hx_copy(d, at):
        to = lax.rem(x + d, XS)
        return remote(head_x.at[x], head_x.at[at], hx_sem.at[0, d], hx_sem.at[1, at], tag="head", emb=(to * ZS + z) * 2 + core)

    def hz_copy(d, at):
        to = lax.rem(z + d, ZS)
        return remote(head_z.at[z], head_z.at[at], hz_sem.at[0, d], hz_sem.at[1, at], tag="head", emb=(x * ZS + to) * 2 + core)

    part(0, tower_ref, tower_delta)
    head_core[0] = lax.dot_general(
        back, active, (((1,), (1,)), ((), ())), preferred_element_type=f32, precision=lax.Precision.HIGHEST
    )
    hc_copy().start()
    weight_grad(0, hiddens, tower_delta)
    hc_copy().wait()
    head_x[x] = head_core[0] + head_core[1]
    for d in range(1, XS):
        hx_copy(d, x).start()
    part_sum(0)
    expert_delta = (own_part[...] * silu_slope(pre_e[...])).astype(bf16)
    part(1, expert_ref, expert_delta)
    for d in range(1, XS):
        hx_copy(d, lax.rem(x + d, XS)).wait_recv()
    head_z[z] = (head_x[0] + head_x[1]) + (head_x[2] + head_x[3])
    for d in range(1, ZS):
        hz_copy(d, z).start()
    core_sum(0)
    weight_grad(1, feats, expert_delta)
    x_relay(0)
    left(feats, feat_sem, "feats")
    left(hiddens, hidden_sem, "hiddens")
    for d in (2, 1, 3):
        sec_copy(shares, share_sem, "shares", d, sec).wait_send()
    part_sum(1)

    @pl.loop(0, SLOTS)
    def _(s):
        grad = own_part[pl.ds(pl.multiple_of(s * DIM, DIM), DIM), :]
        for k in range(2):
            low = jnp.where(bag_ref[pl.ds(s, 1), :] > k, (pos[2 * s + k] >> 7) & 7, -1)
            columns = pl.ds(pl.multiple_of((2 * s + k) * BATCH, BATCH), BATCH)
            for g in range(8):
                spread[g * DIM : (g + 1) * DIM, columns] = jnp.where(low == g, grad, 0.0).astype(bf16)

    @pl.loop(0, 4)
    def _(t):
        pair = lax.rem(x + t, 4)

        for q in range(2 * SLOTS):
            place = pos[q]
            key = ((place >> 10) - 2 * pair) * CAP + (place & (CAP - 1))
            hots[:, q * BATCH : (q + 1) * BATCH] = hot(2 * CAP, key)
        total = mm_nt(spread[...], hots[...]).astype(bf16)
        for h in range(2):
            for g in range(8):
                peer = (2 * pair + h) * 8 + g
                out_grads[peer] = total[g * DIM : (g + 1) * DIM, h * CAP : (h + 1) * CAP]

        @pl.when(t == 0)
        def _():
            in_grads[me] = out_grads[me]

        @pl.loop(0, ZS)
        def _(j):
            base = (pair * ZS + lax.rem(z + z_shift(j), ZS)) * 2
            for c in range(2):
                peer = base + c

                @pl.when(peer != me)
                def _():
                    grad_copy(peer, me).start()

        @pl.when(t == 0)
        def _():
            core_sum(1)
            x_sum(0)

        @pl.when(t == 1)
        def _():
            x_relay(1)

    x_sum(1)
    z_sum(0)
    for d in range(1, ZS):
        hz_copy(d, lax.rem(z + d, ZS)).wait_recv()
    head = head_z[0]
    for j in range(1, ZS):
        head = head + head_z[j]
    packed_ref[64:72, :] = jnp.broadcast_to(head, (8, WIDE))

    grad_ref[...] = jnp.zeros((WIDE, ROWS), f32)

    @pl.loop(1, EMB)
    def _(d):
        peer = lax.rem(me + d, EMB)
        id_copy(peer, me).wait_send()
        row_copy(peer, me).wait_send()


    @pl.loop(0, XS)
    def _(t):
        first = lax.rem(x + XS - t, XS) * 16

        @pl.loop(0, 16)
        def _(j):
            peer = first + j

            @pl.when(peer != me)
            def _():
                grad_copy(peer, peer).wait_recv()

        if "scatter" not in SKIP:

            @pl.loop(0, 8)
            def _(j):
                a = first + 2 * j
                keys = jnp.concatenate([ib[a], ib[a + 1]], axis=1)
                slot = keys >> 9
                grads = jnp.concatenate([in_grads[a], in_grads[a + 1]], axis=1).astype(f32)
                wide = jnp.concatenate([jnp.where(slot == s, grads, 0.0) for s in range(SLOTS)], axis=0).astype(bf16)
                columns = pl.ds(pl.multiple_of(j * 2 * CAP, 2 * CAP), 2 * CAP)
                spread[:, columns] = wide
                row_hots[:, columns] = hot(ROWS, keys & (ROWS - 1))

            grad_ref[...] += mm_nt(spread[:, : 16 * CAP], row_hots[...])

    z_sum(1)
    for d in range(1, XS):
        hx_copy(d, x).wait_send()
    for d in range(1, ZS):
        hz_copy(d, z).wait_send()

    @pl.loop(1, EMB)
    def _(d):
        peer = lax.rem(me + d, EMB)
        grad_copy(peer, me).wait_send()


def update_kernel(table_ref, accum_ref, grad_ref, packed_ref, new_table, new_accum, tower_grad, expert_grad, head_grad):
    @pl.loop(0, SLOTS)
    def _(s):
        rows = pl.ds(pl.multiple_of(s * DIM, DIM), DIM)
        grad = grad_ref[rows, :]
        accum = accum_ref[rows, :] + grad * grad
        new_accum[rows, :] = accum
        new_table[rows, :] = table_ref[rows, :] - learn_rate * grad / jnp.sqrt(accum)

    tower_grad[...] = packed_ref[:32, :]
    expert_grad[...] = packed_ref[32:64, :]
    head_grad[...] = packed_ref[64:65, :]


def body(
    emb_table,
    emb_accum,
    slot_ids,
    bag_len,
    expert_w,
    tower_w,
    tower_out,
    section_task,
    click_like,
    watch,
):
    vmem = pl.BlockSpec(memory_space=pltpu.VMEM)
    dma = pltpu.SemaphoreType.DMA
    table = emb_table.transpose(0, 2, 1).reshape(SLOTS * DIM, ROWS)
    accum = emb_accum.transpose(0, 2, 1).reshape(SLOTS * DIM, ROWS)
    anywhere = pl.BlockSpec(memory_space=pl.ANY)
    row_grad, packed = pl.pallas_call(
        step_kernel,
        out_shape=(
            jax.ShapeDtypeStruct((SLOTS * DIM, ROWS), f32),
            jax.ShapeDtypeStruct((72, WIDE), f32),
        ),
        in_specs=[pl.BlockSpec(memory_space=pltpu.SMEM), vmem, vmem, vmem, anywhere, anywhere, vmem, vmem, vmem],
        out_specs=(vmem,) * 2,
        scratch_shapes=[
            pltpu.VMEM((2 * SLOTS, 1, BATCH), i32),
            pltpu.VMEM((EMB, 1, CAP), i32),
            pltpu.VMEM((EMB, 1, CAP), i32),
            pltpu.VMEM((EMB, DIM, CAP), bf16),
            pltpu.VMEM((EMB, DIM, CAP), bf16),
            pltpu.VMEM((8 * DIM, 4 * CAP), bf16),
            pltpu.VMEM((8 * DIM, BATCH), f32),
            pltpu.VMEM((SLOTS * DIM, ROWS), bf16),
            pltpu.VMEM((SEC * WIDE, WIDE), bf16),
            pltpu.VMEM((SEC * WIDE, WIDE), bf16),
            pltpu.VMEM((SEC, WIDE, BATCH), bf16),
            pltpu.VMEM((SEC, WIDE, BATCH), bf16),
            pltpu.VMEM((SEC, WIDE, WIDE), bf16),
            pltpu.VMEM((SEC, WIDE, WIDE), bf16),
            pltpu.VMEM((WIDE, BATCH), f32),
            pltpu.VMEM((WIDE, BATCH), f32),
            pltpu.VMEM((SEC, 8, BATCH), f32),
            pltpu.VMEM((2, 6, WIDE // 2, BATCH), bf16),
            pltpu.VMEM((2, 6, WIDE // 2, BATCH), bf16),
            pltpu.VMEM((2, WIDE // 2, BATCH), f32),
            pltpu.VMEM((2, EMB, 32, WIDE), f32),
            pltpu.VMEM((WIDE, BATCH), f32),
            pltpu.VMEM((2, 32, 32, WIDE), bf16),
            pltpu.VMEM((2, 32, 32, WIDE), bf16),
            pltpu.VMEM((2, 6, ZS // 2, 32, WIDE), bf16),
            pltpu.VMEM((2, 6, ZS // 2, 32, WIDE), bf16),
            pltpu.VMEM((2, ZS, 32, WIDE), bf16),
            pltpu.VMEM((2, ZS, 32, WIDE), bf16),
            pltpu.VMEM((2, 1, WIDE), f32),
            pltpu.VMEM((XS, 1, WIDE), f32),
            pltpu.VMEM((ZS, 1, WIDE), f32),
            pltpu.VMEM((8 * DIM, 2 * SLOTS * BATCH), bf16),
            pltpu.VMEM((2 * CAP, 2 * SLOTS * BATCH), bf16),
            pltpu.VMEM((ROWS, 16 * CAP), bf16),
            pltpu.VMEM((EMB, DIM, CAP), bf16),
            pltpu.VMEM((EMB, DIM, CAP), bf16),
            dma((2,)),
            dma((EMB,)),
            dma((EMB,)),
            dma((EMB,)),
            dma((EMB,)),
            dma((2, 6)),
            dma((2, 6)),
            dma((2, SEC)),
            dma((2, 2, 6)),
            dma((2, 2)),
            dma((2, 2, 6)),
            dma((2, 2, ZS)),
            dma((2,)),
            dma((2, XS)),
            dma((2, ZS)),
            dma((EMB,)),
            dma((EMB,)),
        ],
        compiler_params=pltpu.CompilerParams(collective_id=0, has_side_effects=True, vmem_limit_bytes=52 << 20),
    )(
        section_task,
        slot_ids.transpose(1, 2, 0),
        bag_len.T,
        table,
        expert_w,
        tower_w,
        tower_out,
        click_like.T,
        watch.reshape(1, BATCH),
    )
    whole_table = jax.ShapeDtypeStruct((SLOTS * DIM, ROWS), f32)
    new_table, new_accum, tower_grad, expert_grad, head_grad = pl.pallas_call(
        update_kernel,
        out_shape=(
            whole_table,
            whole_table,
            jax.ShapeDtypeStruct((32, WIDE), f32),
            jax.ShapeDtypeStruct((32, WIDE), f32),
            jax.ShapeDtypeStruct((1, WIDE), f32),
        ),
        in_specs=[vmem] * 4,
        out_specs=(vmem,) * 5,
        compiler_params=pltpu.CompilerParams(vmem_limit_bytes=16 << 20),
    )(table, accum, row_grad, packed)

    def back(value):
        return value.reshape(SLOTS, DIM, ROWS).transpose(0, 2, 1)

    return (back(new_table), back(new_accum), expert_grad, tower_grad, head_grad)


def solution(mesh):
    placed = (
        P("sec", "emb", None),
        P("sec", "emb", None),
        P("emb", "sec", None),
        P("emb", "sec"),
        P(None, "sec"),
        P(None, "sec"),
        P("sec", None),
        P("sec"),
        P("emb", None),
        P("emb"),
    )
    return jax.shard_map(
        body,
        mesh=mesh,
        in_specs=placed,
        out_specs=(
            P("sec", "emb", None),
            P("sec", "emb", None),
            P("emb", "sec"),
            P("emb", "sec"),
            P("sec", None),
        ),
        check_vma=False,
    )
```

```python
import jax
import jax.numpy as jnp
from jax import lax
from jax.experimental import pallas as pl
from jax.experimental.pallas import tpu as pltpu
from jax.sharding import PartitionSpec as P

MESH = pl.DeviceIdType.MESH
learn_rate = 0.2
f32 = jnp.float32
bf16 = jnp.bfloat16
i32 = jnp.int32

EMB = 64
SEC = 4
XS = 4
ZS = 8
CAP = 128
DIM = 64
SLOTS = 8
BATCH = 256
ROWS = 512
WIDE = 512


def mm(a, b):
    return lax.dot_general(a, b, (((1,), (0,)), ((), ())), preferred_element_type=f32)


def mm_nt(a, b):
    return lax.dot_general(a, b, (((1,), (1,)), ((), ())), preferred_element_type=f32)


def silu_slope(value):
    logistic = jax.nn.sigmoid(value)
    return logistic * (1.0 + value * (1.0 - logistic))


def hot(size, keys):
    rows = lax.broadcasted_iota(i32, (size, keys.shape[1]), 0)
    return jnp.where(rows == keys, 1.0, 0.0).astype(bf16)


SKIP = ()


class Nothing:
    def start(self):
        pass

    wait = wait_send = wait_recv = start


def remote(src, dst, send, recv, tag, **where):
    if tag in SKIP:
        return Nothing()
    return pltpu.make_async_remote_copy(
        src_ref=src, dst_ref=dst, send_sem=send, recv_sem=recv, device_id=where, device_id_type=MESH
    )


def greet(emb, sec):
    barrier = pltpu.get_barrier_semaphore()

    @pl.loop(1, EMB)
    def _(d):
        pl.semaphore_signal(barrier, inc=1, device_id={"emb": lax.rem(emb + d, EMB)}, device_id_type=MESH)

    for d in range(1, SEC):
        pl.semaphore_signal(barrier, inc=1, device_id={"sec": lax.rem(sec + d, SEC)}, device_id_type=MESH)


def meet():
    pl.semaphore_wait(pltpu.get_barrier_semaphore(), EMB - 1 + SEC - 1)


def route(ids_ref, ob, pos):
    before = lax.broadcasted_iota(i32, (BATCH, BATCH), 0)
    after = lax.broadcasted_iota(i32, (BATCH, BATCH), 1)
    upper = jnp.where(before < after, 1.0, 0.0).astype(bf16)
    shard_row = lax.broadcasted_iota(i32, (EMB, BATCH), 0)
    rank_row = lax.broadcasted_iota(i32, (CAP, BATCH), 0)
    carry = jnp.zeros((EMB, 1), f32)
    total = jnp.zeros((EMB, 2 * CAP), f32)
    for q in range(2 * SLOTS):
        ids = ids_ref[q // 2, q % 2 : q % 2 + 1, :]
        owner = ids >> 9
        key = (ids & (ROWS - 1)) + ((q // 2) * ROWS + 1)
        owned = jnp.where(shard_row == owner, 1.0, 0.0)
        owned_b = owned.astype(bf16)
        prefix = mm(owned_b, upper) + carry
        rank = jnp.sum(owned * prefix, axis=0, keepdims=True).astype(i32)
        carry = carry + jnp.sum(owned, axis=1, keepdims=True)
        pos[q] = owner * CAP + rank
        ranked = rank_row == rank
        high = jnp.where(ranked, (key >> 6).astype(f32), 0.0).astype(bf16)
        low = jnp.where(ranked, (key & 63).astype(f32), 0.0).astype(bf16)
        total = total + mm_nt(owned_b, jnp.concatenate([high, low], axis=0))
    keys = (total[:, :CAP] * 64.0 + total[:, CAP:]).astype(i32) - 1
    for s in range(EMB):
        ob[s] = keys[s : s + 1, :]


def step_kernel(
    task_ref, ids_ref, bag_ref, table_ref, expert_hbm, tower_hbm, out_row_ref, click_ref, watch_ref,
    grad_ref, packed_ref,
    pos, ob, ib, out_rows, in_rows, wide_rows, pooled_ref, tb, expert_ref, tower_ref,
    feats, hiddens, expert_t, tower_t, pre_e, pre_t, shares, part_out, part_in, relay, whole, own_part,
    core_out, core_in, x_out, x_in, z_out, z_in, head_core, head_x, head_z,
    spread, hots, row_hots, out_grads, in_grads,
    load_sem, id_send, id_recv, row_send, row_recv,
    feat_sem, hidden_sem, share_sem, part_sem, core_sem, x_sem, z_sem, hcore_sem, hx_sem, hz_sem, grad_send, grad_recv,
):
    me = lax.axis_index("emb")
    sec = lax.axis_index("sec")
    core = lax.rem(me, 2)
    z = lax.rem(lax.div(me, 2), ZS)
    x = lax.div(me, 2 * ZS)
    half = lax.div(me, 32)
    inner = lax.rem(me, 32)
    partner = me + 1 - 2 * core
    expert_load = pltpu.make_async_copy(expert_hbm, expert_ref, load_sem.at[0])
    tower_load = pltpu.make_async_copy(tower_hbm, tower_ref, load_sem.at[1])
    expert_load.start()
    tower_load.start()
    greet(me, sec)
    route(ids_ref, ob, pos)
    meet()

    def rows_of(r):
        return pl.ds(pl.multiple_of(r * WIDE, WIDE), WIDE)

    def ahead(d):
        group = lax.rem(half + lax.div(d, 32), 2)
        return group * 32 + lax.rem(inner + d, 32)

    def z_shift(i):
        step, odd = lax.div(i + 1, 2), lax.rem(i, 2)
        return lax.rem(step * odd + (ZS - step) * (1 - odd), ZS)

    def chip(t, way):
        group = lax.rem(half + lax.div(t, 16), 2)
        column = 2 * group + lax.rem(x + lax.div(t, ZS), 2)
        return (column * ZS + lax.rem(z + ZS + way * z_shift(lax.rem(t, ZS)), ZS)) * 2

    def id_copy(peer, at):
        return remote(ob.at[peer], ib.at[at], id_send.at[peer], id_recv.at[at], tag="ids", emb=peer)

    def row_copy(peer, at):
        return remote(out_rows.at[peer], in_rows.at[at], row_send.at[peer], row_recv.at[at], tag="rows", emb=peer)

    def grad_copy(peer, at):
        return remote(out_grads.at[peer], in_grads.at[at], grad_send.at[peer], grad_recv.at[at], tag="grads", emb=peer)

    def across(d):
        return lax.rem(sec + d, SEC)

    def sec_copy(buffer, sems, tag, d, at):
        return remote(buffer.at[sec], buffer.at[at], sems.at[0, d], sems.at[1, at], tag=tag, sec=across(d))

    def ring_copy(buffer, sems, tag, i, arriving=False):
        offset, part, way = ((0, 0, 1), (0, 1, 1), (0, 1, 3), (0, 0, 3), (3, 0, 1), (1, 1, 3))[i]
        rows = pl.ds(part * (WIDE // 2), WIDE // 2)
        source = across(offset)
        target = across(4 - way + offset) if arriving else source
        return remote(
            buffer.at[source, rows], buffer.at[target, rows], sems.at[0, i], sems.at[1, i], tag=tag, sec=across(way)
        )

    def gather_sec(buffer, sems, tag, weights, total):
        def came(i):
            ring_copy(buffer, sems, tag, i, True).wait_recv()

        total[...] = mm(weights[sec], buffer[sec])
        came(0)
        ring_copy(buffer, sems, tag, 4).start()
        came(2)
        ring_copy(buffer, sems, tag, 5).start()
        came(1)
        total[...] += mm(weights[across(3)], buffer[across(3)])
        came(3)
        total[...] += mm(weights[across(1)], buffer[across(1)])
        came(4)
        came(5)
        total[...] += mm(weights[across(2)], buffer[across(2)])

    def left(buffer, sems, tag):
        for i in range(6):
            ring_copy(buffer, sems, tag, i).wait_send()

    @pl.loop(0, EMB // 2)
    def _(t):
        base = chip(t, 1)

        @pl.when(t > 0)
        def _():
            id_copy(base + core, me).start()

        id_copy(base + 1 - core, me).start()

    ib[me] = ob[me]
    tb[...] = table_ref[...].astype(bf16)
    expert_load.wait()
    tower_load.wait()

    if "transpose" not in SKIP:

        @pl.loop(0, SEC)
        def _(r):
            expert_t[r] = expert_ref[rows_of(r), :].T
            tower_t[r] = tower_ref[rows_of(r), :].T

    @pl.loop(0, EMB // 2)
    def _(t):
        a = chip(t, -1) + core
        b = chip(t, -1) + 1 - core

        @pl.when(t > 0)
        def _():
            id_copy(a, a).wait_recv()

        id_copy(b, b).wait_recv()
        if "gather" not in SKIP:
            keys = jnp.concatenate([ib[a], ib[b]], axis=1)
            slot = keys >> 9
            picked = mm(tb[...], hot(ROWS, keys & (ROWS - 1)))
            rows = jnp.zeros((DIM, 2 * CAP), f32)
            for s in range(SLOTS):
                rows = rows + jnp.where(slot == s, picked[s * DIM : (s + 1) * DIM], 0.0)
            rows = rows.astype(bf16)
            out_rows[a] = rows[:, :CAP]
            out_rows[b] = rows[:, CAP:]

            @pl.when(t == 0)
            def _():
                in_rows[me] = rows[:, :CAP]

        @pl.when(t > 0)
        def _():
            row_copy(a, me).start()

        row_copy(b, me).start()

    def widen(base, slabs):
        for h in range(slabs):
            wide_rows[:, h * CAP : (h + 1) * CAP] = in_rows[pl.ds((base + h) * 8, 8)].reshape(8 * DIM, CAP)

    def pool(base, slabs, first, last, begin, end):
        @pl.loop(begin, end)
        def _(s):
            rows = pl.ds(pl.multiple_of(s * DIM, DIM), DIM)
            pooled = jnp.zeros((DIM, BATCH), f32) if first else pooled_ref[rows, :]
            for k in range(2):
                place = pos[2 * s + k]
                shard = place >> 7
                low = jnp.where(bag_ref[pl.ds(s, 1), :] > k, shard & 7, -1)
                key = ((shard >> 3) - base) * CAP + (place & (CAP - 1))
                picked = mm(wide_rows[:, : slabs * CAP], hot(slabs * CAP, key))
                for g in range(8):
                    pooled = pooled + jnp.where(low == g, picked[g * DIM : (g + 1) * DIM], 0.0)
            if last:
                feats[sec, rows, :] = pooled.astype(bf16)
            else:
                pooled_ref[rows, :] = pooled

    @pl.loop(1, 32)
    def _(d):
        peer = ahead(d)
        row_copy(peer, peer).wait_recv()

    widen(4 * half, 4)
    pool(4 * half, 4, True, False, 0, SLOTS)

    def column_came(column):
        @pl.loop(0, 16)
        def _(j):
            peer = column * 16 + j
            row_copy(peer, peer).wait_recv()

    near = 2 * (1 - half) + lax.rem(x, 2)
    far = 2 * (1 - half) + lax.rem(x + 1, 2)
    column_came(near)
    widen(2 * near, 2)
    pool(2 * near, 2, False, False, 0, SLOTS)
    column_came(far)
    widen(2 * far, 2)
    pool(2 * far, 2, False, True, 0, SLOTS // 2)
    ring_copy(feats, feat_sem, "feats", 0).start()
    ring_copy(feats, feat_sem, "feats", 3).start()
    pool(2 * far, 2, False, True, SLOTS // 2, SLOTS)
    ring_copy(feats, feat_sem, "feats", 2).start()
    ring_copy(feats, feat_sem, "feats", 1).start()
    gather_sec(feats, feat_sem, "feats", expert_t, pre_e)
    hiddens[sec] = jax.nn.silu(pre_e[...]).astype(bf16)
    for i in (0, 2, 1, 3):
        ring_copy(hiddens, hidden_sem, "hiddens", i).start()
    gather_sec(hiddens, hidden_sem, "hiddens", tower_t, pre_t)
    out_col = jnp.broadcast_to(out_row_ref[...], (8, WIDE)).T[:, 0:1]
    active = jax.nn.silu(pre_t[...])
    share = jnp.sum(active * out_col, axis=0, keepdims=True)
    chosen = jnp.where(lax.broadcasted_iota(i32, (8, BATCH), 0) == task_ref[0], 1.0, 0.0)
    shares[sec] = share * chosen
    for d in (2, 1, 3):
        sec_copy(shares, share_sem, "shares", d, sec).start()
    slope = out_col * silu_slope(pre_t[...])
    for d in (1, 3, 2):
        sec_copy(shares, share_sem, "shares", d, across(d)).wait_recv()
    logits = (shares[0] + shares[1]) + (shares[2] + shares[3])
    err = logits[0:1] + logits[1:2] + logits[2:3] - watch_ref[...]
    chance = jax.nn.sigmoid(logits[0:2]) - click_ref[...] + err
    back = chance[0:1] * chosen[0:1] + chance[1:2] * chosen[1:2] + err * chosen[2:3]
    tower_delta = (back * slope).astype(bf16)

    low_half = slice(0, WIDE // 2)
    high_half = slice(WIDE // 2, WIDE)

    def part_copy(n, i):
        return remote(
            part_out.at[n, i], part_in.at[n, i], part_sem.at[n, 0, i], part_sem.at[n, 1, i],
            tag="part", sec=across((1, 3, 1, 3, 1, 3)[i]),
        )

    def part(n, weights_ref, delta):
        def send(i, value):
            part_out[n, i] = value.astype(bf16)
            part_copy(n, i).start()

        value = mm(weights_ref[rows_of(across(2)), :], delta)
        send(0, value[low_half])
        send(1, value[high_half])
        value = mm(weights_ref[rows_of(across(1)), :], delta)
        send(2, value[high_half])
        relay[0] = value[low_half]
        value = mm(weights_ref[rows_of(across(3)), :], delta)
        send(3, value[low_half])
        relay[1] = value[high_half]
        own_part[...] = mm(weights_ref[rows_of(sec), :], delta)
        for i in range(2):
            part_copy(n, i).wait_recv()
            send(4 + i, relay[i] + part_in[n, i].astype(f32))

    def part_sum(n):
        for i in range(2, 6):
            part_copy(n, i).wait_recv()
        own_part[low_half, :] += part_in[n, 3].astype(f32) + part_in[n, 4].astype(f32)
        own_part[high_half, :] += part_in[n, 2].astype(f32) + part_in[n, 5].astype(f32)
        for i in range(6):
            part_copy(n, i).wait_send()

    def core_copy(n):
        return remote(core_out.at[n], core_in.at[n], core_sem.at[0, n], core_sem.at[1, n], tag="core", emb=partner)

    def weight_grad(n, source, delta):
        @pl.loop(0, SEC)
        def _(r):
            whole[n, pl.ds(r * 16, 16)] = mm_nt(source[r], delta).reshape(16, 32, WIDE)

        @pl.loop(0, 32)
        def _(j):
            core_out[n, j] = whole[n, 2 * j + 1 - core].astype(bf16)

        core_copy(n).start()

    def x_copy(n, i):
        to = lax.rem(x + (1, 3, 1, 3, 1, 3)[i], XS)
        return remote(
            x_out.at[n, i], x_in.at[n, i], x_sem.at[n, 0, i], x_sem.at[n, 1, i], tag="x", emb=(to * ZS + z) * 2 + core
        )

    def z_copy(n, d):
        to = lax.rem(z + d, ZS)
        return remote(
            z_out.at[n, to], z_in.at[n, z], z_sem.at[n, 0, d], z_sem.at[n, 1, z], tag="z", emb=(x * ZS + to) * 2 + core
        )

    def z_arrive(n, d):
        to = lax.rem(z + d, ZS)
        return remote(
            z_out.at[n, to], z_in.at[n, to], z_sem.at[n, 0, d], z_sem.at[n, 1, to], tag="z", emb=(x * ZS + to) * 2 + core
        )

    def core_sum(n):
        core_copy(n).wait()

        @pl.loop(0, 32)
        def _(j):
            value = whole[n, 2 * j + core] + core_in[n, j].astype(f32)
            whole[n, 2 * j + core] = value

        for i, (d, part) in enumerate(((2, 0), (2, 1), (1, 1), (3, 0))):

            @pl.loop(0, ZS // 2)
            def _(j):
                x_out[n, i, j] = whole[n, place_of(d, part * (ZS // 2) + j)].astype(bf16)

            x_copy(n, i).start()

    def place_of(d, j):
        return 2 * (lax.rem(x + d, XS) * ZS + j) + core

    def x_relay(n):
        for i, d in ((0, 1), (1, 3)):
            x_copy(n, i).wait_recv()

            @pl.loop(0, ZS // 2)
            def _(j):
                value = whole[n, place_of(d, i * (ZS // 2) + j)] + x_in[n, i, j].astype(f32)
                x_out[n, 4 + i, j] = value.astype(bf16)

            x_copy(n, 4 + i).start()

    def x_sum(n):
        for part, (one, two) in enumerate(((3, 4), (2, 5))):
            x_copy(n, one).wait_recv()
            x_copy(n, two).wait_recv()

            @pl.loop(0, ZS // 2)
            def _(j):
                at = part * (ZS // 2) + j
                value = whole[n, place_of(0, at)] + x_in[n, one, j].astype(f32) + x_in[n, two, j].astype(f32)
                whole[n, place_of(0, at)] = value
                z_out[n, at] = value.astype(bf16)

        for d in range(1, ZS):
            z_copy(n, d).start()

    def z_sum(n):
        for d in range(1, ZS):
            z_arrive(n, d).wait_recv()
        value = whole[n, me]
        for d in range(1, ZS):
            value = value + z_in[n, lax.rem(z + d, ZS)].astype(f32)
        packed_ref[pl.ds(32 * n, 32), :] = value
        for i in range(6):
            x_copy(n, i).wait_send()
        for d in range(1, ZS):
            z_copy(n, d).wait_send()

    def hc_copy():
        return remote(head_core.at[0], head_core.at[1], hcore_sem.at[0], hcore_sem.at[1], tag="head", emb=partner)

    def hx_copy(d, at):
        to = lax.rem(x + d, XS)
        return remote(head_x.at[x], head_x.at[at], hx_sem.at[0, d], hx_sem.at[1, at], tag="head", emb=(to * ZS + z) * 2 + core)

    def hz_copy(d, at):
        to = lax.rem(z + d, ZS)
        return remote(head_z.at[z], head_z.at[at], hz_sem.at[0, d], hz_sem.at[1, at], tag="head", emb=(x * ZS + to) * 2 + core)

    part(0, tower_ref, tower_delta)
    head_core[0] = lax.dot_general(
        back, active, (((1,), (1,)), ((), ())), preferred_element_type=f32, precision=lax.Precision.HIGHEST
    )
    hc_copy().start()
    weight_grad(0, hiddens, tower_delta)
    hc_copy().wait()
    head_x[x] = head_core[0] + head_core[1]
    for d in range(1, XS):
        hx_copy(d, x).start()
    part_sum(0)
    expert_delta = (own_part[...] * silu_slope(pre_e[...])).astype(bf16)
    part(1, expert_ref, expert_delta)
    for d in range(1, XS):
        hx_copy(d, lax.rem(x + d, XS)).wait_recv()
    head_z[z] = (head_x[0] + head_x[1]) + (head_x[2] + head_x[3])
    for d in range(1, ZS):
        hz_copy(d, z).start()
    core_sum(0)
    weight_grad(1, feats, expert_delta)
    x_relay(0)
    core_sum(1)
    left(feats, feat_sem, "feats")
    left(hiddens, hidden_sem, "hiddens")
    for d in (2, 1, 3):
        sec_copy(shares, share_sem, "shares", d, sec).wait_send()
    part_sum(1)

    @pl.loop(0, SLOTS)
    def _(s):
        grad = own_part[pl.ds(pl.multiple_of(s * DIM, DIM), DIM), :]
        for k in range(2):
            low = jnp.where(bag_ref[pl.ds(s, 1), :] > k, (pos[2 * s + k] >> 7) & 7, -1)
            columns = pl.ds(pl.multiple_of((2 * s + k) * BATCH, BATCH), BATCH)
            for g in range(8):
                spread[g * DIM : (g + 1) * DIM, columns] = jnp.where(low == g, grad, 0.0).astype(bf16)

    @pl.loop(0, 4)
    def _(t):
        pair = lax.rem(x + t, 4)

        for q in range(2 * SLOTS):
            place = pos[q]
            key = ((place >> 10) - 2 * pair) * CAP + (place & (CAP - 1))
            hots[:, q * BATCH : (q + 1) * BATCH] = hot(2 * CAP, key)
        total = mm_nt(spread[...], hots[...]).astype(bf16)
        for h in range(2):
            for g in range(8):
                peer = (2 * pair + h) * 8 + g
                out_grads[peer] = total[g * DIM : (g + 1) * DIM, h * CAP : (h + 1) * CAP]

        @pl.when(t == 0)
        def _():
            in_grads[me] = out_grads[me]

        @pl.loop(0, ZS)
        def _(j):
            base = (pair * ZS + lax.rem(z + z_shift(j), ZS)) * 2
            for c in range(2):
                peer = base + c

                @pl.when(peer != me)
                def _():
                    grad_copy(peer, me).start()

        @pl.when(t == 0)
        def _():
            x_relay(1)
            x_sum(0)

    x_sum(1)
    z_sum(0)
    for d in range(1, ZS):
        hz_copy(d, lax.rem(z + d, ZS)).wait_recv()
    head = head_z[0]
    for j in range(1, ZS):
        head = head + head_z[j]
    packed_ref[64:72, :] = jnp.broadcast_to(head, (8, WIDE))

    grad_ref[...] = jnp.zeros((WIDE, ROWS), f32)

    @pl.loop(1, EMB)
    def _(d):
        peer = lax.rem(me + d, EMB)
        id_copy(peer, me).wait_send()
        row_copy(peer, me).wait_send()


    @pl.loop(0, XS)
    def _(t):
        first = lax.rem(x + XS - t, XS) * 16

        @pl.loop(0, 16)
        def _(j):
            peer = first + j

            @pl.when(peer != me)
            def _():
                grad_copy(peer, peer).wait_recv()

        if "scatter" not in SKIP:

            @pl.loop(0, 8)
            def _(j):
                a = first + 2 * j
                keys = jnp.concatenate([ib[a], ib[a + 1]], axis=1)
                slot = keys >> 9
                grads = jnp.concatenate([in_grads[a], in_grads[a + 1]], axis=1).astype(f32)
                wide = jnp.concatenate([jnp.where(slot == s, grads, 0.0) for s in range(SLOTS)], axis=0).astype(bf16)
                columns = pl.ds(pl.multiple_of(j * 2 * CAP, 2 * CAP), 2 * CAP)
                spread[:, columns] = wide
                row_hots[:, columns] = hot(ROWS, keys & (ROWS - 1))

            grad_ref[...] += mm_nt(spread[:, : 16 * CAP], row_hots[...])

    z_sum(1)
    for d in range(1, XS):
        hx_copy(d, x).wait_send()
    for d in range(1, ZS):
        hz_copy(d, z).wait_send()

    @pl.loop(1, EMB)
    def _(d):
        peer = lax.rem(me + d, EMB)
        grad_copy(peer, me).wait_send()


def update_kernel(table_ref, accum_ref, grad_ref, packed_ref, new_table, new_accum, tower_grad, expert_grad, head_grad):
    @pl.loop(0, SLOTS)
    def _(s):
        rows = pl.ds(pl.multiple_of(s * DIM, DIM), DIM)
        grad = grad_ref[rows, :]
        accum = accum_ref[rows, :] + grad * grad
        new_accum[rows, :] = accum
        new_table[rows, :] = table_ref[rows, :] - learn_rate * grad / jnp.sqrt(accum)

    tower_grad[...] = packed_ref[:32, :]
    expert_grad[...] = packed_ref[32:64, :]
    head_grad[...] = packed_ref[64:65, :]


def body(
    emb_table,
    emb_accum,
    slot_ids,
    bag_len,
    expert_w,
    tower_w,
    tower_out,
    section_task,
    click_like,
    watch,
):
    vmem = pl.BlockSpec(memory_space=pltpu.VMEM)
    dma = pltpu.SemaphoreType.DMA
    table = emb_table.transpose(0, 2, 1).reshape(SLOTS * DIM, ROWS)
    accum = emb_accum.transpose(0, 2, 1).reshape(SLOTS * DIM, ROWS)
    anywhere = pl.BlockSpec(memory_space=pl.ANY)
    row_grad, packed = pl.pallas_call(
        step_kernel,
        out_shape=(
            jax.ShapeDtypeStruct((SLOTS * DIM, ROWS), f32),
            jax.ShapeDtypeStruct((72, WIDE), f32),
        ),
        in_specs=[pl.BlockSpec(memory_space=pltpu.SMEM), vmem, vmem, vmem, anywhere, anywhere, vmem, vmem, vmem],
        out_specs=(vmem,) * 2,
        scratch_shapes=[
            pltpu.VMEM((2 * SLOTS, 1, BATCH), i32),
            pltpu.VMEM((EMB, 1, CAP), i32),
            pltpu.VMEM((EMB, 1, CAP), i32),
            pltpu.VMEM((EMB, DIM, CAP), bf16),
            pltpu.VMEM((EMB, DIM, CAP), bf16),
            pltpu.VMEM((8 * DIM, 4 * CAP), bf16),
            pltpu.VMEM((8 * DIM, BATCH), f32),
            pltpu.VMEM((SLOTS * DIM, ROWS), bf16),
            pltpu.VMEM((SEC * WIDE, WIDE), bf16),
            pltpu.VMEM((SEC * WIDE, WIDE), bf16),
            pltpu.VMEM((SEC, WIDE, BATCH), bf16),
            pltpu.VMEM((SEC, WIDE, BATCH), bf16),
            pltpu.VMEM((SEC, WIDE, WIDE), bf16),
            pltpu.VMEM((SEC, WIDE, WIDE), bf16),
            pltpu.VMEM((WIDE, BATCH), f32),
            pltpu.VMEM((WIDE, BATCH), f32),
            pltpu.VMEM((SEC, 8, BATCH), f32),
            pltpu.VMEM((2, 6, WIDE // 2, BATCH), bf16),
            pltpu.VMEM((2, 6, WIDE // 2, BATCH), bf16),
            pltpu.VMEM((2, WIDE // 2, BATCH), f32),
            pltpu.VMEM((2, EMB, 32, WIDE), f32),
            pltpu.VMEM((WIDE, BATCH), f32),
            pltpu.VMEM((2, 32, 32, WIDE), bf16),
            pltpu.VMEM((2, 32, 32, WIDE), bf16),
            pltpu.VMEM((2, 6, ZS // 2, 32, WIDE), bf16),
            pltpu.VMEM((2, 6, ZS // 2, 32, WIDE), bf16),
            pltpu.VMEM((2, ZS, 32, WIDE), bf16),
            pltpu.VMEM((2, ZS, 32, WIDE), bf16),
            pltpu.VMEM((2, 1, WIDE), f32),
            pltpu.VMEM((XS, 1, WIDE), f32),
            pltpu.VMEM((ZS, 1, WIDE), f32),
            pltpu.VMEM((8 * DIM, 2 * SLOTS * BATCH), bf16),
            pltpu.VMEM((2 * CAP, 2 * SLOTS * BATCH), bf16),
            pltpu.VMEM((ROWS, 16 * CAP), bf16),
            pltpu.VMEM((EMB, DIM, CAP), bf16),
            pltpu.VMEM((EMB, DIM, CAP), bf16),
            dma((2,)),
            dma((EMB,)),
            dma((EMB,)),
            dma((EMB,)),
            dma((EMB,)),
            dma((2, 6)),
            dma((2, 6)),
            dma((2, SEC)),
            dma((2, 2, 6)),
            dma((2, 2)),
            dma((2, 2, 6)),
            dma((2, 2, ZS)),
            dma((2,)),
            dma((2, XS)),
            dma((2, ZS)),
            dma((EMB,)),
            dma((EMB,)),
        ],
        compiler_params=pltpu.CompilerParams(collective_id=0, has_side_effects=True, vmem_limit_bytes=52 << 20),
    )(
        section_task,
        slot_ids.transpose(1, 2, 0),
        bag_len.T,
        table,
        expert_w,
        tower_w,
        tower_out,
        click_like.T,
        watch.reshape(1, BATCH),
    )
    whole_table = jax.ShapeDtypeStruct((SLOTS * DIM, ROWS), f32)
    new_table, new_accum, tower_grad, expert_grad, head_grad = pl.pallas_call(
        update_kernel,
        out_shape=(
            whole_table,
            whole_table,
            jax.ShapeDtypeStruct((32, WIDE), f32),
            jax.ShapeDtypeStruct((32, WIDE), f32),
            jax.ShapeDtypeStruct((1, WIDE), f32),
        ),
        in_specs=[vmem] * 4,
        out_specs=(vmem,) * 5,
        compiler_params=pltpu.CompilerParams(vmem_limit_bytes=16 << 20),
    )(table, accum, row_grad, packed)

    def back(value):
        return value.reshape(SLOTS, DIM, ROWS).transpose(0, 2, 1)

    return (back(new_table), back(new_accum), expert_grad, tower_grad, head_grad)


def solution(mesh):
    placed = (
        P("sec", "emb", None),
        P("sec", "emb", None),
        P("emb", "sec", None),
        P("emb", "sec"),
        P(None, "sec"),
        P(None, "sec"),
        P("sec", None),
        P("sec"),
        P("emb", None),
        P("emb"),
    )
    return jax.shard_map(
        body,
        mesh=mesh,
        in_specs=placed,
        out_specs=(
            P("sec", "emb", None),
            P("sec", "emb", None),
            P("emb", "sec"),
            P("emb", "sec"),
            P("sec", None),
        ),
        check_vma=False,
    )
```

```python
import jax
import jax.numpy as jnp
from jax import lax
from jax.experimental import pallas as pl
from jax.experimental.pallas import tpu as pltpu
from jax.sharding import PartitionSpec as P

MESH = pl.DeviceIdType.MESH
learn_rate = 0.2
f32 = jnp.float32
bf16 = jnp.bfloat16
i32 = jnp.int32

EMB = 64
SEC = 4
XS = 4
ZS = 8
CAP = 128
DIM = 64
SLOTS = 8
BATCH = 256
ROWS = 512
WIDE = 512


def mm(a, b):
    return lax.dot_general(a, b, (((1,), (0,)), ((), ())), preferred_element_type=f32)


def mm_nt(a, b):
    return lax.dot_general(a, b, (((1,), (1,)), ((), ())), preferred_element_type=f32)


def silu_slope(value):
    logistic = jax.nn.sigmoid(value)
    return logistic * (1.0 + value * (1.0 - logistic))


def hot(size, keys):
    rows = lax.broadcasted_iota(i32, (size, keys.shape[1]), 0)
    return jnp.where(rows == keys, 1.0, 0.0).astype(bf16)


SKIP = ()


class Nothing:
    def start(self):
        pass

    wait = wait_send = wait_recv = start


def remote(src, dst, send, recv, tag, **where):
    if tag in SKIP:
        return Nothing()
    return pltpu.make_async_remote_copy(
        src_ref=src, dst_ref=dst, send_sem=send, recv_sem=recv, device_id=where, device_id_type=MESH
    )


def greet(emb, sec):
    barrier = pltpu.get_barrier_semaphore()

    @pl.loop(1, EMB)
    def _(d):
        pl.semaphore_signal(barrier, inc=1, device_id={"emb": lax.rem(emb + d, EMB)}, device_id_type=MESH)

    for d in range(1, SEC):
        pl.semaphore_signal(barrier, inc=1, device_id={"sec": lax.rem(sec + d, SEC)}, device_id_type=MESH)


def meet():
    pl.semaphore_wait(pltpu.get_barrier_semaphore(), EMB - 1 + SEC - 1)


def route(ids_ref, ob, pos):
    before = lax.broadcasted_iota(i32, (BATCH, BATCH), 0)
    after = lax.broadcasted_iota(i32, (BATCH, BATCH), 1)
    upper = jnp.where(before < after, 1.0, 0.0).astype(bf16)
    shard_row = lax.broadcasted_iota(i32, (EMB, BATCH), 0)
    rank_row = lax.broadcasted_iota(i32, (CAP, BATCH), 0)
    carry = jnp.zeros((EMB, 1), f32)
    total = jnp.zeros((EMB, 2 * CAP), f32)
    for q in range(2 * SLOTS):
        ids = ids_ref[q // 2, q % 2 : q % 2 + 1, :]
        owner = ids >> 9
        key = (ids & (ROWS - 1)) + ((q // 2) * ROWS + 1)
        owned = jnp.where(shard_row == owner, 1.0, 0.0)
        owned_b = owned.astype(bf16)
        prefix = mm(owned_b, upper) + carry
        rank = jnp.sum(owned * prefix, axis=0, keepdims=True).astype(i32)
        carry = carry + jnp.sum(owned, axis=1, keepdims=True)
        pos[q] = owner * CAP + rank
        ranked = rank_row == rank
        high = jnp.where(ranked, (key >> 6).astype(f32), 0.0).astype(bf16)
        low = jnp.where(ranked, (key & 63).astype(f32), 0.0).astype(bf16)
        total = total + mm_nt(owned_b, jnp.concatenate([high, low], axis=0))
    keys = (total[:, :CAP] * 64.0 + total[:, CAP:]).astype(i32) - 1
    for s in range(EMB):
        ob[s] = keys[s : s + 1, :]


def step_kernel(
    task_ref, ids_ref, bag_ref, table_ref, expert_hbm, tower_hbm, out_row_ref, click_ref, watch_ref,
    grad_ref, packed_ref,
    pos, ob, ib, out_rows, in_rows, wide_rows, pooled_ref, tb, expert_ref, tower_ref,
    feats, hiddens, expert_t, tower_t, pre_e, pre_t, shares, part_out, part_in, relay, whole, own_part,
    core_out, core_in, x_out, x_in, z_out, z_in, head_core, head_x, head_z,
    spread, hots, row_hots, out_grads, in_grads,
    load_sem, id_send, id_recv, row_send, row_recv,
    feat_sem, hidden_sem, share_sem, part_sem, core_sem, x_sem, z_sem, hcore_sem, hx_sem, hz_sem, grad_send, grad_recv,
):
    me = lax.axis_index("emb")
    sec = lax.axis_index("sec")
    core = lax.rem(me, 2)
    z = lax.rem(lax.div(me, 2), ZS)
    x = lax.div(me, 2 * ZS)
    half = lax.div(me, 32)
    inner = lax.rem(me, 32)
    partner = me + 1 - 2 * core
    expert_load = pltpu.make_async_copy(expert_hbm, expert_ref, load_sem.at[0])
    tower_load = pltpu.make_async_copy(tower_hbm, tower_ref, load_sem.at[1])
    expert_load.start()
    tower_load.start()
    greet(me, sec)
    route(ids_ref, ob, pos)
    meet()

    def rows_of(r):
        return pl.ds(pl.multiple_of(r * WIDE, WIDE), WIDE)

    def ahead(d):
        group = lax.rem(half + lax.div(d, 32), 2)
        return group * 32 + lax.rem(inner + d, 32)

    def z_shift(i):
        step, odd = lax.div(i + 1, 2), lax.rem(i, 2)
        return lax.rem(step * odd + (ZS - step) * (1 - odd), ZS)

    def chip(t, way):
        group = lax.rem(half + lax.div(t, 16), 2)
        column = 2 * group + lax.rem(x + lax.div(t, ZS), 2)
        return (column * ZS + lax.rem(z + ZS + way * z_shift(lax.rem(t, ZS)), ZS)) * 2

    def id_copy(peer, at):
        return remote(ob.at[peer], ib.at[at], id_send.at[peer], id_recv.at[at], tag="ids", emb=peer)

    def row_copy(peer, at):
        return remote(out_rows.at[peer], in_rows.at[at], row_send.at[peer], row_recv.at[at], tag="rows", emb=peer)

    def grad_copy(peer, at):
        return remote(out_grads.at[peer], in_grads.at[at], grad_send.at[peer], grad_recv.at[at], tag="grads", emb=peer)

    def across(d):
        return lax.rem(sec + d, SEC)

    def sec_copy(buffer, sems, tag, d, at):
        return remote(buffer.at[sec], buffer.at[at], sems.at[0, d], sems.at[1, at], tag=tag, sec=across(d))

    def ring_copy(buffer, sems, tag, i, arriving=False):
        offset, part, way = ((0, 0, 1), (0, 1, 1), (0, 1, 3), (0, 0, 3), (3, 0, 1), (1, 1, 3))[i]
        rows = pl.ds(part * (WIDE // 2), WIDE // 2)
        source = across(offset)
        target = across(4 - way + offset) if arriving else source
        return remote(
            buffer.at[source, rows], buffer.at[target, rows], sems.at[0, i], sems.at[1, i], tag=tag, sec=across(way)
        )

    def gather_sec(buffer, sems, tag, weights, total):
        def came(i):
            ring_copy(buffer, sems, tag, i, True).wait_recv()

        total[...] = mm(weights[sec], buffer[sec])
        came(0)
        ring_copy(buffer, sems, tag, 4).start()
        came(2)
        ring_copy(buffer, sems, tag, 5).start()
        came(1)
        total[...] += mm(weights[across(3)], buffer[across(3)])
        came(3)
        total[...] += mm(weights[across(1)], buffer[across(1)])
        came(4)
        came(5)
        total[...] += mm(weights[across(2)], buffer[across(2)])

    def left(buffer, sems, tag):
        for i in range(6):
            ring_copy(buffer, sems, tag, i).wait_send()

    @pl.loop(0, EMB // 2)
    def _(t):
        base = chip(t, 1)

        @pl.when(t > 0)
        def _():
            id_copy(base + core, me).start()

        id_copy(base + 1 - core, me).start()

    ib[me] = ob[me]
    tb[...] = table_ref[...].astype(bf16)
    expert_load.wait()
    tower_load.wait()

    if "transpose" not in SKIP:

        @pl.loop(0, SEC)
        def _(r):
            expert_t[r] = expert_ref[rows_of(r), :].T
            tower_t[r] = tower_ref[rows_of(r), :].T

    @pl.loop(0, EMB // 2)
    def _(t):
        a = chip(t, -1) + core
        b = chip(t, -1) + 1 - core

        @pl.when(t > 0)
        def _():
            id_copy(a, a).wait_recv()

        id_copy(b, b).wait_recv()
        if "gather" not in SKIP:
            keys = jnp.concatenate([ib[a], ib[b]], axis=1)
            slot = keys >> 9
            picked = mm(tb[...], hot(ROWS, keys & (ROWS - 1)))
            rows = jnp.zeros((DIM, 2 * CAP), f32)
            for s in range(SLOTS):
                rows = rows + jnp.where(slot == s, picked[s * DIM : (s + 1) * DIM], 0.0)
            rows = rows.astype(bf16)
            out_rows[a] = rows[:, :CAP]
            out_rows[b] = rows[:, CAP:]

            @pl.when(t == 0)
            def _():
                in_rows[me] = rows[:, :CAP]

        @pl.when(t > 0)
        def _():
            row_copy(a, me).start()

        row_copy(b, me).start()

    def widen(base, slabs):
        for h in range(slabs):
            wide_rows[:, h * CAP : (h + 1) * CAP] = in_rows[pl.ds((base + h) * 8, 8)].reshape(8 * DIM, CAP)

    def pool(base, slabs, first, last, begin, end):
        @pl.loop(begin, end)
        def _(s):
            rows = pl.ds(pl.multiple_of(s * DIM, DIM), DIM)
            pooled = jnp.zeros((DIM, BATCH), f32) if first else pooled_ref[rows, :]
            for k in range(2):
                place = pos[2 * s + k]
                shard = place >> 7
                low = jnp.where(bag_ref[pl.ds(s, 1), :] > k, shard & 7, -1)
                key = ((shard >> 3) - base) * CAP + (place & (CAP - 1))
                picked = mm(wide_rows[:, : slabs * CAP], hot(slabs * CAP, key))
                for g in range(8):
                    pooled = pooled + jnp.where(low == g, picked[g * DIM : (g + 1) * DIM], 0.0)
            if last:
                feats[sec, rows, :] = pooled.astype(bf16)
            else:
                pooled_ref[rows, :] = pooled

    @pl.loop(1, 32)
    def _(d):
        peer = ahead(d)
        row_copy(peer, peer).wait_recv()

    widen(4 * half, 4)
    pool(4 * half, 4, True, False, 0, SLOTS)

    def column_came(column):
        @pl.loop(0, 16)
        def _(j):
            peer = column * 16 + j
            row_copy(peer, peer).wait_recv()

    near = 2 * (1 - half) + lax.rem(x, 2)
    far = 2 * (1 - half) + lax.rem(x + 1, 2)
    column_came(near)
    widen(2 * near, 2)
    pool(2 * near, 2, False, False, 0, SLOTS)
    column_came(far)
    widen(2 * far, 2)
    pool(2 * far, 2, False, True, 0, SLOTS // 2)
    ring_copy(feats, feat_sem, "feats", 0).start()
    ring_copy(feats, feat_sem, "feats", 3).start()
    pool(2 * far, 2, False, True, SLOTS // 2, SLOTS)
    ring_copy(feats, feat_sem, "feats", 2).start()
    ring_copy(feats, feat_sem, "feats", 1).start()
    gather_sec(feats, feat_sem, "feats", expert_t, pre_e)
    hiddens[sec] = jax.nn.silu(pre_e[...]).astype(bf16)
    for i in (0, 2, 1, 3):
        ring_copy(hiddens, hidden_sem, "hiddens", i).start()
    gather_sec(hiddens, hidden_sem, "hiddens", tower_t, pre_t)
    out_col = jnp.broadcast_to(out_row_ref[...], (8, WIDE)).T[:, 0:1]
    active = jax.nn.silu(pre_t[...])
    share = jnp.sum(active * out_col, axis=0, keepdims=True)
    chosen = jnp.where(lax.broadcasted_iota(i32, (8, BATCH), 0) == task_ref[0], 1.0, 0.0)
    shares[sec] = share * chosen
    for d in (2, 1, 3):
        sec_copy(shares, share_sem, "shares", d, sec).start()
    slope = out_col * silu_slope(pre_t[...])
    for d in (1, 3, 2):
        sec_copy(shares, share_sem, "shares", d, across(d)).wait_recv()
    logits = (shares[0] + shares[1]) + (shares[2] + shares[3])
    err = logits[0:1] + logits[1:2] + logits[2:3] - watch_ref[...]
    chance = jax.nn.sigmoid(logits[0:2]) - click_ref[...] + err
    back = chance[0:1] * chosen[0:1] + chance[1:2] * chosen[1:2] + err * chosen[2:3]
    tower_delta = (back * slope).astype(bf16)

    low_half = slice(0, WIDE // 2)
    high_half = slice(WIDE // 2, WIDE)

    def part_copy(n, i):
        return remote(
            part_out.at[n, i], part_in.at[n, i], part_sem.at[n, 0, i], part_sem.at[n, 1, i],
            tag="part", sec=across((1, 3, 1, 3, 1, 3)[i]),
        )

    def part(n, weights_ref, delta):
        def send(i, value):
            part_out[n, i] = value.astype(bf16)
            part_copy(n, i).start()

        value = mm(weights_ref[rows_of(across(2)), :], delta)
        send(0, value[low_half])
        send(1, value[high_half])
        value = mm(weights_ref[rows_of(across(1)), :], delta)
        send(2, value[high_half])
        relay[0] = value[low_half]
        value = mm(weights_ref[rows_of(across(3)), :], delta)
        send(3, value[low_half])
        relay[1] = value[high_half]
        own_part[...] = mm(weights_ref[rows_of(sec), :], delta)
        for i in range(2):
            part_copy(n, i).wait_recv()
            send(4 + i, relay[i] + part_in[n, i].astype(f32))

    def part_sum(n):
        for i in range(2, 6):
            part_copy(n, i).wait_recv()
        own_part[low_half, :] += part_in[n, 3].astype(f32) + part_in[n, 4].astype(f32)
        own_part[high_half, :] += part_in[n, 2].astype(f32) + part_in[n, 5].astype(f32)
        for i in range(6):
            part_copy(n, i).wait_send()

    def core_copy(n):
        return remote(core_out.at[n], core_in.at[n], core_sem.at[0, n], core_sem.at[1, n], tag="core", emb=partner)

    def weight_grad(n, source, delta):
        @pl.loop(0, SEC)
        def _(r):
            whole[n, pl.ds(r * 16, 16)] = mm_nt(source[r], delta).reshape(16, 32, WIDE)

        @pl.loop(0, 32)
        def _(j):
            core_out[n, j] = whole[n, 2 * j + 1 - core].astype(bf16)

        core_copy(n).start()

    def x_copy(n, i):
        to = lax.rem(x + (1, 3, 1, 3, 1, 3)[i], XS)
        return remote(
            x_out.at[n, i], x_in.at[n, i], x_sem.at[n, 0, i], x_sem.at[n, 1, i], tag="x", emb=(to * ZS + z) * 2 + core
        )

    def z_copy(n, d):
        to = lax.rem(z + d, ZS)
        return remote(
            z_out.at[n, to], z_in.at[n, z], z_sem.at[n, 0, d], z_sem.at[n, 1, z], tag="z", emb=(x * ZS + to) * 2 + core
        )

    def z_arrive(n, d):
        to = lax.rem(z + d, ZS)
        return remote(
            z_out.at[n, to], z_in.at[n, to], z_sem.at[n, 0, d], z_sem.at[n, 1, to], tag="z", emb=(x * ZS + to) * 2 + core
        )

    def core_sum(n):
        core_copy(n).wait()

        @pl.loop(0, 32)
        def _(j):
            value = whole[n, 2 * j + core] + core_in[n, j].astype(f32)
            whole[n, 2 * j + core] = value

        for i, (d, part) in enumerate(((2, 0), (2, 1), (1, 1), (3, 0))):

            @pl.loop(0, ZS // 2)
            def _(j):
                x_out[n, i, j] = whole[n, place_of(d, part * (ZS // 2) + j)].astype(bf16)

            x_copy(n, i).start()

    def place_of(d, j):
        return 2 * (lax.rem(x + d, XS) * ZS + j) + core

    def x_relay(n):
        for i, d in ((0, 1), (1, 3)):
            x_copy(n, i).wait_recv()

            @pl.loop(0, ZS // 2)
            def _(j):
                value = whole[n, place_of(d, i * (ZS // 2) + j)] + x_in[n, i, j].astype(f32)
                x_out[n, 4 + i, j] = value.astype(bf16)

            x_copy(n, 4 + i).start()

    def x_sum(n):
        for part, (one, two) in enumerate(((3, 4), (2, 5))):
            x_copy(n, one).wait_recv()
            x_copy(n, two).wait_recv()

            @pl.loop(0, ZS // 2)
            def _(j):
                at = part * (ZS // 2) + j
                value = whole[n, place_of(0, at)] + x_in[n, one, j].astype(f32) + x_in[n, two, j].astype(f32)
                whole[n, place_of(0, at)] = value
                z_out[n, at] = value.astype(bf16)

        for d in range(1, ZS):
            z_copy(n, d).start()

    def z_sum(n):
        for d in range(1, ZS):
            z_arrive(n, d).wait_recv()
        value = whole[n, me]
        for d in range(1, ZS):
            value = value + z_in[n, lax.rem(z + d, ZS)].astype(f32)
        packed_ref[pl.ds(32 * n, 32), :] = value
        for i in range(6):
            x_copy(n, i).wait_send()
        for d in range(1, ZS):
            z_copy(n, d).wait_send()

    def hc_copy():
        return remote(head_core.at[0], head_core.at[1], hcore_sem.at[0], hcore_sem.at[1], tag="head", emb=partner)

    def hx_copy(d, at):
        to = lax.rem(x + d, XS)
        return remote(head_x.at[x], head_x.at[at], hx_sem.at[0, d], hx_sem.at[1, at], tag="head", emb=(to * ZS + z) * 2 + core)

    def hz_copy(d, at):
        to = lax.rem(z + d, ZS)
        return remote(head_z.at[z], head_z.at[at], hz_sem.at[0, d], hz_sem.at[1, at], tag="head", emb=(x * ZS + to) * 2 + core)

    part(0, tower_ref, tower_delta)
    head_core[0] = lax.dot_general(
        back, active, (((1,), (1,)), ((), ())), preferred_element_type=f32, precision=lax.Precision.HIGHEST
    )
    hc_copy().start()
    weight_grad(0, hiddens, tower_delta)
    hc_copy().wait()
    head_x[x] = head_core[0] + head_core[1]
    for d in range(1, XS):
        hx_copy(d, x).start()
    part_sum(0)
    expert_delta = (own_part[...] * silu_slope(pre_e[...])).astype(bf16)
    part(1, expert_ref, expert_delta)
    for d in range(1, XS):
        hx_copy(d, lax.rem(x + d, XS)).wait_recv()
    head_z[z] = (head_x[0] + head_x[1]) + (head_x[2] + head_x[3])
    for d in range(1, ZS):
        hz_copy(d, z).start()
    core_sum(0)
    weight_grad(1, feats, expert_delta)
    x_relay(0)
    left(feats, feat_sem, "feats")
    left(hiddens, hidden_sem, "hiddens")
    for d in (2, 1, 3):
        sec_copy(shares, share_sem, "shares", d, sec).wait_send()
    part_sum(1)

    @pl.loop(0, SLOTS)
    def _(s):
        grad = own_part[pl.ds(pl.multiple_of(s * DIM, DIM), DIM), :]
        for k in range(2):
            low = jnp.where(bag_ref[pl.ds(s, 1), :] > k, (pos[2 * s + k] >> 7) & 7, -1)
            columns = pl.ds(pl.multiple_of((2 * s + k) * BATCH, BATCH), BATCH)
            for g in range(8):
                spread[g * DIM : (g + 1) * DIM, columns] = jnp.where(low == g, grad, 0.0).astype(bf16)

    @pl.loop(0, 4)
    def _(t):
        pair = lax.rem(x + t, 4)

        for q in range(2 * SLOTS):
            place = pos[q]
            key = ((place >> 10) - 2 * pair) * CAP + (place & (CAP - 1))
            hots[:, q * BATCH : (q + 1) * BATCH] = hot(2 * CAP, key)
        total = mm_nt(spread[...], hots[...]).astype(bf16)
        for h in range(2):
            for g in range(8):
                peer = (2 * pair + h) * 8 + g
                out_grads[peer] = total[g * DIM : (g + 1) * DIM, h * CAP : (h + 1) * CAP]

        @pl.when(t == 0)
        def _():
            in_grads[me] = out_grads[me]

        @pl.loop(0, ZS)
        def _(j):
            base = (pair * ZS + lax.rem(z + z_shift(j), ZS)) * 2
            for c in range(2):
                peer = base + c

                @pl.when(peer != me)
                def _():
                    grad_copy(peer, me).start()

        @pl.when(t == 0)
        def _():
            core_sum(1)
            x_sum(0)

        @pl.when(t == 1)
        def _():
            x_relay(1)

    x_sum(1)
    z_sum(0)
    for d in range(1, ZS):
        hz_copy(d, lax.rem(z + d, ZS)).wait_recv()
    head = head_z[0]
    for j in range(1, ZS):
        head = head + head_z[j]
    packed_ref[64:72, :] = jnp.broadcast_to(head, (8, WIDE))

    grad_ref[...] = jnp.zeros((WIDE, ROWS), f32)

    @pl.loop(1, EMB)
    def _(d):
        peer = lax.rem(me + d, EMB)
        id_copy(peer, me).wait_send()
        row_copy(peer, me).wait_send()


    @pl.loop(0, XS)
    def _(t):
        first = lax.rem(x + XS - t, XS) * 16

        @pl.loop(0, 16)
        def _(j):
            peer = first + j

            @pl.when(peer != me)
            def _():
                grad_copy(peer, peer).wait_recv()

        if "scatter" not in SKIP:

            @pl.loop(0, 8)
            def _(j):
                a = first + 2 * j
                keys = jnp.concatenate([ib[a], ib[a + 1]], axis=1)
                slot = keys >> 9
                grads = jnp.concatenate([in_grads[a], in_grads[a + 1]], axis=1).astype(f32)
                wide = jnp.concatenate([jnp.where(slot == s, grads, 0.0) for s in range(SLOTS)], axis=0).astype(bf16)
                columns = pl.ds(pl.multiple_of(j * 2 * CAP, 2 * CAP), 2 * CAP)
                spread[:, columns] = wide
                row_hots[:, columns] = hot(ROWS, keys & (ROWS - 1))

            grad_ref[...] += mm_nt(spread[:, : 16 * CAP], row_hots[...])

    z_sum(1)
    for d in range(1, XS):
        hx_copy(d, x).wait_send()
    for d in range(1, ZS):
        hz_copy(d, z).wait_send()

    @pl.loop(1, EMB)
    def _(d):
        peer = lax.rem(me + d, EMB)
        grad_copy(peer, me).wait_send()


def update_kernel(table_ref, accum_ref, grad_ref, packed_ref, new_table, new_accum, tower_grad, expert_grad, head_grad):
    @pl.loop(0, SLOTS)
    def _(s):
        rows = pl.ds(pl.multiple_of(s * DIM, DIM), DIM)
        grad = grad_ref[rows, :]
        accum = accum_ref[rows, :] + grad * grad
        new_accum[rows, :] = accum
        new_table[rows, :] = table_ref[rows, :] - learn_rate * grad / jnp.sqrt(accum)

    tower_grad[...] = packed_ref[:32, :]
    expert_grad[...] = packed_ref[32:64, :]
    head_grad[...] = packed_ref[64:65, :]


def body(
    emb_table,
    emb_accum,
    slot_ids,
    bag_len,
    expert_w,
    tower_w,
    tower_out,
    section_task,
    click_like,
    watch,
):
    vmem = pl.BlockSpec(memory_space=pltpu.VMEM)
    dma = pltpu.SemaphoreType.DMA
    table = emb_table.transpose(0, 2, 1).reshape(SLOTS * DIM, ROWS)
    accum = emb_accum.transpose(0, 2, 1).reshape(SLOTS * DIM, ROWS)
    anywhere = pl.BlockSpec(memory_space=pl.ANY)
    row_grad, packed = pl.pallas_call(
        step_kernel,
        out_shape=(
            jax.ShapeDtypeStruct((SLOTS * DIM, ROWS), f32),
            jax.ShapeDtypeStruct((72, WIDE), f32),
        ),
        in_specs=[pl.BlockSpec(memory_space=pltpu.SMEM), vmem, vmem, vmem, anywhere, anywhere, vmem, vmem, vmem],
        out_specs=(vmem,) * 2,
        scratch_shapes=[
            pltpu.VMEM((2 * SLOTS, 1, BATCH), i32),
            pltpu.VMEM((EMB, 1, CAP), i32),
            pltpu.VMEM((EMB, 1, CAP), i32),
            pltpu.VMEM((EMB, DIM, CAP), bf16),
            pltpu.VMEM((EMB, DIM, CAP), bf16),
            pltpu.VMEM((8 * DIM, 4 * CAP), bf16),
            pltpu.VMEM((8 * DIM, BATCH), f32),
            pltpu.VMEM((SLOTS * DIM, ROWS), bf16),
            pltpu.VMEM((SEC * WIDE, WIDE), bf16),
            pltpu.VMEM((SEC * WIDE, WIDE), bf16),
            pltpu.VMEM((SEC, WIDE, BATCH), bf16),
            pltpu.VMEM((SEC, WIDE, BATCH), bf16),
            pltpu.VMEM((SEC, WIDE, WIDE), bf16),
            pltpu.VMEM((SEC, WIDE, WIDE), bf16),
            pltpu.VMEM((WIDE, BATCH), f32),
            pltpu.VMEM((WIDE, BATCH), f32),
            pltpu.VMEM((SEC, 8, BATCH), f32),
            pltpu.VMEM((2, 6, WIDE // 2, BATCH), bf16),
            pltpu.VMEM((2, 6, WIDE // 2, BATCH), bf16),
            pltpu.VMEM((2, WIDE // 2, BATCH), f32),
            pltpu.VMEM((2, EMB, 32, WIDE), f32),
            pltpu.VMEM((WIDE, BATCH), f32),
            pltpu.VMEM((2, 32, 32, WIDE), bf16),
            pltpu.VMEM((2, 32, 32, WIDE), bf16),
            pltpu.VMEM((2, 6, ZS // 2, 32, WIDE), bf16),
            pltpu.VMEM((2, 6, ZS // 2, 32, WIDE), bf16),
            pltpu.VMEM((2, ZS, 32, WIDE), bf16),
            pltpu.VMEM((2, ZS, 32, WIDE), bf16),
            pltpu.VMEM((2, 1, WIDE), f32),
            pltpu.VMEM((XS, 1, WIDE), f32),
            pltpu.VMEM((ZS, 1, WIDE), f32),
            pltpu.VMEM((8 * DIM, 2 * SLOTS * BATCH), bf16),
            pltpu.VMEM((2 * CAP, 2 * SLOTS * BATCH), bf16),
            pltpu.VMEM((ROWS, 16 * CAP), bf16),
            pltpu.VMEM((EMB, DIM, CAP), bf16),
            pltpu.VMEM((EMB, DIM, CAP), bf16),
            dma((2,)),
            dma((EMB,)),
            dma((EMB,)),
            dma((EMB,)),
            dma((EMB,)),
            dma((2, 6)),
            dma((2, 6)),
            dma((2, SEC)),
            dma((2, 2, 6)),
            dma((2, 2)),
            dma((2, 2, 6)),
            dma((2, 2, ZS)),
            dma((2,)),
            dma((2, XS)),
            dma((2, ZS)),
            dma((EMB,)),
            dma((EMB,)),
        ],
        compiler_params=pltpu.CompilerParams(collective_id=0, has_side_effects=True, vmem_limit_bytes=52 << 20),
    )(
        section_task,
        slot_ids.transpose(1, 2, 0),
        bag_len.T,
        table,
        expert_w,
        tower_w,
        tower_out,
        click_like.T,
        watch.reshape(1, BATCH),
    )
    whole_table = jax.ShapeDtypeStruct((SLOTS * DIM, ROWS), f32)
    new_table, new_accum, tower_grad, expert_grad, head_grad = pl.pallas_call(
        update_kernel,
        out_shape=(
            whole_table,
            whole_table,
            jax.ShapeDtypeStruct((32, WIDE), f32),
            jax.ShapeDtypeStruct((32, WIDE), f32),
            jax.ShapeDtypeStruct((1, WIDE), f32),
        ),
        in_specs=[vmem] * 4,
        out_specs=(vmem,) * 5,
        compiler_params=pltpu.CompilerParams(vmem_limit_bytes=16 << 20),
    )(table, accum, row_grad, packed)

    def back(value):
        return value.reshape(SLOTS, DIM, ROWS).transpose(0, 2, 1)

    return (back(new_table), back(new_accum), expert_grad, tower_grad, head_grad)


def solution(mesh):
    placed = (
        P("sec", "emb", None),
        P("sec", "emb", None),
        P("emb", "sec", None),
        P("emb", "sec"),
        P(None, "sec"),
        P(None, "sec"),
        P("sec", None),
        P("sec"),
        P("emb", None),
        P("emb"),
    )
    return jax.shard_map(
        body,
        mesh=mesh,
        in_specs=placed,
        out_specs=(
            P("sec", "emb", None),
            P("sec", "emb", None),
            P("emb", "sec"),
            P("emb", "sec"),
            P("sec", None),
        ),
        check_vma=False,
    )
```
